32 devices in a mesh: fsdp: 8 (over z, core), seq: 4 (over y, x).
Axes of the slice: x: 2, y: 2, z: 4, core: 2. Of those that a mesh axis runs over, the one named last changes fastest.
Arguments:
- tokens: bfloat16 [8, 512, 2880], P('fsdp', 'seq'), may hold values from -6 to 6
- queries: bfloat16 [8, 512, 2048], P('fsdp', 'seq'), may hold values from -6 to 6
- kv_weight: bfloat16 [2880, 512], P('fsdp'), may hold values from -0.109375 to 0.109375
- sink_logit_values: float32 [32], replicated, may hold values from 1 to 6
- roll_offsets: int32 [8], P('fsdp'), may hold values from 0 to 511
- out_grad: bfloat16 [8, 512, 2048], P('fsdp', 'seq'), may hold values from -6 to 6
Outputs:
- attn_out: bfloat16 [8, 512, 2048], P('fsdp', 'seq')
- query_grad: bfloat16 [8, 512, 2048], P('fsdp', 'seq')
- token_grad: bfloat16 [8, 512, 2880], P('fsdp', 'seq')
- weight_grad: float32 [4, 2880, 128], P('seq', 'fsdp')
The draws below stay inside these ranges and needn't reach their ends.
All inputs are finite; a program needn't handle non-finite values.
Results may differ from the reference program's by a relative error of at most 0.012.
Values may be sent and summed in bfloat16 or wider, within the bound.
A program may use at most 64 MiB of HBM per device.

```python
import jax
import jax.numpy as jnp
from jax import lax

D = 2880
QUERY_HEADS = 32
KEY_VALUE_HEADS = 4
HEAD_SIZE = 64
WINDOW = 128
STREAMS = 8
SEQLEN = 512
QW = 2048
KW = 512
GRAD_BLOCK_ROWS = 2880
N_SEQ = 4


def with_ends(array, key, least, high):
    longest = array.shape.index(max(array.shape))
    spots = []
    for shift in (0, 1):
        where = [jax.random.randint(jax.random.fold_in(key, axis), (), 0, length) for axis, length in enumerate(array.shape)]
        where[longest] = (where[longest] + shift) % array.shape[longest]
        spots.append(tuple(where))
    return array.at[spots[0]].set(least).at[spots[1]].set(high)


def with_spikes(entries, stream_key, source, target, shards_of, factor):
    def block_of(dim):
        return (jnp.arange(entries.shape[dim]) // (entries.shape[dim] // shards_of)).reshape((-1,) + (1,) * (entries.ndim - 1 - dim))

    one_side = jax.random.permutation(stream_key, shards_of)[block_of(target)]
    far = (block_of(target) + shards_of // 2) % shards_of
    return jnp.where((block_of(source) == one_side) | (block_of(source) == far), factor * entries, entries)


def block_scale(own_key, dims, split, low, top_value):
    def one(axis_at, blocks):
        draws = jax.random.uniform(jax.random.fold_in(jax.random.fold_in(own_key, 6), axis_at), (blocks,), jnp.float32, low / len(split), top_value / len(split))
        return jnp.repeat(jnp.exp(draws), dims[axis_at] // blocks).reshape((-1,) + (1,) * (len(dims) - axis_at - 1))

    loudness = one(*split[0])
    for cut in split[1:]:
        loudness = loudness * one(*cut)
    return loudness


def bell_draw(key, shape, deviation, reach, pieces=(), kind=jnp.bfloat16):
    gain = block_scale(key, shape, pieces, -0.22, 0.18) if pieces else 1.0
    drawn = jax.random.normal(key, shape, jnp.float32) * deviation * gain
    return jnp.minimum(jnp.maximum(drawn, -reach), reach).astype(kind)


def noise_with(rng, dims, width, bound, shards, heavy, kind=jnp.bfloat16):
    entries = width * jax.random.normal(rng, dims, jnp.float32)
    if shards:
        entries = entries * block_scale(rng, dims, shards, -0.22, 0.18)
    return jnp.clip(with_spikes(entries, jax.random.fold_in(rng, 3), *heavy), -bound, bound).astype(kind)


def setup_inputs(seed: int = 0) -> dict:
    seeds = jax.random.split(jax.random.key(seed), 7)
    return {
        "tokens": noise_with(seeds[0], (STREAMS, SEQLEN, D), 1.0, 6.0, ((0, 8), (1, 4)), (0, 2, 8, 2.0)),
        "queries": bell_draw(seeds[1], (STREAMS, SEQLEN, QW), 1.0, 6.0, ((0, 8), (1, 4))),
        "kv_weight": bell_draw(seeds[2], (D, KW), D ** -0.5, 0.109375, ((0, 8),)),
        "sink_logit_values": jnp.clip(jax.random.uniform(seeds[3], (QUERY_HEADS,), jnp.float32, 1.0, 6.0), 1.0, 6.0),
        "roll_offsets": with_ends(jax.random.randint(seeds[4], (STREAMS,), 0, SEQLEN), jax.random.fold_in(seeds[4], 1), 0, SEQLEN - 1).astype(jnp.int32),
        "out_grad": noise_with(seeds[5], (STREAMS, SEQLEN, QW), 1.0, 6.0, ((0, 8), (1, 4)), (1, 2, 4, 2.0)),
    }


rope_base = 150000.0


def rope_tables(positions):
    half_width = HEAD_SIZE // 2
    frequency = rope_base ** (-jnp.arange(half_width, dtype=jnp.float32) / half_width)
    angle = positions.astype(jnp.float32)[:, None] * frequency[None, :]
    return jnp.cos(angle), jnp.sin(angle)


def apply_rotary(values, cosine_lookup, sine_lookup, head_count, direction):
    row_count = values.shape[0]
    halves = values.reshape(row_count, head_count, 2, HEAD_SIZE // 2)
    front_half = halves[:, :, 0]
    back_half = halves[:, :, 1]
    cosine_rows = cosine_lookup[:, None, :]
    sine_rows = sine_lookup[:, None, :] * direction
    turned = jnp.stack([front_half * cosine_rows - back_half * sine_rows,
                        front_half * sine_rows + back_half * cosine_rows], axis=2)
    return turned.reshape(row_count, head_count * HEAD_SIZE)


def attend_group(query_g, key_g, value_g, grad_g, sink_g, allowed):
    score_scale = HEAD_SIZE ** -0.5
    query_f = query_g.astype(jnp.float32)
    key_f = key_g.astype(jnp.float32)
    value_f = value_g.astype(jnp.float32)
    grad_f = grad_g.astype(jnp.float32)
    scores = jnp.einsum('bgd,kd->gbk', query_f, key_f) * score_scale
    exponent = jnp.where(allowed[None], jnp.exp(scores), 0.0)
    denominator = jnp.exp(sink_g)[:, None] + jnp.sum(exponent, axis=2)
    softmax_w = exponent / denominator[:, :, None]
    softmax_b = softmax_w.astype(jnp.bfloat16).astype(jnp.float32)
    attended = jnp.einsum('gbk,kd->bgd', softmax_b, value_f)
    dprob = jnp.einsum('bgd,kd->gbk', grad_f, value_f)
    row_delta = jnp.sum(softmax_w * dprob, axis=2)
    dscore = (softmax_w * (dprob - row_delta[:, :, None]) * score_scale).astype(jnp.bfloat16).astype(jnp.float32)
    query_diff = jnp.einsum('gbk,kd->bgd', dscore, key_f)
    key_diff = jnp.einsum('gbk,bgd->kd', dscore, query_f)
    value_diff = jnp.einsum('gbk,bgd->kd', softmax_b, grad_f)
    return attended.astype(jnp.bfloat16), query_diff, key_diff, value_diff


def attend_block(query_block, key_block, gradient_block, sink_logit_values, key_first):
    block_row_span = query_block.shape[0]
    key_row_slice = key_block.shape[0]
    group_width = QUERY_HEADS // KEY_VALUE_HEADS
    key_span_width = KEY_VALUE_HEADS * HEAD_SIZE
    rows_idx = jnp.arange(block_row_span, dtype=jnp.int32)[:, None]
    cols_idx = jnp.arange(key_row_slice, dtype=jnp.int32)[None, :]
    allowed = (cols_idx > rows_idx) & (cols_idx <= rows_idx + WINDOW) & (cols_idx + key_first >= 0)
    query_head_rows = query_block.reshape(block_row_span, KEY_VALUE_HEADS, group_width, HEAD_SIZE).transpose(1, 0, 2, 3)
    gradient_heads = gradient_block.reshape(block_row_span, KEY_VALUE_HEADS, group_width, HEAD_SIZE).transpose(1, 0, 2, 3)
    key_head_rows = key_block[:, :key_span_width].reshape(key_row_slice, KEY_VALUE_HEADS, HEAD_SIZE).transpose(1, 0, 2)
    value_head_rows = key_block[:, key_span_width:].reshape(key_row_slice, KEY_VALUE_HEADS, HEAD_SIZE).transpose(1, 0, 2)
    sink_per_head = sink_logit_values.reshape(KEY_VALUE_HEADS, group_width)

    def per_group(packed):
        return attend_group(packed[0], packed[1], packed[2], packed[3], packed[4], allowed)

    attended, query_diff, key_diff, value_diff = lax.map(per_group, (query_head_rows, key_head_rows, value_head_rows, gradient_heads, sink_per_head))
    attended = attended.transpose(1, 0, 2, 3).reshape(block_row_span, QUERY_HEADS * HEAD_SIZE)
    query_diff = query_diff.transpose(1, 0, 2, 3).reshape(block_row_span, QUERY_HEADS * HEAD_SIZE)
    kv_diff = jnp.concatenate([key_diff.transpose(1, 0, 2).reshape(key_row_slice, key_span_width),
                               value_diff.transpose(1, 0, 2).reshape(key_row_slice, key_span_width)], axis=1)
    return attended, query_diff, kv_diff


def band_pass(query_rot, keys_all, grad_out, sink_logit_values, row_start):
    row_total = query_rot.shape[0]
    block_row_span = min(row_total, 512)

    def block_step(grad_all, block_index):
        block_begin = block_index * block_row_span
        query_block = lax.dynamic_slice_in_dim(query_rot, block_begin, block_row_span, 0)
        key_block = lax.dynamic_slice_in_dim(keys_all, block_begin, block_row_span + WINDOW, 0)
        gradient_block = lax.dynamic_slice_in_dim(grad_out, block_begin, block_row_span, 0)
        attended, query_diff, kv_diff = attend_block(query_block, key_block, gradient_block, sink_logit_values, row_start + block_begin - WINDOW)
        previous = lax.dynamic_slice_in_dim(grad_all, block_begin, block_row_span + WINDOW, 0)
        grad_all = lax.dynamic_update_slice_in_dim(grad_all, previous + kv_diff, block_begin, 0)
        return grad_all, (attended, query_diff)

    start_grad = jnp.zeros((row_total + WINDOW, keys_all.shape[1]), jnp.float32)
    grad_all, (attended, query_diff) = lax.scan(block_step, start_grad, jnp.arange(row_total // block_row_span, dtype=jnp.int32))
    return attended.reshape(row_total, QUERY_HEADS * HEAD_SIZE), query_diff.reshape(row_total, QUERY_HEADS * HEAD_SIZE), grad_all


def reference(tokens, queries, kv_weight, sink_logit_values, roll_offsets, out_grad):
    key_span_width = KEY_VALUE_HEADS * HEAD_SIZE

    def one_stream(weight_sum, stream_data):
        token_rows, query_rows, grad_rows, roll_start = stream_data
        projected_rows = jnp.dot(token_rows, kv_weight, preferred_element_type=jnp.float32)
        positions = (jnp.arange(SEQLEN, dtype=jnp.int32) + roll_start) % SEQLEN
        cosine_lookup, sine_lookup = rope_tables(positions)
        key_value_rotated = jnp.concatenate([apply_rotary(projected_rows[:, :key_span_width], cosine_lookup, sine_lookup, KEY_VALUE_HEADS, 1.0),
                                  projected_rows[:, key_span_width:]], axis=1).astype(jnp.bfloat16)
        query_rot = apply_rotary(query_rows.astype(jnp.float32), cosine_lookup, sine_lookup, QUERY_HEADS, 1.0).astype(jnp.bfloat16)
        keys_all = jnp.concatenate([jnp.zeros((WINDOW, 2 * key_span_width), jnp.bfloat16), key_value_rotated], axis=0)
        attended, query_diff, grad_all = band_pass(query_rot, keys_all, grad_rows, sink_logit_values, jnp.int32(0))
        local_gradient = grad_all[WINDOW:]
        query_back = apply_rotary(query_diff, cosine_lookup, sine_lookup, QUERY_HEADS, -1.0).astype(jnp.bfloat16)
        key_value_backward = jnp.concatenate([apply_rotary(local_gradient[:, :key_span_width], cosine_lookup, sine_lookup, KEY_VALUE_HEADS, -1.0),
                                   local_gradient[:, key_span_width:]], axis=1).astype(jnp.bfloat16)
        token_back = jnp.dot(key_value_backward, kv_weight.T, preferred_element_type=jnp.float32).astype(jnp.bfloat16)
        weight_part = lax.dot_general(token_rows, key_value_backward, (((0,), (0,)), ((), ())), preferred_element_type=jnp.float32)
        return weight_sum + weight_part, (attended, query_back, token_back)

    start_sum = jnp.zeros((D, 2 * key_span_width), jnp.float32)
    weight_sum, (attn_out, query_grad, token_grad) = lax.scan(one_stream, start_sum, (tokens, queries, out_grad, roll_offsets))
    weight_grad = weight_sum.reshape(N_SEQ, GRAD_BLOCK_ROWS, 128)
    return attn_out, query_grad, token_grad, weight_grad
```

```python
import functools

import jax
import jax.numpy as jnp
from jax import lax
from jax.experimental import pallas as pl
from jax.experimental.pallas import tpu as pltpu
from jax.sharding import PartitionSpec as P

QUERY_HEADS = 32
KEY_VALUE_HEADS = 4
HEAD_SIZE = 64
WINDOW = 128


rope_base = 150000.0


def from_behind(array, axis, by):
    peers = lax.axis_size(axis)
    pairs = [(i, i + by) for i in range(peers) if 0 <= i + by < peers]
    return lax.ppermute(array, axis, pairs)


def rope_tables(positions):
    half_width = HEAD_SIZE // 2
    frequency = rope_base ** (-jnp.arange(half_width, dtype=jnp.float32) / half_width)
    angle = positions.astype(jnp.float32)[:, None] * frequency[None, :]
    return (jnp.cos(angle), jnp.sin(angle))


def apply_rotary(values, cosine_lookup, sine_lookup, head_count, direction):
    row_count = values.shape[0]
    halves = values.reshape(row_count, head_count, 2, HEAD_SIZE // 2)
    front_half = halves[:, :, 0]
    back_half = halves[:, :, 1]
    cosine_rows = cosine_lookup[:, None, :]
    sine_rows = sine_lookup[:, None, :] * direction
    turned = jnp.stack(
        [
            front_half * cosine_rows - back_half * sine_rows,
            front_half * sine_rows + back_half * cosine_rows,
        ],
        axis=2,
    )
    return turned.reshape(row_count, head_count * HEAD_SIZE)


def attend_group(query_g, key_g, value_g, grad_g, sink_g, allowed):
    score_scale = HEAD_SIZE ** (-0.5)
    scores = (
        jnp.einsum("bgd,kd->gbk", query_g, key_g, preferred_element_type=jnp.float32) * score_scale
    )
    exponent = jnp.where(allowed[None], jnp.exp(scores), 0.0)
    denominator = jnp.exp(sink_g)[:, None] + jnp.sum(exponent, axis=2)
    softmax_w = exponent / denominator[:, :, None]
    softmax_b = softmax_w.astype(jnp.bfloat16)
    attended = jnp.einsum("gbk,kd->bgd", softmax_b, value_g, preferred_element_type=jnp.float32)
    dprob = jnp.einsum("bgd,kd->gbk", grad_g, value_g, preferred_element_type=jnp.float32)
    row_delta = jnp.sum(softmax_w * dprob, axis=2)
    dscore = (softmax_w * (dprob - row_delta[:, :, None]) * score_scale).astype(jnp.bfloat16)
    query_diff = jnp.einsum("gbk,kd->bgd", dscore, key_g, preferred_element_type=jnp.float32)
    key_diff = jnp.einsum("gbk,bgd->kd", dscore, query_g, preferred_element_type=jnp.float32)
    value_diff = jnp.einsum("gbk,bgd->kd", softmax_b, grad_g, preferred_element_type=jnp.float32)
    return (attended.astype(jnp.bfloat16), query_diff, key_diff, value_diff)


def attend_block(query_block, key_block, gradient_block, sink_logit_values, key_first):
    block_row_span = query_block.shape[0]
    key_row_slice = key_block.shape[0]
    group_width = QUERY_HEADS // KEY_VALUE_HEADS
    key_span_width = KEY_VALUE_HEADS * HEAD_SIZE
    rows_idx = jnp.arange(block_row_span, dtype=jnp.int32)[:, None]
    cols_idx = jnp.arange(key_row_slice, dtype=jnp.int32)[None, :]
    allowed = (cols_idx > rows_idx) & (cols_idx <= rows_idx + WINDOW) & (cols_idx + key_first >= 0)
    query_head_rows = query_block.reshape(
        block_row_span, KEY_VALUE_HEADS, group_width, HEAD_SIZE
    ).transpose(1, 0, 2, 3)
    gradient_heads = gradient_block.reshape(
        block_row_span, KEY_VALUE_HEADS, group_width, HEAD_SIZE
    ).transpose(1, 0, 2, 3)
    key_head_rows = (
        key_block[:, :key_span_width]
        .reshape(key_row_slice, KEY_VALUE_HEADS, HEAD_SIZE)
        .transpose(1, 0, 2)
    )
    value_head_rows = (
        key_block[:, key_span_width:]
        .reshape(key_row_slice, KEY_VALUE_HEADS, HEAD_SIZE)
        .transpose(1, 0, 2)
    )
    sink_per_head = sink_logit_values.reshape(KEY_VALUE_HEADS, group_width)

    def per_group(packed):
        return attend_group(packed[0], packed[1], packed[2], packed[3], packed[4], allowed)

    attended, query_diff, key_diff, value_diff = lax.map(
        per_group, (query_head_rows, key_head_rows, value_head_rows, gradient_heads, sink_per_head)
    )
    attended = attended.transpose(1, 0, 2, 3).reshape(block_row_span, QUERY_HEADS * HEAD_SIZE)
    query_diff = query_diff.transpose(1, 0, 2, 3).reshape(block_row_span, QUERY_HEADS * HEAD_SIZE)
    kv_diff = jnp.concatenate(
        [
            key_diff.transpose(1, 0, 2).reshape(key_row_slice, key_span_width),
            value_diff.transpose(1, 0, 2).reshape(key_row_slice, key_span_width),
        ],
        axis=1,
    )
    return (attended, query_diff, kv_diff)


def band_pass(query_rot, keys_all, grad_out, sink_logit_values, row_start):
    row_total = query_rot.shape[0]
    block_row_span = min(row_total, 512)

    def block_step(grad_all, block_index):
        block_begin = block_index * block_row_span
        attended, query_diff, kv_diff = attend_block(
            query_rot, keys_all, grad_out, sink_logit_values, row_start + block_begin - WINDOW
        )
        previous = grad_all
        grad_all = previous + kv_diff
        return (grad_all, (attended, query_diff))

    start_grad = jnp.zeros((row_total + WINDOW, keys_all.shape[1]), jnp.float32)
    grad_all, (attended, query_diff) = lax.scan(
        block_step, start_grad, jnp.arange(row_total // block_row_span, dtype=jnp.int32)
    )
    return (
        attended.reshape(row_total, QUERY_HEADS * HEAD_SIZE),
        query_diff.reshape(row_total, QUERY_HEADS * HEAD_SIZE),
        grad_all,
    )


def local(tokens, queries, kv_weight, sink_logit_values, roll_offsets, out_grad):
    token_rows = tokens[0]
    query_rows = queries[0]
    grad_rows = out_grad[0]
    row_total = token_rows.shape[0]
    key_span_width = KEY_VALUE_HEADS * HEAD_SIZE
    seq_index = lax.axis_index("seq")
    seq_count = lax.axis_size("seq")
    stream_length = row_total * seq_count
    row_start = seq_index * row_total
    whole_weight = lax.all_gather(kv_weight, "fsdp", axis=0, tiled=True)
    projected_rows = jnp.dot(token_rows, whole_weight, preferred_element_type=jnp.float32)
    positions = (
        row_start + jnp.arange(row_total, dtype=jnp.int32) + roll_offsets[0]
    ) % stream_length
    cosine_lookup, sine_lookup = rope_tables(positions)
    key_value_rotated = jnp.concatenate(
        [
            apply_rotary(
                projected_rows[:, :key_span_width], cosine_lookup, sine_lookup, KEY_VALUE_HEADS, 1.0
            ),
            projected_rows[:, key_span_width:],
        ],
        axis=1,
    ).astype(jnp.bfloat16)
    query_rot = apply_rotary(
        query_rows.astype(jnp.float32), cosine_lookup, sine_lookup, QUERY_HEADS, 1.0
    ).astype(jnp.bfloat16)
    edge_rows = from_behind(key_value_rotated, "seq", 1)
    keys_all = jnp.concatenate([edge_rows, key_value_rotated], axis=0)
    attended, query_diff, grad_all = band_pass(
        query_rot, keys_all, grad_rows, sink_logit_values, row_start
    )
    incoming = from_behind(grad_all[:WINDOW].astype(jnp.bfloat16), "seq", -1).astype(jnp.float32)
    local_gradient = grad_all[WINDOW:]
    local_gradient = jnp.concatenate(
        [local_gradient[: row_total - WINDOW], local_gradient + incoming], axis=0
    )
    query_back = apply_rotary(query_diff, cosine_lookup, sine_lookup, QUERY_HEADS, -1.0).astype(
        jnp.bfloat16
    )
    key_value_backward = jnp.concatenate(
        [
            apply_rotary(
                local_gradient[:, :key_span_width],
                cosine_lookup,
                sine_lookup,
                KEY_VALUE_HEADS,
                -1.0,
            ),
            local_gradient[:, key_span_width:],
        ],
        axis=1,
    ).astype(jnp.bfloat16)
    token_back = lax.dot_general(
        key_value_backward,
        whole_weight,
        (((1,), (1,)), ((), ())),
        preferred_element_type=jnp.float32,
    ).astype(jnp.bfloat16)
    feature_block = lax.all_to_all(token_rows, "seq", split_axis=1, concat_axis=0, tiled=True)
    block_term = lax.dot_general(
        feature_block,
        lax.all_gather(key_value_backward, "seq", axis=0, tiled=True),
        (((0,), (0,)), ((), ())),
        preferred_element_type=jnp.float32,
    )
    flat_block = block_term.reshape(-1, 128)
    weight_share = lax.psum_scatter(flat_block, "fsdp", scatter_dimension=0, tiled=True)
    return (attended[None], query_back[None], token_back[None], weight_share[None])


def nt(a, b):
    return lax.dot_general(a, b, (((1,), (1,)), ((), ())), preferred_element_type=jnp.float32)


def tn(a, b):
    return lax.dot_general(a, b, (((0,), (0,)), ((), ())), preferred_element_type=jnp.float32)


def nn(a, b):
    return lax.dot_general(a, b, (((1,), (0,)), ((), ())), preferred_element_type=jnp.float32)


def turn(x, cosine, sine, back):
    width = x.shape[1]
    lane = lax.broadcasted_iota(jnp.int32, x.shape, 1)
    swapped = jnp.where(
        lane % HEAD_SIZE < HEAD_SIZE // 2,
        pltpu.roll(x, width - HEAD_SIZE // 2, 1),
        pltpu.roll(x, HEAD_SIZE // 2, 1),
    )
    times = width // cosine.shape[1]
    cosine = jnp.concatenate([cosine] * times, axis=1)
    sine = jnp.concatenate([sine] * times, axis=1)
    if back:
        return x * cosine - swapped * sine
    return x * cosine + swapped * sine


def fused_kernel(
    nz, ns, share, pad,
    tok, q, w, esink, ct, st, og,
    attn, qgrad, tgrad, wgrad,
    wall, tokf, tokpad, tokblk, qs, gs, kvbuf, own_g, hg_out, hg_in, dkv_all,
    core_out, core_in, z_out, z_in,
    bar_z, zs, zr, qsn, qrn, ps, pr, ts, tr, hs, hr, gsn, grn, ds_, dr, cs, cr, rs, rr,
):
    nf = 2 * nz
    rows = tok.shape[0]
    krows = w.shape[0]
    groups = KEY_VALUE_HEADS
    per = QUERY_HEADS // KEY_VALUE_HEADS
    span = per * HEAD_SIZE
    f = lax.axis_index("fsdp")
    s = lax.axis_index("seq")
    z = f // 2
    c = f % 2
    partner = (f + 1 - 2 * c, s)

    def zpeer(d):
        return lax.rem(z + d, nz) * 2 + c

    def speer(d):
        return lax.rem(s + d, ns)

    def remote(src, dst, a, b, dev):
        return pltpu.make_async_remote_copy(
            src_ref=src, dst_ref=dst, send_sem=a, recv_sem=b,
            device_id=dev, device_id_type=pl.DeviceIdType.MESH,
        )

    cols = pl.ds(pl.multiple_of(s * 128, 128), 128)

    barrier = pltpu.get_barrier_semaphore()
    for d in range(1, nz):
        pl.semaphore_signal(barrier, inc=1, device_id=(zpeer(d), s), device_id_type=pl.DeviceIdType.MESH)
    for d in range(1, ns):
        pl.semaphore_signal(barrier, inc=1, device_id=(f, speer(d)), device_id_type=pl.DeviceIdType.MESH)
    pl.semaphore_signal(barrier, inc=1, device_id=partner, device_id_type=pl.DeviceIdType.MESH)
    pl.semaphore_wait(barrier, nz + ns - 1)

    sent = []
    for d in range(1, nz):
        cp = remote(w.at[:, cols], wall.at[f, :, cols], zs.at[d - 1], zr.at[d - 1], (zpeer(d), s))
        cp.start()
        sent.append(cp)
    cp = remote(w, wall.at[f], ps.at[0], pr.at[0], partner)
    cp.start()
    sent.append(cp)

    wall[f] = w[...]
    for i in range(nf):
        tokf[i, :, :krows] = tok[:, i * krows : (i + 1) * krows]
    cosine = ct[...]
    sine = st[...]

    wait_z = []
    for d in range(1, nz):
        block = lax.rem(z + nz - d, nz) * 2 + c
        remote(w.at[:, cols], wall.at[block, :, cols], zs.at[d - 1], zr.at[d - 1], (zpeer(d), s)).wait_recv()
        for e in range(1, ns):
            cp = remote(
                wall.at[block, :, cols], wall.at[block, :, cols],
                qsn.at[d - 1, e - 1], qrn.at[d - 1, e - 1], (f, speer(e)),
            )
            cp.start()
            sent.append(cp)

    tokpad[...] = jnp.zeros_like(tokpad)
    for t in range(ns):
        for k in range(2):
            for i in range(nz):
                start = t * nf * share + (2 * i + k) * share
                to = (k * nz + i) * pad
                tokpad[t, :, to : to + share] = tok[:, start : start + share]
    for e in range(1, ns):
        cp = remote(tokpad.at[speer(e)], tokblk.at[s], ts.at[e - 1], tr.at[e - 1], (f, speer(e)))
        cp.start()
        sent.append(cp)
    tokblk[s] = tokpad[s]

    @pl.loop(0, groups)
    def _(g):
        here = pl.ds(pl.multiple_of(g * span, span), span)
        x = turn(q[:, here].astype(jnp.float32), cosine, sine, False).astype(jnp.bfloat16)
        x = x * jnp.asarray(HEAD_SIZE ** (-0.5), jnp.bfloat16)
        o = og[:, here]
        for h in range(per):
            qs[g, h * rows : (h + 1) * rows, :] = x[:, h * HEAD_SIZE : (h + 1) * HEAD_SIZE]
            gs[g, h * rows : (h + 1) * rows, :] = o[:, h * HEAD_SIZE : (h + 1) * HEAD_SIZE]

    def part(block):
        return nn(tokf[block][:, :krows], wall[block])

    total = part(f)
    other = f + 1 - 2 * c
    remote(w, wall.at[other], ps.at[0], pr.at[0], partner).wait_recv()
    total = total + part(other)
    for d in range(1, nz):
        block = lax.rem(z + nz - d, nz) * 2 + c
        for e in range(1, ns):
            there = pl.ds(pl.multiple_of(lax.rem(s + ns - e, ns) * 128, 128), 128)
            remote(
                wall.at[block, :, there], wall.at[block, :, there],
                qsn.at[d - 1, e - 1], qrn.at[d - 1, e - 1], (f, speer(e)),
            ).wait_recv()
        cp = remote(wall.at[block], wall.at[block], ps.at[d], pr.at[d], partner)
        cp.start()
        sent.append(cp)
        total = total + part(block)
    for d in range(1, nz):
        block = lax.rem(z + nz - d, nz) * 2 + 1 - c
        remote(wall.at[block], wall.at[block], ps.at[d], pr.at[d], partner).wait_recv()
        total = total + part(block)

    key_width = groups * HEAD_SIZE
    keys = turn(total[:, :key_width], cosine, sine, False).astype(jnp.bfloat16)
    values = total[:, key_width:].astype(jnp.bfloat16)
    for g in range(groups):
        lo, hi = g * HEAD_SIZE, (g + 1) * HEAD_SIZE
        kvbuf[g, WINDOW:, :] = jnp.concatenate([keys[:, lo:hi], values[:, lo:hi]], axis=1)
    halo = remote(
        kvbuf.at[:, pl.ds(WINDOW, WINDOW), :], kvbuf.at[:, pl.ds(0, WINDOW), :], hs, hr, (f, speer(1))
    )
    halo.start()
    halo.wait()

    r = lax.broadcasted_iota(jnp.int32, (rows, rows + WINDOW), 0)
    k = lax.broadcasted_iota(jnp.int32, (rows, rows + WINDOW), 1)
    allowed = (k > r) & (k <= r + WINDOW) & (k + s * rows - WINDOW >= 0)
    before = speer(ns - 1)

    @pl.loop(0, groups)
    def _(g):
        here = pl.ds(pl.multiple_of(g * span, span), span)
        kv = kvbuf[g]
        key, value = kv[:, :HEAD_SIZE], kv[:, HEAD_SIZE:]
        query, grad = qs[g], gs[g]
        wide = (per, rows, rows + WINDOW)
        flat = (per * rows, rows + WINDOW)
        expo = jnp.where(allowed[None], jnp.exp(nt(query, key).reshape(wide)), 0.0)
        denominator = esink[g][:, :, :1] + jnp.sum(expo, axis=2, keepdims=True)
        probs = expo * (1.0 / denominator)
        probs_b = probs.astype(jnp.bfloat16).reshape(flat)
        dprob = nt(grad, value).reshape(wide)
        delta = jnp.sum(probs * dprob, axis=2, keepdims=True)
        dscore = (probs * (dprob - delta)).astype(jnp.bfloat16).reshape(flat)
        out = nn(probs_b, value).astype(jnp.bfloat16)
        dq = nn(dscore, key) * (HEAD_SIZE ** (-0.5))

        def unstack(a):
            return jnp.concatenate([a[h * rows : (h + 1) * rows, :] for h in range(per)], axis=1)

        attn[:, here] = unstack(out)
        qgrad[:, here] = turn(unstack(dq), cosine, sine, True).astype(jnp.bfloat16)
        dkv = jnp.concatenate([tn(dscore, query), tn(probs_b, grad)], axis=1)
        hg_out[g] = dkv[:WINDOW].astype(jnp.bfloat16)
        own_g[g] = dkv[WINDOW:]
        remote(hg_out.at[g], hg_in.at[g], gsn.at[g], grn.at[g], (f, before)).start()

    both = []
    for g in range(groups):
        remote(hg_out.at[g], hg_in.at[g], gsn.at[g], grn.at[g], (f, before)).wait()
        both.append(own_g[g] + hg_in[g].astype(jnp.float32))
    dkey = jnp.concatenate([b[:, :HEAD_SIZE] for b in both], axis=1)
    dvalue = jnp.concatenate([b[:, HEAD_SIZE:] for b in both], axis=1)
    dkv = jnp.concatenate([turn(dkey, cosine, sine, True), dvalue], axis=1).astype(jnp.bfloat16)
    dkv_all[s] = dkv
    for e in range(1, ns):
        cp = remote(dkv_all.at[s], dkv_all.at[s], ds_.at[e - 1], dr.at[e - 1], (f, speer(e)))
        cp.start()
        sent.append(cp)
    for i in range(nf):
        tgrad[:, i * krows : (i + 1) * krows] = nt(dkv, wall[i]).astype(jnp.bfloat16)

    for e in range(1, ns):
        src = lax.rem(s + ns - e, ns)
        remote(tokpad.at[src], tokblk.at[src], ts.at[e - 1], tr.at[e - 1], (f, src)).wait_recv()
        remote(dkv_all.at[src], dkv_all.at[src], ds_.at[e - 1], dr.at[e - 1], (f, src)).wait_recv()
    half = nz * pad
    all_dkv = dkv_all[...].reshape(ns * rows, KW_COLUMNS)

    def wpart(core):
        lanes = pl.ds(pl.multiple_of(core * half, 128), half)
        return tn(tokblk[:, :, lanes].reshape(ns * rows, half), all_dkv)

    core_out[...] = wpart(1 - c).astype(jnp.bfloat16)
    core_copy = remote(core_out, core_in, cs, cr, partner)
    core_copy.start()
    mine = wpart(c)
    core_copy.wait()
    z_out[...] = (mine + core_in[...].astype(jnp.float32)).reshape(nz, pad, KW_COLUMNS)
    z_send = []
    for d in range(1, nz):
        bar_z[d - 1] = z_out[lax.rem(z + d, nz)].astype(jnp.bfloat16)
        cp = remote(bar_z.at[d - 1], z_in.at[d - 1], rs.at[d - 1], rr.at[d - 1], (zpeer(d), s))
        cp.start()
        z_send.append(cp)
    acc = z_out[z]
    for cp in z_send:
        cp.wait_recv()
    for d in range(1, nz):
        acc = acc + z_in[d - 1].astype(jnp.float32)
    wgrad[...] = acc[:share]
    for cp in sent + z_send:
        cp.wait_send()


KW_COLUMNS = 2 * KEY_VALUE_HEADS * HEAD_SIZE


def fused(tokens, queries, kv_weight, sink_logit_values, roll_offsets, out_grad):
    nf = lax.axis_size("fsdp")
    ns = lax.axis_size("seq")
    nz = nf // 2
    rows, width = tokens.shape[1:]
    krows = kv_weight.shape[0]
    share = width // (nf * ns)
    pad = -(-share // 16) * 16
    query_width = QUERY_HEADS * HEAD_SIZE
    groups = KEY_VALUE_HEADS
    per = QUERY_HEADS // groups
    positions = (
        lax.axis_index("seq") * rows + jnp.arange(rows, dtype=jnp.int32) + roll_offsets[0]
    ) % (rows * ns)
    cosine, sine = rope_tables(positions)
    ct = jnp.concatenate([cosine] * 4, axis=1)
    st = jnp.concatenate([-sine, sine] * 2, axis=1)
    esink = jnp.broadcast_to(jnp.exp(sink_logit_values).reshape(groups, per, 1, 1), (groups, per, 1, 128))
    bf, f32 = jnp.bfloat16, jnp.float32
    sem = pltpu.SemaphoreType.DMA
    vm = pltpu.VMEM
    shape = jax.ShapeDtypeStruct
    attn, qgrad, tgrad, wgrad = pl.pallas_call(
        functools.partial(fused_kernel, nz, ns, share, pad),
        out_shape=(
            shape((rows, query_width), bf),
            shape((rows, query_width), bf),
            shape((rows, width), bf),
            shape((share, KW_COLUMNS), f32),
        ),
        in_specs=[pl.BlockSpec(memory_space=pltpu.VMEM)] * 7,
        out_specs=[pl.BlockSpec(memory_space=pltpu.VMEM)] * 4,
        scratch_shapes=[
            vm((nf, krows, KW_COLUMNS), bf),
            vm((nf, rows, -(-krows // 128) * 128), bf),
            vm((ns, rows, nf * pad), bf),
            vm((ns, rows, nf * pad), bf),
            vm((groups, per * rows, HEAD_SIZE), bf),
            vm((groups, per * rows, HEAD_SIZE), bf),
            vm((groups, rows + WINDOW, 2 * HEAD_SIZE), bf),
            vm((groups, rows, 2 * HEAD_SIZE), f32),
            vm((groups, WINDOW, 2 * HEAD_SIZE), bf),
            vm((groups, WINDOW, 2 * HEAD_SIZE), bf),
            vm((ns, rows, KW_COLUMNS), bf),
            vm((nz * pad, KW_COLUMNS), bf),
            vm((nz * pad, KW_COLUMNS), bf),
            vm((nz, pad, KW_COLUMNS), f32),
            vm((nz - 1, pad, KW_COLUMNS), bf),
            vm((nz - 1, pad, KW_COLUMNS), bf),
            sem((nz - 1,)), sem((nz - 1,)),
            sem((nz - 1, ns - 1)), sem((nz - 1, ns - 1)),
            sem((nz,)), sem((nz,)),
            sem((ns - 1,)), sem((ns - 1,)),
            sem, sem,
            sem((groups,)), sem((groups,)),
            sem((ns - 1,)), sem((ns - 1,)),
            sem, sem,
            sem((nz - 1,)), sem((nz - 1,)),
        ],
        compiler_params=pltpu.CompilerParams(
            collective_id=0, has_side_effects=True, vmem_limit_bytes=48 * 1024 * 1024
        ),
    )(tokens[0], queries[0], kv_weight, esink, ct, st, out_grad[0])
    return (attn[None], qgrad[None], tgrad[None], wgrad.reshape(1, -1, 128))


def fits_fused(mesh):
    nf, ns = mesh.shape["fsdp"], mesh.shape["seq"]
    return nf == 8 and KW_COLUMNS == 128 * ns


def solution(mesh):
    placed = (
        P("fsdp", "seq", None),
        P("fsdp", "seq", None),
        P("fsdp", None),
        P(),
        P("fsdp"),
        P("fsdp", "seq", None),
    )
    return jax.shard_map(
        fused if fits_fused(mesh) else local,
        mesh=mesh,
        in_specs=placed,
        out_specs=(
            P("fsdp", "seq", None),
            P("fsdp", "seq", None),
            P("fsdp", "seq", None),
            P("seq", "fsdp", None),
        ),
        check_vma=False,
    )
```

```python
import functools

import jax
import jax.numpy as jnp
from jax import lax
from jax.experimental import pallas as pl
from jax.experimental.pallas import tpu as pltpu
from jax.sharding import PartitionSpec as P

QUERY_HEADS = 32
KEY_VALUE_HEADS = 4
HEAD_SIZE = 64
WINDOW = 128


rope_base = 150000.0


def from_behind(array, axis, by):
    peers = lax.axis_size(axis)
    pairs = [(i, i + by) for i in range(peers) if 0 <= i + by < peers]
    return lax.ppermute(array, axis, pairs)


def rope_tables(positions):
    half_width = HEAD_SIZE // 2
    frequency = rope_base ** (-jnp.arange(half_width, dtype=jnp.float32) / half_width)
    angle = positions.astype(jnp.float32)[:, None] * frequency[None, :]
    return (jnp.cos(angle), jnp.sin(angle))


def apply_rotary(values, cosine_lookup, sine_lookup, head_count, direction):
    row_count = values.shape[0]
    halves = values.reshape(row_count, head_count, 2, HEAD_SIZE // 2)
    front_half = halves[:, :, 0]
    back_half = halves[:, :, 1]
    cosine_rows = cosine_lookup[:, None, :]
    sine_rows = sine_lookup[:, None, :] * direction
    turned = jnp.stack(
        [
            front_half * cosine_rows - back_half * sine_rows,
            front_half * sine_rows + back_half * cosine_rows,
        ],
        axis=2,
    )
    return turned.reshape(row_count, head_count * HEAD_SIZE)


def attend_group(query_g, key_g, value_g, grad_g, sink_g, allowed):
    score_scale = HEAD_SIZE ** (-0.5)
    scores = (
        jnp.einsum("bgd,kd->gbk", query_g, key_g, preferred_element_type=jnp.float32) * score_scale
    )
    exponent = jnp.where(allowed[None], jnp.exp(scores), 0.0)
    denominator = jnp.exp(sink_g)[:, None] + jnp.sum(exponent, axis=2)
    softmax_w = exponent / denominator[:, :, None]
    softmax_b = softmax_w.astype(jnp.bfloat16)
    attended = jnp.einsum("gbk,kd->bgd", softmax_b, value_g, preferred_element_type=jnp.float32)
    dprob = jnp.einsum("bgd,kd->gbk", grad_g, value_g, preferred_element_type=jnp.float32)
    row_delta = jnp.sum(softmax_w * dprob, axis=2)
    dscore = (softmax_w * (dprob - row_delta[:, :, None]) * score_scale).astype(jnp.bfloat16)
    query_diff = jnp.einsum("gbk,kd->bgd", dscore, key_g, preferred_element_type=jnp.float32)
    key_diff = jnp.einsum("gbk,bgd->kd", dscore, query_g, preferred_element_type=jnp.float32)
    value_diff = jnp.einsum("gbk,bgd->kd", softmax_b, grad_g, preferred_element_type=jnp.float32)
    return (attended.astype(jnp.bfloat16), query_diff, key_diff, value_diff)


def attend_block(query_block, key_block, gradient_block, sink_logit_values, key_first):
    block_row_span = query_block.shape[0]
    key_row_slice = key_block.shape[0]
    group_width = QUERY_HEADS // KEY_VALUE_HEADS
    key_span_width = KEY_VALUE_HEADS * HEAD_SIZE
    rows_idx = jnp.arange(block_row_span, dtype=jnp.int32)[:, None]
    cols_idx = jnp.arange(key_row_slice, dtype=jnp.int32)[None, :]
    allowed = (cols_idx > rows_idx) & (cols_idx <= rows_idx + WINDOW) & (cols_idx + key_first >= 0)
    query_head_rows = query_block.reshape(
        block_row_span, KEY_VALUE_HEADS, group_width, HEAD_SIZE
    ).transpose(1, 0, 2, 3)
    gradient_heads = gradient_block.reshape(
        block_row_span, KEY_VALUE_HEADS, group_width, HEAD_SIZE
    ).transpose(1, 0, 2, 3)
    key_head_rows = (
        key_block[:, :key_span_width]
        .reshape(key_row_slice, KEY_VALUE_HEADS, HEAD_SIZE)
        .transpose(1, 0, 2)
    )
    value_head_rows = (
        key_block[:, key_span_width:]
        .reshape(key_row_slice, KEY_VALUE_HEADS, HEAD_SIZE)
        .transpose(1, 0, 2)
    )
    sink_per_head = sink_logit_values.reshape(KEY_VALUE_HEADS, group_width)

    def per_group(packed):
        return attend_group(packed[0], packed[1], packed[2], packed[3], packed[4], allowed)

    attended, query_diff, key_diff, value_diff = lax.map(
        per_group, (query_head_rows, key_head_rows, value_head_rows, gradient_heads, sink_per_head)
    )
    attended = attended.transpose(1, 0, 2, 3).reshape(block_row_span, QUERY_HEADS * HEAD_SIZE)
    query_diff = query_diff.transpose(1, 0, 2, 3).reshape(block_row_span, QUERY_HEADS * HEAD_SIZE)
    kv_diff = jnp.concatenate(
        [
            key_diff.transpose(1, 0, 2).reshape(key_row_slice, key_span_width),
            value_diff.transpose(1, 0, 2).reshape(key_row_slice, key_span_width),
        ],
        axis=1,
    )
    return (attended, query_diff, kv_diff)


def band_pass(query_rot, keys_all, grad_out, sink_logit_values, row_start):
    row_total = query_rot.shape[0]
    block_row_span = min(row_total, 512)

    def block_step(grad_all, block_index):
        block_begin = block_index * block_row_span
        attended, query_diff, kv_diff = attend_block(
            query_rot, keys_all, grad_out, sink_logit_values, row_start + block_begin - WINDOW
        )
        previous = grad_all
        grad_all = previous + kv_diff
        return (grad_all, (attended, query_diff))

    start_grad = jnp.zeros((row_total + WINDOW, keys_all.shape[1]), jnp.float32)
    grad_all, (attended, query_diff) = lax.scan(
        block_step, start_grad, jnp.arange(row_total // block_row_span, dtype=jnp.int32)
    )
    return (
        attended.reshape(row_total, QUERY_HEADS * HEAD_SIZE),
        query_diff.reshape(row_total, QUERY_HEADS * HEAD_SIZE),
        grad_all,
    )


def local(tokens, queries, kv_weight, sink_logit_values, roll_offsets, out_grad):
    token_rows = tokens[0]
    query_rows = queries[0]
    grad_rows = out_grad[0]
    row_total = token_rows.shape[0]
    key_span_width = KEY_VALUE_HEADS * HEAD_SIZE
    seq_index = lax.axis_index("seq")
    seq_count = lax.axis_size("seq")
    stream_length = row_total * seq_count
    row_start = seq_index * row_total
    whole_weight = lax.all_gather(kv_weight, "fsdp", axis=0, tiled=True)
    projected_rows = jnp.dot(token_rows, whole_weight, preferred_element_type=jnp.float32)
    positions = (
        row_start + jnp.arange(row_total, dtype=jnp.int32) + roll_offsets[0]
    ) % stream_length
    cosine_lookup, sine_lookup = rope_tables(positions)
    key_value_rotated = jnp.concatenate(
        [
            apply_rotary(
                projected_rows[:, :key_span_width], cosine_lookup, sine_lookup, KEY_VALUE_HEADS, 1.0
            ),
            projected_rows[:, key_span_width:],
        ],
        axis=1,
    ).astype(jnp.bfloat16)
    query_rot = apply_rotary(
        query_rows.astype(jnp.float32), cosine_lookup, sine_lookup, QUERY_HEADS, 1.0
    ).astype(jnp.bfloat16)
    edge_rows = from_behind(key_value_rotated, "seq", 1)
    keys_all = jnp.concatenate([edge_rows, key_value_rotated], axis=0)
    attended, query_diff, grad_all = band_pass(
        query_rot, keys_all, grad_rows, sink_logit_values, row_start
    )
    incoming = from_behind(grad_all[:WINDOW].astype(jnp.bfloat16), "seq", -1).astype(jnp.float32)
    local_gradient = grad_all[WINDOW:]
    local_gradient = jnp.concatenate(
        [local_gradient[: row_total - WINDOW], local_gradient + incoming], axis=0
    )
    query_back = apply_rotary(query_diff, cosine_lookup, sine_lookup, QUERY_HEADS, -1.0).astype(
        jnp.bfloat16
    )
    key_value_backward = jnp.concatenate(
        [
            apply_rotary(
                local_gradient[:, :key_span_width],
                cosine_lookup,
                sine_lookup,
                KEY_VALUE_HEADS,
                -1.0,
            ),
            local_gradient[:, key_span_width:],
        ],
        axis=1,
    ).astype(jnp.bfloat16)
    token_back = lax.dot_general(
        key_value_backward,
        whole_weight,
        (((1,), (1,)), ((), ())),
        preferred_element_type=jnp.float32,
    ).astype(jnp.bfloat16)
    feature_block = lax.all_to_all(token_rows, "seq", split_axis=1, concat_axis=0, tiled=True)
    block_term = lax.dot_general(
        feature_block,
        lax.all_gather(key_value_backward, "seq", axis=0, tiled=True),
        (((0,), (0,)), ((), ())),
        preferred_element_type=jnp.float32,
    )
    flat_block = block_term.reshape(-1, 128)
    weight_share = lax.psum_scatter(flat_block, "fsdp", scatter_dimension=0, tiled=True)
    return (attended[None], query_back[None], token_back[None], weight_share[None])


def nt(a, b):
    return lax.dot_general(a, b, (((1,), (1,)), ((), ())), preferred_element_type=jnp.float32)


def tn(a, b):
    return lax.dot_general(a, b, (((0,), (0,)), ((), ())), preferred_element_type=jnp.float32)


def nn(a, b):
    return lax.dot_general(a, b, (((1,), (0,)), ((), ())), preferred_element_type=jnp.float32)


def turn(x, cosine, sine, back):
    width = x.shape[1]
    lane = lax.broadcasted_iota(jnp.int32, x.shape, 1)
    swapped = jnp.where(
        lane % HEAD_SIZE < HEAD_SIZE // 2,
        pltpu.roll(x, width - HEAD_SIZE // 2, 1),
        pltpu.roll(x, HEAD_SIZE // 2, 1),
    )
    times = width // cosine.shape[1]
    cosine = jnp.concatenate([cosine] * times, axis=1)
    sine = jnp.concatenate([sine] * times, axis=1)
    if back:
        return x * cosine - swapped * sine
    return x * cosine + swapped * sine


def fused_kernel(
    nz, ns, share, pad,
    tok_hbm, q_hbm, w, esink, table, og_hbm,
    attn, qgrad, tgrad, wgrad,
    wall, tok, q, og, tokf, tokpad, tokblk, qs, gs, kvbuf, maskf, prob_t, dscore_t,
    own_g, hg_out, hg_in, dkv_all, core_out, core_in, mine, zsum, z_out, z_in,
    attn_v, qgrad_v, tgrad_v,
    ins, outs, zs, zr, qsn, qrn, ps, pr, ts, tr, hs, hr, gsn, grn, dsn, drn, cs, cr, rs, rr,
):
    nf = 2 * nz
    rows = q.shape[0]
    krows = w.shape[0]
    groups = KEY_VALUE_HEADS
    per = QUERY_HEADS // KEY_VALUE_HEADS
    span = per * HEAD_SIZE
    half = nz * pad
    f = lax.axis_index("fsdp")
    s = lax.axis_index("seq")
    z = f // 2
    c = f % 2
    partner = (f + 1 - 2 * c, s)

    def zpeer(d):
        return lax.rem(z + d, nz) * 2 + c

    def speer(d):
        return lax.rem(s + d, ns)

    def remote(src, dst, a, b, dev):
        return pltpu.make_async_remote_copy(
            src_ref=src, dst_ref=dst, send_sem=a, recv_sem=b,
            device_id=dev, device_id_type=pl.DeviceIdType.MESH,
        )

    def lanes_of(i, size):
        return pl.ds(pl.multiple_of(i * size, 128), size)

    cols = lanes_of(s, 128)
    loads = [
        pltpu.make_async_copy(w, wall.at[f], ins.at[0]),
        pltpu.make_async_copy(tok_hbm, tok, ins.at[1]),
        pltpu.make_async_copy(q_hbm, q, ins.at[2]),
        pltpu.make_async_copy(og_hbm, og, ins.at[3]),
    ]
    for cp in loads:
        cp.start()

    barrier = pltpu.get_barrier_semaphore()
    for d in range(1, nz):
        pl.semaphore_signal(barrier, inc=1, device_id=(zpeer(d), s), device_id_type=pl.DeviceIdType.MESH)
    for d in range(1, ns):
        pl.semaphore_signal(barrier, inc=1, device_id=(f, speer(d)), device_id_type=pl.DeviceIdType.MESH)
    pl.semaphore_signal(barrier, inc=1, device_id=partner, device_id_type=pl.DeviceIdType.MESH)
    pl.semaphore_wait(barrier, nz + ns - 1)

    sent = []

    def send(*args):
        cp = remote(*args)
        cp.start()
        sent.append(cp)

    for d in range(1, nz):
        send(w.at[:, cols], wall.at[f, :, cols], zs.at[d - 1], zr.at[d - 1], (zpeer(d), s))
    send(w, wall.at[f], ps.at[0], pr.at[0], partner)

    loads[1].wait()
    for i in range(nf):
        tokf[i, :, :krows] = tok[i * krows : (i + 1) * krows, :].T
    r = lax.broadcasted_iota(jnp.int32, maskf.shape, 1) % rows
    k = lax.broadcasted_iota(jnp.int32, maskf.shape, 0)
    allowed = (k > r) & (k <= r + WINDOW) & (k + s * rows - WINDOW >= 0)
    maskf[...] = allowed.astype(jnp.float32)
    turns = table[...]
    cosine = jnp.concatenate([turns[:, :HEAD_SIZE]] * 2, axis=1)
    sine = jnp.concatenate([turns[:, HEAD_SIZE:]] * 2, axis=1)

    for d in range(1, nz):
        block = lax.rem(z + nz - d, nz) * 2 + c
        remote(w.at[:, cols], wall.at[block, :, cols], zs.at[d - 1], zr.at[d - 1], (zpeer(d), s)).wait_recv()
        for e in range(1, ns):
            piece = wall.at[block, :, cols]
            send(piece, piece, qsn.at[d - 1, e - 1], qrn.at[d - 1, e - 1], (f, speer(e)))

    tokpad[...] = jnp.zeros_like(tokpad)
    for t in range(ns):
        for j in range(2):
            for i in range(nz):
                start = (t * nf + 2 * i + j) * share
                to = (j * nz + i) * pad
                tokpad[t, to : to + share, :] = tok[start : start + share, :]
    for e in range(1, ns):
        send(tokpad.at[speer(e)], tokblk.at[:, cols], ts.at[e - 1], tr.at[e - 1], (f, speer(e)))
    tokblk[:, cols] = tokpad[s]

    loads[2].wait()
    loads[3].wait()

    @pl.loop(0, groups)
    def _(g):
        here = lanes_of(g, span)
        x = turn(q[:, here].astype(jnp.float32), cosine, sine, False).astype(jnp.bfloat16)
        x = x * jnp.asarray(HEAD_SIZE ** (-0.5), jnp.bfloat16)
        o = og[:, here]
        for h in range(per):
            qs[g, h * rows : (h + 1) * rows, :] = x[:, h * HEAD_SIZE : (h + 1) * HEAD_SIZE]
            gs[g, h * rows : (h + 1) * rows, :] = o[:, h * HEAD_SIZE : (h + 1) * HEAD_SIZE]

    def part(block):
        return nn(tokf[block][:, :krows], wall[block])

    loads[0].wait()
    total = part(f)
    other = f + 1 - 2 * c
    remote(w, wall.at[other], ps.at[0], pr.at[0], partner).wait_recv()
    total = total + part(other)
    for d in range(1, nz):
        block = lax.rem(z + nz - d, nz) * 2 + c
        for e in range(1, ns):
            piece = wall.at[block, :, lanes_of(lax.rem(s + ns - e, ns), 128)]
            remote(piece, piece, qsn.at[d - 1, e - 1], qrn.at[d - 1, e - 1], (f, speer(e))).wait_recv()
        send(wall.at[block], wall.at[block], ps.at[d], pr.at[d], partner)
        total = total + part(block)
    for d in range(1, nz):
        block = lax.rem(z + nz - d, nz) * 2 + 1 - c
        remote(wall.at[block], wall.at[block], ps.at[d], pr.at[d], partner).wait_recv()
        total = total + part(block)

    key_width = groups * HEAD_SIZE
    keys = turn(total[:, :key_width], cosine, sine, False).astype(jnp.bfloat16)
    values = total[:, key_width:].astype(jnp.bfloat16)
    for g in range(groups):
        lo, hi = g * HEAD_SIZE, (g + 1) * HEAD_SIZE
        kvbuf[g, WINDOW:, :] = jnp.concatenate([keys[:, lo:hi], values[:, lo:hi]], axis=1)
    halo = remote(
        kvbuf.at[:, pl.ds(WINDOW, WINDOW), :], kvbuf.at[:, pl.ds(0, WINDOW), :], hs, hr, (f, speer(1))
    )
    halo.start()
    halo.wait()
    before = speer(ns - 1)
    mine_rows = pl.ds(pl.multiple_of(s * rows, 128), rows)

    def hg_copy(g):
        return remote(hg_out.at[g], hg_in.at[g], gsn.at[g], grn.at[g], (f, before))

    def out_copies(g):
        here = lanes_of(g, span)
        return (
            pltpu.make_async_copy(attn_v.at[:, here], attn.at[:, here], outs.at[0, g]),
            pltpu.make_async_copy(qgrad_v.at[:, here], qgrad.at[:, here], outs.at[1, g]),
        )

    def attention(g):
        kv = kvbuf[g]
        key, value = kv[:, :HEAD_SIZE], kv[:, HEAD_SIZE:]
        kv_t = kv.T
        key_t, value_t = kv_t[:HEAD_SIZE], kv_t[HEAD_SIZE:]
        for p in range(per // 2):
            two = slice(p * 2 * rows, (p + 1) * 2 * rows)
            query, grad = qs[g, two, :], gs[g, two, :]
            expo = jnp.where(maskf[...] > 0.0, jnp.exp(nt(key, query)), 0.0)
            denominator = esink[g * (per // 2) + p] + jnp.sum(expo, axis=0, keepdims=True)
            probs = expo * (1.0 / denominator)
            probs_b = probs.astype(jnp.bfloat16)
            dprob = nt(value, grad)
            delta = jnp.sum(probs * dprob, axis=0, keepdims=True)
            dscore = (probs * (dprob - delta)).astype(jnp.bfloat16)
            prob_t[:, two] = probs_b
            dscore_t[:, two] = dscore
            out = nn(value_t, probs_b)
            dq = nn(key_t, dscore) * (HEAD_SIZE ** (-0.5))
            out = jnp.concatenate([out[:, :rows], out[:, rows:]], axis=0).T
            dq = jnp.concatenate([dq[:, :rows], dq[:, rows:]], axis=0).T
            here = pl.ds(pl.multiple_of(g * span + p * 128, 128), 128)
            attn_v[:, here] = out.astype(jnp.bfloat16)
            qgrad_v[:, here] = turn(dq, cosine, sine, True).astype(jnp.bfloat16)
        dkv = jnp.concatenate([nn(dscore_t[...], qs[g]), nn(prob_t[...], gs[g])], axis=1)
        hg_out[g] = dkv[:WINDOW].astype(jnp.bfloat16)
        own_g[g] = dkv[WINDOW:]
        hg_copy(g).start()
        for cp in out_copies(g):
            cp.start()

    def dkv_copy(g, e):
        piece = dkv_all.at[g, mine_rows, :]
        return remote(piece, piece, dsn.at[g, e - 1], drn.at[g, e - 1], (f, speer(e)))

    def finish(g):
        hg_copy(g).wait_recv()
        both = own_g[g] + hg_in[g].astype(jnp.float32)
        lane = lax.broadcasted_iota(jnp.int32, both.shape, 1)
        dkv = jnp.where(lane < HEAD_SIZE, turn(both, cosine, sine, True), both)
        dkv_all[g, mine_rows, :] = dkv.astype(jnp.bfloat16)
        for e in range(1, ns):
            dkv_copy(g, e).start()

    def core_copy(g):
        return remote(core_out.at[g], core_in.at[g], cs.at[g], cr.at[g], partner)

    def weight_part(g):
        for e in range(1, ns):
            src = lax.rem(s + ns - e, ns)
            piece = dkv_all.at[g, pl.ds(pl.multiple_of(src * rows, 128), rows), :]
            remote(piece, piece, dsn.at[g, e - 1], drn.at[g, e - 1], (f, src)).wait_recv()
        dkv = dkv_all[g]
        theirs = tokblk[pl.ds(pl.multiple_of((1 - c) * half, 128), half), :]
        core_out[g] = nn(theirs, dkv).astype(jnp.bfloat16)
        core_copy(g).start()
        mine[g] = nn(tokblk[pl.ds(pl.multiple_of(c * half, 128), half), :], dkv)

    def z_copy(g, d):
        return remote(z_out.at[g, d - 1], z_in.at[g, d - 1], rs.at[g, d - 1], rr.at[g, d - 1], (zpeer(d), s))

    def z_part(g):
        core_copy(g).wait_recv()
        zsum[g] = (mine[g] + core_in[g].astype(jnp.float32)).reshape(nz, pad, 128)
        for d in range(1, nz):
            z_out[g, d - 1] = zsum[g, lax.rem(z + d, nz)].astype(jnp.bfloat16)
            z_copy(g, d).start()

    def token_blocks():
        for e in range(1, ns):
            src = lax.rem(s + ns - e, ns)
            remote(tokpad.at[src], tokblk.at[:, lanes_of(src, 128)], ts.at[e - 1], tr.at[e - 1], (f, src)).wait_recv()

    @pl.loop(0, groups)
    def _(g):
        attention(g)

        @pl.when(g >= 1)
        def _():
            finish(g - 1)

        @pl.when(g == 2)
        def _():
            token_blocks()

        @pl.when(g >= 2)
        def _():
            weight_part(g - 2)

        @pl.when(g >= 3)
        def _():
            z_part(g - 3)

    finish(groups - 1)
    weight_part(groups - 2)
    z_part(groups - 3)
    pieces = [dkv_all[g, mine_rows, :] for g in range(groups)]
    dkv = jnp.concatenate([b[:, :HEAD_SIZE] for b in pieces] + [b[:, HEAD_SIZE:] for b in pieces], axis=1)
    for i in range(nf):
        tgrad_v[i * krows : (i + 1) * krows, :] = nt(wall[i], dkv).astype(jnp.bfloat16)
    tg_copy = pltpu.make_async_copy(tgrad_v, tgrad, outs.at[2, 0])
    tg_copy.start()
    weight_part(groups - 1)
    z_part(groups - 2)
    z_part(groups - 1)

    sums = []
    for g in range(groups):
        acc = zsum[g, z]
        for d in range(1, nz):
            z_copy(g, d).wait_recv()
            acc = acc + z_in[g, d - 1].astype(jnp.float32)
        sums.append(acc[:share])
    order = []
    for lo in (0, HEAD_SIZE):
        for g in range(0, groups, 2):
            order.append(jnp.concatenate([sums[g][:, lo : lo + HEAD_SIZE], sums[g + 1][:, lo : lo + HEAD_SIZE]], axis=1))
    for j in range(groups):
        wgrad[pl.ds(j, share, stride=groups), :] = order[j]

    for cp in sent:
        cp.wait_send()
    for g in range(groups):
        hg_copy(g).wait_send()
        core_copy(g).wait_send()
        for e in range(1, ns):
            dkv_copy(g, e).wait_send()
        for d in range(1, nz):
            z_copy(g, d).wait_send()
        for cp in out_copies(g):
            cp.wait()
    tg_copy.wait()


KW_COLUMNS = 2 * KEY_VALUE_HEADS * HEAD_SIZE


def fused(tokens, queries, kv_weight, sink_logit_values, roll_offsets, out_grad):
    nf = lax.axis_size("fsdp")
    ns = lax.axis_size("seq")
    nz = nf // 2
    rows, width = tokens.shape[1:]
    krows = kv_weight.shape[0]
    share = width // (nf * ns)
    pad = -(-share // 16) * 16
    half = nz * pad
    query_width = QUERY_HEADS * HEAD_SIZE
    groups = KEY_VALUE_HEADS
    per = QUERY_HEADS // groups
    positions = (
        lax.axis_index("seq") * rows + jnp.arange(rows, dtype=jnp.int32) + roll_offsets[0]
    ) % (rows * ns)
    cosine, sine = rope_tables(positions)
    table = jnp.concatenate([cosine, cosine, -sine, sine], axis=1)
    esink = jnp.broadcast_to(
        jnp.exp(sink_logit_values).reshape(QUERY_HEADS // 2, 1, 2, 1), (QUERY_HEADS // 2, 1, 2, rows)
    ).reshape(QUERY_HEADS // 2, 1, 2 * rows)
    bf, f32 = jnp.bfloat16, jnp.float32
    sem = pltpu.SemaphoreType.DMA
    vm = pltpu.VMEM
    shape = jax.ShapeDtypeStruct
    anywhere = pl.BlockSpec(memory_space=pl.ANY)
    inside = pl.BlockSpec(memory_space=pltpu.VMEM)
    attn, qgrad, tgrad, wgrad = pl.pallas_call(
        functools.partial(fused_kernel, nz, ns, share, pad),
        out_shape=(
            shape((rows, query_width), bf),
            shape((rows, query_width), bf),
            shape((width, rows), bf),
            shape((share * groups, 128), f32),
        ),
        in_specs=[anywhere, anywhere, anywhere, inside, inside, anywhere],
        out_specs=[anywhere, anywhere, anywhere, inside],
        scratch_shapes=[
            vm((nf, krows, KW_COLUMNS), bf),
            vm((width, rows), bf),
            vm((rows, query_width), bf),
            vm((rows, query_width), bf),
            vm((nf, rows, -(-krows // 128) * 128), bf),
            vm((ns, nf * pad, rows), bf),
            vm((nf * pad, ns * rows), bf),
            vm((groups, per * rows, HEAD_SIZE), bf),
            vm((groups, per * rows, HEAD_SIZE), bf),
            vm((groups, rows + WINDOW, 2 * HEAD_SIZE), bf),
            vm((rows + WINDOW, 2 * rows), f32),
            vm((rows + WINDOW, per * rows), bf),
            vm((rows + WINDOW, per * rows), bf),
            vm((groups, rows, 2 * HEAD_SIZE), f32),
            vm((groups, WINDOW, 2 * HEAD_SIZE), bf),
            vm((groups, WINDOW, 2 * HEAD_SIZE), bf),
            vm((groups, ns * rows, 2 * HEAD_SIZE), bf),
            vm((groups, half, 128), bf),
            vm((groups, half, 128), bf),
            vm((groups, half, 128), f32),
            vm((groups, nz, pad, 128), f32),
            vm((groups, nz - 1, pad, 128), bf),
            vm((groups, nz - 1, pad, 128), bf),
            vm((rows, query_width), bf),
            vm((rows, query_width), bf),
            vm((width, rows), bf),
            sem((4,)), sem((3, groups)),
            sem((nz - 1,)), sem((nz - 1,)),
            sem((nz - 1, ns - 1)), sem((nz - 1, ns - 1)),
            sem((nz,)), sem((nz,)),
            sem((ns - 1,)), sem((ns - 1,)),
            sem, sem,
            sem((groups,)), sem((groups,)),
            sem((groups, ns - 1)), sem((groups, ns - 1)),
            sem((groups,)), sem((groups,)),
            sem((groups, nz - 1)), sem((groups, nz - 1)),
        ],
        compiler_params=pltpu.CompilerParams(
            collective_id=0, has_side_effects=True, vmem_limit_bytes=56 * 1024 * 1024
        ),
    )(tokens[0].T, queries[0], kv_weight, esink, table, out_grad[0])
    return (attn[None], qgrad[None], tgrad.T[None], wgrad[None])


def fits_fused(mesh):
    nf, ns = mesh.shape["fsdp"], mesh.shape["seq"]
    return nf == 8 and KW_COLUMNS == 128 * ns


def solution(mesh):
    placed = (
        P("fsdp", "seq", None),
        P("fsdp", "seq", None),
        P("fsdp", None),
        P(),
        P("fsdp"),
        P("fsdp", "seq", None),
    )
    return jax.shard_map(
        fused if fits_fused(mesh) else local,
        mesh=mesh,
        in_specs=placed,
        out_specs=(
            P("fsdp", "seq", None),
            P("fsdp", "seq", None),
            P("fsdp", "seq", None),
            P("seq", "fsdp", None),
        ),
        check_vma=False,
    )
```

```python
import functools
import math

import jax
import jax.numpy as jnp
from jax import lax
from jax.experimental import pallas as pl
from jax.experimental.pallas import tpu as pltpu
from jax.sharding import PartitionSpec as P

QUERY_HEADS = 32
KEY_VALUE_HEADS = 4
HEAD_SIZE = 64
WINDOW = 128


rope_base = 150000.0


def from_behind(array, axis, by):
    peers = lax.axis_size(axis)
    pairs = [(i, i + by) for i in range(peers) if 0 <= i + by < peers]
    return lax.ppermute(array, axis, pairs)


def rope_tables(positions):
    half_width = HEAD_SIZE // 2
    frequency = rope_base ** (-jnp.arange(half_width, dtype=jnp.float32) / half_width)
    angle = positions.astype(jnp.float32)[:, None] * frequency[None, :]
    return (jnp.cos(angle), jnp.sin(angle))


def apply_rotary(values, cosine_lookup, sine_lookup, head_count, direction):
    row_count = values.shape[0]
    halves = values.reshape(row_count, head_count, 2, HEAD_SIZE // 2)
    front_half = halves[:, :, 0]
    back_half = halves[:, :, 1]
    cosine_rows = cosine_lookup[:, None, :]
    sine_rows = sine_lookup[:, None, :] * direction
    turned = jnp.stack(
        [
            front_half * cosine_rows - back_half * sine_rows,
            front_half * sine_rows + back_half * cosine_rows,
        ],
        axis=2,
    )
    return turned.reshape(row_count, head_count * HEAD_SIZE)


def attend_group(query_g, key_g, value_g, grad_g, sink_g, allowed):
    score_scale = HEAD_SIZE ** (-0.5)
    scores = (
        jnp.einsum("bgd,kd->gbk", query_g, key_g, preferred_element_type=jnp.float32) * score_scale
    )
    exponent = jnp.where(allowed[None], jnp.exp(scores), 0.0)
    denominator = jnp.exp(sink_g)[:, None] + jnp.sum(exponent, axis=2)
    softmax_w = exponent / denominator[:, :, None]
    softmax_b = softmax_w.astype(jnp.bfloat16)
    attended = jnp.einsum("gbk,kd->bgd", softmax_b, value_g, preferred_element_type=jnp.float32)
    dprob = jnp.einsum("bgd,kd->gbk", grad_g, value_g, preferred_element_type=jnp.float32)
    row_delta = jnp.sum(softmax_w * dprob, axis=2)
    dscore = (softmax_w * (dprob - row_delta[:, :, None]) * score_scale).astype(jnp.bfloat16)
    query_diff = jnp.einsum("gbk,kd->bgd", dscore, key_g, preferred_element_type=jnp.float32)
    key_diff = jnp.einsum("gbk,bgd->kd", dscore, query_g, preferred_element_type=jnp.float32)
    value_diff = jnp.einsum("gbk,bgd->kd", softmax_b, grad_g, preferred_element_type=jnp.float32)
    return (attended.astype(jnp.bfloat16), query_diff, key_diff, value_diff)


def attend_block(query_block, key_block, gradient_block, sink_logit_values, key_first):
    block_row_span = query_block.shape[0]
    key_row_slice = key_block.shape[0]
    group_width = QUERY_HEADS // KEY_VALUE_HEADS
    key_span_width = KEY_VALUE_HEADS * HEAD_SIZE
    rows_idx = jnp.arange(block_row_span, dtype=jnp.int32)[:, None]
    cols_idx = jnp.arange(key_row_slice, dtype=jnp.int32)[None, :]
    allowed = (cols_idx > rows_idx) & (cols_idx <= rows_idx + WINDOW) & (cols_idx + key_first >= 0)
    query_head_rows = query_block.reshape(
        block_row_span, KEY_VALUE_HEADS, group_width, HEAD_SIZE
    ).transpose(1, 0, 2, 3)
    gradient_heads = gradient_block.reshape(
        block_row_span, KEY_VALUE_HEADS, group_width, HEAD_SIZE
    ).transpose(1, 0, 2, 3)
    key_head_rows = (
        key_block[:, :key_span_width]
        .reshape(key_row_slice, KEY_VALUE_HEADS, HEAD_SIZE)
        .transpose(1, 0, 2)
    )
    value_head_rows = (
        key_block[:, key_span_width:]
        .reshape(key_row_slice, KEY_VALUE_HEADS, HEAD_SIZE)
        .transpose(1, 0, 2)
    )
    sink_per_head = sink_logit_values.reshape(KEY_VALUE_HEADS, group_width)

    def per_group(packed):
        return attend_group(packed[0], packed[1], packed[2], packed[3], packed[4], allowed)

    attended, query_diff, key_diff, value_diff = lax.map(
        per_group, (query_head_rows, key_head_rows, value_head_rows, gradient_heads, sink_per_head)
    )
    attended = attended.transpose(1, 0, 2, 3).reshape(block_row_span, QUERY_HEADS * HEAD_SIZE)
    query_diff = query_diff.transpose(1, 0, 2, 3).reshape(block_row_span, QUERY_HEADS * HEAD_SIZE)
    kv_diff = jnp.concatenate(
        [
            key_diff.transpose(1, 0, 2).reshape(key_row_slice, key_span_width),
            value_diff.transpose(1, 0, 2).reshape(key_row_slice, key_span_width),
        ],
        axis=1,
    )
    return (attended, query_diff, kv_diff)


def band_pass(query_rot, keys_all, grad_out, sink_logit_values, row_start):
    row_total = query_rot.shape[0]
    block_row_span = min(row_total, 512)

    def block_step(grad_all, block_index):
        block_begin = block_index * block_row_span
        attended, query_diff, kv_diff = attend_block(
            query_rot, keys_all, grad_out, sink_logit_values, row_start + block_begin - WINDOW
        )
        previous = grad_all
        grad_all = previous + kv_diff
        return (grad_all, (attended, query_diff))

    start_grad = jnp.zeros((row_total + WINDOW, keys_all.shape[1]), jnp.float32)
    grad_all, (attended, query_diff) = lax.scan(
        block_step, start_grad, jnp.arange(row_total // block_row_span, dtype=jnp.int32)
    )
    return (
        attended.reshape(row_total, QUERY_HEADS * HEAD_SIZE),
        query_diff.reshape(row_total, QUERY_HEADS * HEAD_SIZE),
        grad_all,
    )


def local(tokens, queries, kv_weight, sink_logit_values, roll_offsets, out_grad):
    token_rows = tokens[0]
    query_rows = queries[0]
    grad_rows = out_grad[0]
    row_total = token_rows.shape[0]
    key_span_width = KEY_VALUE_HEADS * HEAD_SIZE
    seq_index = lax.axis_index("seq")
    seq_count = lax.axis_size("seq")
    stream_length = row_total * seq_count
    row_start = seq_index * row_total
    whole_weight = lax.all_gather(kv_weight, "fsdp", axis=0, tiled=True)
    projected_rows = jnp.dot(token_rows, whole_weight, preferred_element_type=jnp.float32)
    positions = (
        row_start + jnp.arange(row_total, dtype=jnp.int32) + roll_offsets[0]
    ) % stream_length
    cosine_lookup, sine_lookup = rope_tables(positions)
    key_value_rotated = jnp.concatenate(
        [
            apply_rotary(
                projected_rows[:, :key_span_width], cosine_lookup, sine_lookup, KEY_VALUE_HEADS, 1.0
            ),
            projected_rows[:, key_span_width:],
        ],
        axis=1,
    ).astype(jnp.bfloat16)
    query_rot = apply_rotary(
        query_rows.astype(jnp.float32), cosine_lookup, sine_lookup, QUERY_HEADS, 1.0
    ).astype(jnp.bfloat16)
    edge_rows = from_behind(key_value_rotated, "seq", 1)
    keys_all = jnp.concatenate([edge_rows, key_value_rotated], axis=0)
    attended, query_diff, grad_all = band_pass(
        query_rot, keys_all, grad_rows, sink_logit_values, row_start
    )
    incoming = from_behind(grad_all[:WINDOW].astype(jnp.bfloat16), "seq", -1).astype(jnp.float32)
    local_gradient = grad_all[WINDOW:]
    local_gradient = jnp.concatenate(
        [local_gradient[: row_total - WINDOW], local_gradient + incoming], axis=0
    )
    query_back = apply_rotary(query_diff, cosine_lookup, sine_lookup, QUERY_HEADS, -1.0).astype(
        jnp.bfloat16
    )
    key_value_backward = jnp.concatenate(
        [
            apply_rotary(
                local_gradient[:, :key_span_width],
                cosine_lookup,
                sine_lookup,
                KEY_VALUE_HEADS,
                -1.0,
            ),
            local_gradient[:, key_span_width:],
        ],
        axis=1,
    ).astype(jnp.bfloat16)
    token_back = lax.dot_general(
        key_value_backward,
        whole_weight,
        (((1,), (1,)), ((), ())),
        preferred_element_type=jnp.float32,
    ).astype(jnp.bfloat16)
    feature_block = lax.all_to_all(token_rows, "seq", split_axis=1, concat_axis=0, tiled=True)
    block_term = lax.dot_general(
        feature_block,
        lax.all_gather(key_value_backward, "seq", axis=0, tiled=True),
        (((0,), (0,)), ((), ())),
        preferred_element_type=jnp.float32,
    )
    flat_block = block_term.reshape(-1, 128)
    weight_share = lax.psum_scatter(flat_block, "fsdp", scatter_dimension=0, tiled=True)
    return (attended[None], query_back[None], token_back[None], weight_share[None])


def nt(a, b):
    return lax.dot_general(a, b, (((1,), (1,)), ((), ())), preferred_element_type=jnp.float32)


def tn(a, b):
    return lax.dot_general(a, b, (((0,), (0,)), ((), ())), preferred_element_type=jnp.float32)


def nn(a, b):
    return lax.dot_general(a, b, (((1,), (0,)), ((), ())), preferred_element_type=jnp.float32)


def turn(x, cosine, sine, back):
    width = x.shape[1]
    lane = lax.broadcasted_iota(jnp.int32, x.shape, 1)
    swapped = jnp.where(
        lane % HEAD_SIZE < HEAD_SIZE // 2,
        pltpu.roll(x, width - HEAD_SIZE // 2, 1),
        pltpu.roll(x, HEAD_SIZE // 2, 1),
    )
    times = width // cosine.shape[1]
    cosine = jnp.concatenate([cosine] * times, axis=1)
    sine = jnp.concatenate([sine] * times, axis=1)
    if back:
        return x * cosine - swapped * sine
    return x * cosine + swapped * sine


def fused_kernel(
    nz, ns, share, pad,
    tok_hbm, q_hbm, w, sinks, rolls, og_hbm,
    attn_v, qgrad_v, tgrad_v, wgrad,
    wall, tok, q, og, tokf, tokpad, tokblk, qs, gs, kvbuf, maskf, prob_t, dscore_t,
    own_g, hg_out, hg_in, dkv_all, core_out, core_in, mine, zsum, z_out, z_in, total, esink,
    ins, rs_l, rr_l, rs_r, rr_r, qsn, qrn, ps, pr, ts, tr, hs, hr, gsn, grn, dsn, drn, cs, cr, rs, rr,
):
    nf = 2 * nz
    rows = q.shape[0]
    krows = w.shape[0]
    groups = KEY_VALUE_HEADS
    per = QUERY_HEADS // KEY_VALUE_HEADS
    span = per * HEAD_SIZE
    half = nz * pad
    f = lax.axis_index("fsdp")
    s = lax.axis_index("seq")
    z = f // 2
    c = f % 2
    partner = (f + 1 - 2 * c, s)

    def zpeer(d):
        return lax.rem(z + d, nz) * 2 + c

    def speer(d):
        return lax.rem(s + d, ns)

    def remote(src, dst, a, b, dev):
        return pltpu.make_async_remote_copy(
            src_ref=src, dst_ref=dst, send_sem=a, recv_sem=b,
            device_id=dev, device_id_type=pl.DeviceIdType.MESH,
        )

    def lanes_of(i, size):
        return pl.ds(pl.multiple_of(i * size, 128), size)

    cols = lanes_of(s, 128)
    loads = [
        pltpu.make_async_copy(tok_hbm, tok, ins.at[0]),
        pltpu.make_async_copy(q_hbm, q, ins.at[1]),
        pltpu.make_async_copy(og_hbm, og, ins.at[2]),
    ]
    for j in range(ns):
        own = w.at[:, j * 128 : (j + 1) * 128]
        loads.append(pltpu.make_async_copy(own, wall.at[j, f], ins.at[3 + j]))
    for cp in loads:
        cp.start()

    barrier = pltpu.get_barrier_semaphore()
    for d in range(1, nz):
        pl.semaphore_signal(barrier, inc=1, device_id=(zpeer(d), s), device_id_type=pl.DeviceIdType.MESH)
    for d in range(1, ns):
        pl.semaphore_signal(barrier, inc=1, device_id=(f, speer(d)), device_id_type=pl.DeviceIdType.MESH)
    pl.semaphore_signal(barrier, inc=1, device_id=partner, device_id_type=pl.DeviceIdType.MESH)
    pl.semaphore_wait(barrier, nz + ns - 1)

    sent = []

    def send(*args):
        cp = remote(*args)
        cp.start()
        sent.append(cp)

    def chain(k, right):
        at = z + k if right else z - k
        there = at < nz if right else at >= 0
        onward = z >= 1 if right else z + 1 < nz
        onto = ((z - 1 if right else z + 1) * 2 + c, s)
        return at * 2 + c, there, onward, onto

    def link(k, right):
        block, _, _, onto = chain(k, right)
        a, b = (rs_r, rr_r) if right else (rs_l, rr_l)
        piece = wall.at[s, block]
        source = w.at[:, cols] if k == 0 else piece
        return remote(source, piece, a.at[k], b.at[k], onto)

    def arrived(k, right):
        block, _, _, onto = chain(k, right)
        b = rr_r if right else rr_l
        piece = wall.at[s, block]
        return remote(piece, piece, rs_l.at[0], b.at[k - 1], onto)

    def over_seq(block, e):
        piece = wall.at[s, block]
        return remote(piece, piece, qsn.at[block // 2, e - 1], qrn.at[block // 2, e - 1], (f, speer(e)))

    def over_core(block):
        piece = wall.at[:, block]
        return remote(piece, piece, ps.at[block // 2], pr.at[block // 2], partner)

    ways = [(k, right) for k in range(1, nz) for right in (False, True)]

    for right in (False, True):

        @pl.when(chain(0, right)[2])
        def _(right=right):
            link(0, right).start()

    for cp in loads[3:]:
        cp.wait()
    over_core(f).start()

    loads[0].wait()
    for i in range(nf):
        tokf[i, :, :krows] = tok[i * krows : (i + 1) * krows, :].T

    for k, right in ways:
        block, there, onward, _ = chain(k, right)

        @pl.when(there)
        def _(k=k, right=right, block=block):
            arrived(k, right).wait_recv()
            for e in range(1, ns):
                over_seq(block, e).start()

        @pl.when(there & onward)
        def _(k=k, right=right):
            link(k, right).start()

    r = lax.broadcasted_iota(jnp.int32, maskf.shape, 1) % rows
    k = lax.broadcasted_iota(jnp.int32, maskf.shape, 0)
    allowed = (k > r) & (k <= r + WINDOW) & (k + s * rows - WINDOW >= 0)
    maskf[...] = allowed.astype(jnp.float32)
    lane = lax.broadcasted_iota(jnp.int32, (rows, 128), 1)
    turn_lane = (lane % (HEAD_SIZE // 2)).astype(jnp.float32) / (HEAD_SIZE // 2)
    frequency = jnp.exp(turn_lane * (-math.log(rope_base)))
    position = lax.rem(
        s * rows + rolls[0] + lax.broadcasted_iota(jnp.int32, (rows, 128), 0), rows * ns
    )
    angle = position.astype(jnp.float32) * frequency
    cosine = jnp.cos(angle)
    sine = jnp.sin(angle)
    sine = jnp.where(lane % HEAD_SIZE < HEAD_SIZE // 2, -sine, sine)
    for p in range(QUERY_HEADS // 2):
        pair = [jnp.full((1, rows), sinks[2 * p + i], jnp.float32) for i in range(2)]
        esink[p] = jnp.exp(jnp.concatenate(pair, axis=1))

    tokpad[...] = jnp.zeros_like(tokpad)
    for t in range(ns):
        for j in range(2):
            for i in range(nz):
                start = (t * nf + 2 * i + j) * share
                to = (j * nz + i) * pad
                tokpad[t, to : to + share, :] = tok[start : start + share, :]
    tokblk[s] = tokpad[s]

    loads[1].wait()
    loads[2].wait()

    @pl.loop(0, groups)
    def _(g):
        here = lanes_of(g, span)
        x = turn(q[:, here].astype(jnp.float32), cosine, sine, False).astype(jnp.bfloat16)
        x = x * jnp.asarray(HEAD_SIZE ** (-0.5), jnp.bfloat16)
        o = og[:, here]
        for h in range(per):
            qs[g, h * rows : (h + 1) * rows, :] = x[:, h * HEAD_SIZE : (h + 1) * HEAD_SIZE]
            gs[g, h * rows : (h + 1) * rows, :] = o[:, h * HEAD_SIZE : (h + 1) * HEAD_SIZE]

    def whole(block):
        return jnp.concatenate([wall[j, block] for j in range(ns)], axis=1)

    def part(block):
        return nn(tokf[block][:, :krows], whole(block))

    total[...] = part(f)
    other = f + 1 - 2 * c
    over_core(other).wait_recv()
    total[...] += part(other)
    for k, right in ways:
        block, there, _, _ = chain(k, right)

        @pl.when(there)
        def _(block=block):
            for e in range(1, ns):
                piece = wall.at[lax.rem(s + ns - e, ns), block]
                remote(
                    piece, piece, qsn.at[block // 2, e - 1], qrn.at[block // 2, e - 1], (f, speer(e))
                ).wait_recv()
            over_core(block).start()
            total[...] += part(block)

    for k, right in ways:
        block, there, _, _ = chain(k, right)

        @pl.when(there)
        def _(block=block):
            over_core(block + 1 - 2 * c).wait_recv()
            total[...] += part(block + 1 - 2 * c)

    key_width = groups * HEAD_SIZE
    keys = turn(total[:, :key_width], cosine, sine, False).astype(jnp.bfloat16)
    values = total[:, key_width:].astype(jnp.bfloat16)
    for g in range(groups):
        lo, hi = g * HEAD_SIZE, (g + 1) * HEAD_SIZE
        kvbuf[g, WINDOW:, :] = jnp.concatenate([keys[:, lo:hi], values[:, lo:hi]], axis=1)
    halo = remote(
        kvbuf.at[:, pl.ds(WINDOW, WINDOW), :], kvbuf.at[:, pl.ds(0, WINDOW), :], hs, hr, (f, speer(1))
    )
    halo.start()
    halo.wait()
    for e in range(1, ns):
        send(tokpad.at[speer(e)], tokblk.at[s], ts.at[e - 1], tr.at[e - 1], (f, speer(e)))
    before = speer(ns - 1)
    mine_rows = pl.ds(pl.multiple_of(s * rows, 128), rows)

    def hg_copy(g):
        return remote(hg_out.at[g], hg_in.at[g], gsn.at[g], grn.at[g], (f, before))

    def attention(g):
        kv = kvbuf[g]
        key, value = kv[:, :HEAD_SIZE], kv[:, HEAD_SIZE:]
        kv_t = kv.T
        key_t, value_t = kv_t[:HEAD_SIZE], kv_t[HEAD_SIZE:]
        for p in range(per // 2):
            two = slice(p * 2 * rows, (p + 1) * 2 * rows)
            query, grad = qs[g, two, :], gs[g, two, :]
            expo = jnp.where(maskf[...] > 0.0, jnp.exp(nt(key, query)), 0.0)
            denominator = esink[g * (per // 2) + p] + jnp.sum(expo, axis=0, keepdims=True)
            probs = expo * (1.0 / denominator)
            probs_b = probs.astype(jnp.bfloat16)
            dprob = nt(value, grad)
            delta = jnp.sum(probs * dprob, axis=0, keepdims=True)
            dscore = (probs * (dprob - delta)).astype(jnp.bfloat16)
            prob_t[:, two] = probs_b
            dscore_t[:, two] = dscore
            out = nn(value_t, probs_b)
            dq = nn(key_t, dscore) * (HEAD_SIZE ** (-0.5))
            out = jnp.concatenate([out[:, :rows], out[:, rows:]], axis=0).T
            dq = jnp.concatenate([dq[:, :rows], dq[:, rows:]], axis=0).T
            here = pl.ds(pl.multiple_of(g * span + p * 128, 128), 128)
            attn_v[:, here] = out.astype(jnp.bfloat16)
            qgrad_v[:, here] = turn(dq, cosine, sine, True).astype(jnp.bfloat16)
        dkv = jnp.concatenate([nn(dscore_t[...], qs[g]), nn(prob_t[...], gs[g])], axis=1)
        hg_out[g] = dkv[:WINDOW].astype(jnp.bfloat16)
        own_g[g] = dkv[WINDOW:]
        hg_copy(g).start()

    def dkv_copy(g, e):
        piece = dkv_all.at[g, mine_rows, :]
        return remote(piece, piece, dsn.at[g, e - 1], drn.at[g, e - 1], (f, speer(e)))

    def finish(g):
        hg_copy(g).wait_recv()
        both = own_g[g] + hg_in[g].astype(jnp.float32)
        lane = lax.broadcasted_iota(jnp.int32, both.shape, 1)
        dkv = jnp.where(lane < HEAD_SIZE, turn(both, cosine, sine, True), both)
        dkv_all[g, mine_rows, :] = dkv.astype(jnp.bfloat16)
        for e in range(1, ns):
            dkv_copy(g, e).start()

    def core_copy(g):
        return remote(core_out.at[g], core_in.at[g], cs.at[g], cr.at[g], partner)

    def features(core):
        there = pl.ds(pl.multiple_of(core * half, 128), half)
        return jnp.concatenate([tokblk[t, there, :] for t in range(ns)], axis=1)

    def weight_part(g):
        for e in range(1, ns):
            src = lax.rem(s + ns - e, ns)
            piece = dkv_all.at[g, pl.ds(pl.multiple_of(src * rows, 128), rows), :]
            remote(piece, piece, dsn.at[g, e - 1], drn.at[g, e - 1], (f, src)).wait_recv()
        dkv = dkv_all[g]
        core_out[g] = nn(features(1 - c), dkv).astype(jnp.bfloat16)
        core_copy(g).start()
        mine[g] = nn(features(c), dkv)

    def z_copy(g, d):
        return remote(z_out.at[g, d - 1], z_in.at[g, d - 1], rs.at[g, d - 1], rr.at[g, d - 1], (zpeer(d), s))

    def z_part(g):
        core_copy(g).wait_recv()
        zsum[g] = (mine[g] + core_in[g].astype(jnp.float32)).reshape(nz, pad, 128)
        for d in range(1, nz):
            z_out[g, d - 1] = zsum[g, lax.rem(z + d, nz)].astype(jnp.bfloat16)
            z_copy(g, d).start()

    def token_blocks():
        for e in range(1, ns):
            src = lax.rem(s + ns - e, ns)
            remote(tokpad.at[src], tokblk.at[src], ts.at[e - 1], tr.at[e - 1], (f, src)).wait_recv()

    @pl.loop(0, groups)
    def _(g):
        attention(g)

        @pl.when(g >= 1)
        def _():
            finish(g - 1)

        @pl.when(g == 2)
        def _():
            token_blocks()

        @pl.when(g >= 2)
        def _():
            weight_part(g - 2)

        @pl.when(g >= 3)
        def _():
            z_part(g - 3)

    finish(groups - 1)
    weight_part(groups - 2)
    z_part(groups - 3)
    pieces = [dkv_all[g, mine_rows, :] for g in range(groups)]
    dkv = jnp.concatenate([b[:, :HEAD_SIZE] for b in pieces] + [b[:, HEAD_SIZE:] for b in pieces], axis=1)
    for i in range(nf):
        tgrad_v[i * krows : (i + 1) * krows, :] = nt(whole(i), dkv).astype(jnp.bfloat16)
    weight_part(groups - 1)
    z_part(groups - 2)
    z_part(groups - 1)

    sums = []
    for g in range(groups):
        acc = zsum[g, z]
        for d in range(1, nz):
            z_copy(g, d).wait_recv()
            acc = acc + z_in[g, d - 1].astype(jnp.float32)
        sums.append(acc[:share])
    order = []
    for lo in (0, HEAD_SIZE):
        for g in range(0, groups, 2):
            order.append(jnp.concatenate([sums[g][:, lo : lo + HEAD_SIZE], sums[g + 1][:, lo : lo + HEAD_SIZE]], axis=1))
    for j in range(groups):
        wgrad[pl.ds(j, share, stride=groups), :] = order[j]

    for cp in sent:
        cp.wait_send()
    for g in range(groups):
        hg_copy(g).wait_send()
        core_copy(g).wait_send()
        for e in range(1, ns):
            dkv_copy(g, e).wait_send()
        for d in range(1, nz):
            z_copy(g, d).wait_send()
    for k in range(nz):
        for right in (False, True):
            _, there, onward, _ = chain(k, right)

            @pl.when(there & onward)
            def _(k=k, right=right):
                link(k, right).wait_send()

            if k > 0:

                @pl.when(there)
                def _(k=k, right=right):
                    block = chain(k, right)[0]
                    for e in range(1, ns):
                        over_seq(block, e).wait_send()
                    over_core(block).wait_send()

    over_core(f).wait_send()


def write_out(*refs):
    done = refs[8]
    copies = [pltpu.make_async_copy(refs[i], refs[4 + i], done.at[i]) for i in range(4)]
    for cp in copies:
        cp.start()
    for cp in copies:
        cp.wait()


KW_COLUMNS = 2 * KEY_VALUE_HEADS * HEAD_SIZE


def fused(tokens, queries, kv_weight, sink_logit_values, roll_offsets, out_grad):
    nf = lax.axis_size("fsdp")
    ns = lax.axis_size("seq")
    nz = nf // 2
    rows, width = tokens.shape[1:]
    krows = kv_weight.shape[0]
    share = width // (nf * ns)
    pad = -(-share // 16) * 16
    half = nz * pad
    query_width = QUERY_HEADS * HEAD_SIZE
    groups = KEY_VALUE_HEADS
    per = QUERY_HEADS // groups
    bf, f32 = jnp.bfloat16, jnp.float32
    sem = pltpu.SemaphoreType.DMA
    vm = pltpu.VMEM
    shape = jax.ShapeDtypeStruct
    anywhere = pl.BlockSpec(memory_space=pl.ANY)
    inside = pl.BlockSpec(memory_space=pltpu.VMEM)
    scalars = pl.BlockSpec(memory_space=pltpu.SMEM)
    results = pl.pallas_call(
        functools.partial(fused_kernel, nz, ns, share, pad),
        out_shape=(
            shape((rows, query_width), bf),
            shape((rows, query_width), bf),
            shape((width, rows), bf),
            shape((share * groups, 128), f32),
        ),
        in_specs=[anywhere, anywhere, anywhere, scalars, scalars, anywhere],
        out_specs=[inside] * 4,
        scratch_shapes=[
            vm((ns, nf, krows, 128), bf),
            vm((width, rows), bf),
            vm((rows, query_width), bf),
            vm((rows, query_width), bf),
            vm((nf, rows, -(-krows // 128) * 128), bf),
            vm((ns, nf * pad, rows), bf),
            vm((ns, nf * pad, rows), bf),
            vm((groups, per * rows, HEAD_SIZE), bf),
            vm((groups, per * rows, HEAD_SIZE), bf),
            vm((groups, rows + WINDOW, 2 * HEAD_SIZE), bf),
            vm((rows + WINDOW, 2 * rows), f32),
            vm((rows + WINDOW, per * rows), bf),
            vm((rows + WINDOW, per * rows), bf),
            vm((groups, rows, 2 * HEAD_SIZE), f32),
            vm((groups, WINDOW, 2 * HEAD_SIZE), bf),
            vm((groups, WINDOW, 2 * HEAD_SIZE), bf),
            vm((groups, ns * rows, 2 * HEAD_SIZE), bf),
            vm((groups, half, 128), bf),
            vm((groups, half, 128), bf),
            vm((groups, half, 128), f32),
            vm((groups, nz, pad, 128), f32),
            vm((groups, nz - 1, pad, 128), bf),
            vm((groups, nz - 1, pad, 128), bf),
            vm((rows, KW_COLUMNS), f32),
            vm((QUERY_HEADS // 2, 1, 2 * rows), f32),
            sem((3 + ns,)),
            sem((nz,)), sem((nz,)), sem((nz,)), sem((nz,)),
            sem((nz, ns - 1)), sem((nz, ns - 1)),
            sem((nz,)), sem((nz,)),
            sem((ns - 1,)), sem((ns - 1,)),
            sem, sem,
            sem((groups,)), sem((groups,)),
            sem((groups, ns - 1)), sem((groups, ns - 1)),
            sem((groups,)), sem((groups,)),
            sem((groups, nz - 1)), sem((groups, nz - 1)),
        ],
        compiler_params=pltpu.CompilerParams(
            collective_id=0, has_side_effects=True, vmem_limit_bytes=56 * 1024 * 1024
        ),
    )(tokens[0].T, queries[0], kv_weight, sink_logit_values, roll_offsets, out_grad[0])
    attn, qgrad, tgrad, wgrad = pl.pallas_call(
        write_out,
        out_shape=tuple(shape(x.shape, x.dtype) for x in results),
        in_specs=[anywhere] * 4,
        out_specs=[anywhere] * 4,
        scratch_shapes=[sem((4,))],
    )(*results)
    return (attn[None], qgrad[None], tgrad.T[None], wgrad[None])


def fits_fused(mesh):
    nf, ns = mesh.shape["fsdp"], mesh.shape["seq"]
    return nf == 8 and KW_COLUMNS == 128 * ns


def solution(mesh):
    placed = (
        P("fsdp", "seq", None),
        P("fsdp", "seq", None),
        P("fsdp", None),
        P(),
        P("fsdp"),
        P("fsdp", "seq", None),
    )
    return jax.shard_map(
        fused if fits_fused(mesh) else local,
        mesh=mesh,
        in_specs=placed,
        out_specs=(
            P("fsdp", "seq", None),
            P("fsdp", "seq", None),
            P("fsdp", "seq", None),
            P("seq", "fsdp", None),
        ),
        check_vma=False,
    )
```

```python
import functools
import math

import jax
import jax.numpy as jnp
from jax import lax
from jax.experimental import pallas as pl
from jax.experimental.pallas import tpu as pltpu
from jax.sharding import PartitionSpec as P

QUERY_HEADS = 32
KEY_VALUE_HEADS = 4
HEAD_SIZE = 64
WINDOW = 128


rope_base = 150000.0


def from_behind(array, axis, by):
    peers = lax.axis_size(axis)
    pairs = [(i, i + by) for i in range(peers) if 0 <= i + by < peers]
    return lax.ppermute(array, axis, pairs)


def rope_tables(positions):
    half_width = HEAD_SIZE // 2
    frequency = rope_base ** (-jnp.arange(half_width, dtype=jnp.float32) / half_width)
    angle = positions.astype(jnp.float32)[:, None] * frequency[None, :]
    return (jnp.cos(angle), jnp.sin(angle))


def apply_rotary(values, cosine_lookup, sine_lookup, head_count, direction):
    row_count = values.shape[0]
    halves = values.reshape(row_count, head_count, 2, HEAD_SIZE // 2)
    front_half = halves[:, :, 0]
    back_half = halves[:, :, 1]
    cosine_rows = cosine_lookup[:, None, :]
    sine_rows = sine_lookup[:, None, :] * direction
    turned = jnp.stack(
        [
            front_half * cosine_rows - back_half * sine_rows,
            front_half * sine_rows + back_half * cosine_rows,
        ],
        axis=2,
    )
    return turned.reshape(row_count, head_count * HEAD_SIZE)


def attend_group(query_g, key_g, value_g, grad_g, sink_g, allowed):
    score_scale = HEAD_SIZE ** (-0.5)
    scores = (
        jnp.einsum("bgd,kd->gbk", query_g, key_g, preferred_element_type=jnp.float32) * score_scale
    )
    exponent = jnp.where(allowed[None], jnp.exp(scores), 0.0)
    denominator = jnp.exp(sink_g)[:, None] + jnp.sum(exponent, axis=2)
    softmax_w = exponent / denominator[:, :, None]
    softmax_b = softmax_w.astype(jnp.bfloat16)
    attended = jnp.einsum("gbk,kd->bgd", softmax_b, value_g, preferred_element_type=jnp.float32)
    dprob = jnp.einsum("bgd,kd->gbk", grad_g, value_g, preferred_element_type=jnp.float32)
    row_delta = jnp.sum(softmax_w * dprob, axis=2)
    dscore = (softmax_w * (dprob - row_delta[:, :, None]) * score_scale).astype(jnp.bfloat16)
    query_diff = jnp.einsum("gbk,kd->bgd", dscore, key_g, preferred_element_type=jnp.float32)
    key_diff = jnp.einsum("gbk,bgd->kd", dscore, query_g, preferred_element_type=jnp.float32)
    value_diff = jnp.einsum("gbk,bgd->kd", softmax_b, grad_g, preferred_element_type=jnp.float32)
    return (attended.astype(jnp.bfloat16), query_diff, key_diff, value_diff)


def attend_block(query_block, key_block, gradient_block, sink_logit_values, key_first):
    block_row_span = query_block.shape[0]
    key_row_slice = key_block.shape[0]
    group_width = QUERY_HEADS // KEY_VALUE_HEADS
    key_span_width = KEY_VALUE_HEADS * HEAD_SIZE
    rows_idx = jnp.arange(block_row_span, dtype=jnp.int32)[:, None]
    cols_idx = jnp.arange(key_row_slice, dtype=jnp.int32)[None, :]
    allowed = (cols_idx > rows_idx) & (cols_idx <= rows_idx + WINDOW) & (cols_idx + key_first >= 0)
    query_head_rows = query_block.reshape(
        block_row_span, KEY_VALUE_HEADS, group_width, HEAD_SIZE
    ).transpose(1, 0, 2, 3)
    gradient_heads = gradient_block.reshape(
        block_row_span, KEY_VALUE_HEADS, group_width, HEAD_SIZE
    ).transpose(1, 0, 2, 3)
    key_head_rows = (
        key_block[:, :key_span_width]
        .reshape(key_row_slice, KEY_VALUE_HEADS, HEAD_SIZE)
        .transpose(1, 0, 2)
    )
    value_head_rows = (
        key_block[:, key_span_width:]
        .reshape(key_row_slice, KEY_VALUE_HEADS, HEAD_SIZE)
        .transpose(1, 0, 2)
    )
    sink_per_head = sink_logit_values.reshape(KEY_VALUE_HEADS, group_width)

    def per_group(packed):
        return attend_group(packed[0], packed[1], packed[2], packed[3], packed[4], allowed)

    attended, query_diff, key_diff, value_diff = lax.map(
        per_group, (query_head_rows, key_head_rows, value_head_rows, gradient_heads, sink_per_head)
    )
    attended = attended.transpose(1, 0, 2, 3).reshape(block_row_span, QUERY_HEADS * HEAD_SIZE)
    query_diff = query_diff.transpose(1, 0, 2, 3).reshape(block_row_span, QUERY_HEADS * HEAD_SIZE)
    kv_diff = jnp.concatenate(
        [
            key_diff.transpose(1, 0, 2).reshape(key_row_slice, key_span_width),
            value_diff.transpose(1, 0, 2).reshape(key_row_slice, key_span_width),
        ],
        axis=1,
    )
    return (attended, query_diff, kv_diff)


def band_pass(query_rot, keys_all, grad_out, sink_logit_values, row_start):
    row_total = query_rot.shape[0]
    block_row_span = min(row_total, 512)

    def block_step(grad_all, block_index):
        block_begin = block_index * block_row_span
        attended, query_diff, kv_diff = attend_block(
            query_rot, keys_all, grad_out, sink_logit_values, row_start + block_begin - WINDOW
        )
        previous = grad_all
        grad_all = previous + kv_diff
        return (grad_all, (attended, query_diff))

    start_grad = jnp.zeros((row_total + WINDOW, keys_all.shape[1]), jnp.float32)
    grad_all, (attended, query_diff) = lax.scan(
        block_step, start_grad, jnp.arange(row_total // block_row_span, dtype=jnp.int32)
    )
    return (
        attended.reshape(row_total, QUERY_HEADS * HEAD_SIZE),
        query_diff.reshape(row_total, QUERY_HEADS * HEAD_SIZE),
        grad_all,
    )


def local(tokens, queries, kv_weight, sink_logit_values, roll_offsets, out_grad):
    token_rows = tokens[0]
    query_rows = queries[0]
    grad_rows = out_grad[0]
    row_total = token_rows.shape[0]
    key_span_width = KEY_VALUE_HEADS * HEAD_SIZE
    seq_index = lax.axis_index("seq")
    seq_count = lax.axis_size("seq")
    stream_length = row_total * seq_count
    row_start = seq_index * row_total
    whole_weight = lax.all_gather(kv_weight, "fsdp", axis=0, tiled=True)
    projected_rows = jnp.dot(token_rows, whole_weight, preferred_element_type=jnp.float32)
    positions = (
        row_start + jnp.arange(row_total, dtype=jnp.int32) + roll_offsets[0]
    ) % stream_length
    cosine_lookup, sine_lookup = rope_tables(positions)
    key_value_rotated = jnp.concatenate(
        [
            apply_rotary(
                projected_rows[:, :key_span_width], cosine_lookup, sine_lookup, KEY_VALUE_HEADS, 1.0
            ),
            projected_rows[:, key_span_width:],
        ],
        axis=1,
    ).astype(jnp.bfloat16)
    query_rot = apply_rotary(
        query_rows.astype(jnp.float32), cosine_lookup, sine_lookup, QUERY_HEADS, 1.0
    ).astype(jnp.bfloat16)
    edge_rows = from_behind(key_value_rotated, "seq", 1)
    keys_all = jnp.concatenate([edge_rows, key_value_rotated], axis=0)
    attended, query_diff, grad_all = band_pass(
        query_rot, keys_all, grad_rows, sink_logit_values, row_start
    )
    incoming = from_behind(grad_all[:WINDOW].astype(jnp.bfloat16), "seq", -1).astype(jnp.float32)
    local_gradient = grad_all[WINDOW:]
    local_gradient = jnp.concatenate(
        [local_gradient[: row_total - WINDOW], local_gradient + incoming], axis=0
    )
    query_back = apply_rotary(query_diff, cosine_lookup, sine_lookup, QUERY_HEADS, -1.0).astype(
        jnp.bfloat16
    )
    key_value_backward = jnp.concatenate(
        [
            apply_rotary(
                local_gradient[:, :key_span_width],
                cosine_lookup,
                sine_lookup,
                KEY_VALUE_HEADS,
                -1.0,
            ),
            local_gradient[:, key_span_width:],
        ],
        axis=1,
    ).astype(jnp.bfloat16)
    token_back = lax.dot_general(
        key_value_backward,
        whole_weight,
        (((1,), (1,)), ((), ())),
        preferred_element_type=jnp.float32,
    ).astype(jnp.bfloat16)
    feature_block = lax.all_to_all(token_rows, "seq", split_axis=1, concat_axis=0, tiled=True)
    block_term = lax.dot_general(
        feature_block,
        lax.all_gather(key_value_backward, "seq", axis=0, tiled=True),
        (((0,), (0,)), ((), ())),
        preferred_element_type=jnp.float32,
    )
    flat_block = block_term.reshape(-1, 128)
    weight_share = lax.psum_scatter(flat_block, "fsdp", scatter_dimension=0, tiled=True)
    return (attended[None], query_back[None], token_back[None], weight_share[None])


def nt(a, b):
    return lax.dot_general(a, b, (((1,), (1,)), ((), ())), preferred_element_type=jnp.float32)


def tn(a, b):
    return lax.dot_general(a, b, (((0,), (0,)), ((), ())), preferred_element_type=jnp.float32)


def nn(a, b):
    return lax.dot_general(a, b, (((1,), (0,)), ((), ())), preferred_element_type=jnp.float32)


def turn(x, cosine, sine, back):
    width = x.shape[1]
    lane = lax.broadcasted_iota(jnp.int32, x.shape, 1)
    swapped = jnp.where(
        lane % HEAD_SIZE < HEAD_SIZE // 2,
        pltpu.roll(x, width - HEAD_SIZE // 2, 1),
        pltpu.roll(x, HEAD_SIZE // 2, 1),
    )
    times = width // cosine.shape[1]
    cosine = jnp.concatenate([cosine] * times, axis=1)
    sine = jnp.concatenate([sine] * times, axis=1)
    if back:
        return x * cosine - swapped * sine
    return x * cosine + swapped * sine


def fused_kernel(
    nz, ns, share, pad,
    tok_hbm, q_hbm, w, sinks, rolls, og_hbm,
    attn_v, qgrad_v, tgrad_v, wgrad,
    wall, tok, q, og, tokf, tokpad, tokblk, qs, gs, kvbuf, prob_t, dscore_t,
    own_g, hg_out, hg_in, dkv_all, core_out, core_in, mine, zsum, z_out, z_in, total, esink,
    ins, rs_l, rr_l, rs_r, rr_r, qsn, qrn, ps, pr, ts, tr, hs, hr, gsn, grn, dsn, drn, cs, cr, rs, rr,
):
    nf = 2 * nz
    rows = q.shape[0]
    krows = w.shape[0]
    groups = KEY_VALUE_HEADS
    per = QUERY_HEADS // KEY_VALUE_HEADS
    span = per * HEAD_SIZE
    half = nz * pad
    f = lax.axis_index("fsdp")
    s = lax.axis_index("seq")
    z = f // 2
    c = f % 2
    partner = (f + 1 - 2 * c, s)

    def zpeer(d):
        return lax.rem(z + d, nz) * 2 + c

    def speer(d):
        return lax.rem(s + d, ns)

    def remote(src, dst, a, b, dev):
        return pltpu.make_async_remote_copy(
            src_ref=src, dst_ref=dst, send_sem=a, recv_sem=b,
            device_id=dev, device_id_type=pl.DeviceIdType.MESH,
        )

    def lanes_of(i, size):
        return pl.ds(pl.multiple_of(i * size, 128), size)

    cols = lanes_of(s, 128)
    loads = [
        pltpu.make_async_copy(tok_hbm, tok, ins.at[0]),
        pltpu.make_async_copy(q_hbm, q, ins.at[1]),
        pltpu.make_async_copy(og_hbm, og, ins.at[2]),
    ]
    for j in range(ns):
        own = w.at[:, j * 128 : (j + 1) * 128]
        loads.append(pltpu.make_async_copy(own, wall.at[j, f], ins.at[3 + j]))
    for cp in loads:
        cp.start()

    barrier = pltpu.get_barrier_semaphore()
    for d in range(1, nz):
        pl.semaphore_signal(barrier, inc=1, device_id=(zpeer(d), s), device_id_type=pl.DeviceIdType.MESH)
    for d in range(1, ns):
        pl.semaphore_signal(barrier, inc=1, device_id=(f, speer(d)), device_id_type=pl.DeviceIdType.MESH)
    pl.semaphore_signal(barrier, inc=1, device_id=partner, device_id_type=pl.DeviceIdType.MESH)
    pl.semaphore_wait(barrier, nz + ns - 1)

    sent = []

    def send(*args):
        cp = remote(*args)
        cp.start()
        sent.append(cp)

    def chain(k, right):
        at = z + k if right else z - k
        there = at < nz if right else at >= 0
        onward = z >= 1 if right else z + 1 < nz
        onto = ((z - 1 if right else z + 1) * 2 + c, s)
        return at * 2 + c, there, onward, onto

    def link(k, right):
        block, _, _, onto = chain(k, right)
        a, b = (rs_r, rr_r) if right else (rs_l, rr_l)
        piece = wall.at[s, block]
        source = w.at[:, cols] if k == 0 else piece
        return remote(source, piece, a.at[k], b.at[k], onto)

    def arrived(k, right):
        block, _, _, onto = chain(k, right)
        b = rr_r if right else rr_l
        piece = wall.at[s, block]
        return remote(piece, piece, rs_l.at[0], b.at[k - 1], onto)

    def over_seq(block, e):
        piece = wall.at[s, block]
        return remote(piece, piece, qsn.at[block // 2, e - 1], qrn.at[block // 2, e - 1], (f, speer(e)))

    def over_core(block):
        piece = wall.at[:, block]
        return remote(piece, piece, ps.at[block // 2], pr.at[block // 2], partner)

    ways = [(k, right) for k in range(1, nz) for right in (False, True)]

    for right in (False, True):

        @pl.when(chain(0, right)[2])
        def _(right=right):
            link(0, right).start()

    for cp in loads[3:]:
        cp.wait()
    over_core(f).start()

    loads[0].wait()
    for i in range(nf):
        tokf[i, :, :krows] = tok[i * krows : (i + 1) * krows, :].T

    for k, right in ways:
        block, there, onward, _ = chain(k, right)

        @pl.when(there)
        def _(k=k, right=right, block=block):
            arrived(k, right).wait_recv()
            for e in range(1, ns):
                over_seq(block, e).start()

        @pl.when(there & onward)
        def _(k=k, right=right):
            link(k, right).start()

    lane = lax.broadcasted_iota(jnp.int32, (rows, 128), 1)
    turn_lane = (lane % (HEAD_SIZE // 2)).astype(jnp.float32) / (HEAD_SIZE // 2)
    frequency = jnp.exp(turn_lane * (-math.log(rope_base)))
    position = lax.rem(
        s * rows + rolls[0] + lax.broadcasted_iota(jnp.int32, (rows, 128), 0), rows * ns
    )
    angle = position.astype(jnp.float32) * frequency
    cosine = jnp.cos(angle)
    sine = jnp.sin(angle)
    sine = jnp.where(lane % HEAD_SIZE < HEAD_SIZE // 2, -sine, sine)
    for p in range(QUERY_HEADS // 2):
        pair = [jnp.full((1, rows), sinks[2 * p + i], jnp.float32) for i in range(2)]
        esink[p] = jnp.exp(jnp.concatenate(pair, axis=1))

    tokpad[...] = jnp.zeros_like(tokpad)
    for t in range(ns):
        for j in range(2):
            for i in range(nz):
                start = (t * nf + 2 * i + j) * share
                to = (j * nz + i) * pad
                tokpad[t, to : to + share, :] = tok[start : start + share, :]
    tokblk[s] = tokpad[s]

    loads[1].wait()
    loads[2].wait()

    @pl.loop(0, groups)
    def _(g):
        here = lanes_of(g, span)
        x = turn(q[:, here].astype(jnp.float32), cosine, sine, False).astype(jnp.bfloat16)
        x = x * jnp.asarray(HEAD_SIZE ** (-0.5), jnp.bfloat16)
        o = og[:, here]
        for h in range(per):
            qs[g, h * rows : (h + 1) * rows, :] = x[:, h * HEAD_SIZE : (h + 1) * HEAD_SIZE]
            gs[g, h * rows : (h + 1) * rows, :] = o[:, h * HEAD_SIZE : (h + 1) * HEAD_SIZE]

    def whole(block):
        return jnp.concatenate([wall[j, block] for j in range(ns)], axis=1)

    def part(block):
        return nn(tokf[block][:, :krows], whole(block))

    total[...] = part(f)
    other = f + 1 - 2 * c
    over_core(other).wait_recv()
    total[...] += part(other)
    for k, right in ways:
        block, there, _, _ = chain(k, right)

        @pl.when(there)
        def _(block=block):
            for e in range(1, ns):
                piece = wall.at[lax.rem(s + ns - e, ns), block]
                remote(
                    piece, piece, qsn.at[block // 2, e - 1], qrn.at[block // 2, e - 1], (f, speer(e))
                ).wait_recv()
            over_core(block).start()
            total[...] += part(block)

    for k, right in ways:
        block, there, _, _ = chain(k, right)

        @pl.when(there)
        def _(block=block):
            over_core(block + 1 - 2 * c).wait_recv()
            total[...] += part(block + 1 - 2 * c)

    key_width = groups * HEAD_SIZE
    keys = turn(total[:, :key_width], cosine, sine, False).astype(jnp.bfloat16)
    values = total[:, key_width:].astype(jnp.bfloat16)
    for g in range(groups):
        lo, hi = g * HEAD_SIZE, (g + 1) * HEAD_SIZE
        kvbuf[g, WINDOW:, :] = jnp.concatenate([keys[:, lo:hi], values[:, lo:hi]], axis=1)
    halo = remote(
        kvbuf.at[:, pl.ds(WINDOW, WINDOW), :], kvbuf.at[:, pl.ds(0, WINDOW), :], hs, hr, (f, speer(1))
    )
    halo.start()
    halo.wait()
    for e in range(1, ns):
        send(tokpad.at[speer(e)], tokblk.at[s], ts.at[e - 1], tr.at[e - 1], (f, speer(e)))
    before = speer(ns - 1)
    mine_rows = pl.ds(pl.multiple_of(s * rows, 128), rows)

    def hg_copy(g):
        return remote(hg_out.at[g], hg_in.at[g], gsn.at[g], grn.at[g], (f, before))

    def attention(g):
        kv = kvbuf[g]
        key, value = kv[:, :HEAD_SIZE], kv[:, HEAD_SIZE:]
        kv_t = kv.T
        key_t, value_t = kv_t[:HEAD_SIZE], kv_t[HEAD_SIZE:]
        slot = lax.broadcasted_iota(jnp.int32, (rows, 2 * rows), 0)
        at = lax.broadcasted_iota(jnp.int32, (rows, 2 * rows), 1) & (rows - 1)
        is_own = slot <= at
        valid = slot <= at + s * rows

        def chosen(x):
            return jnp.where(is_own, x[WINDOW:], x[:WINDOW])

        def spread(x):
            borrowed = jnp.where(is_own, 0.0, x)
            return jnp.concatenate([borrowed, jnp.where(is_own, x, 0.0)], axis=0).astype(jnp.bfloat16)

        for p in range(per // 2):
            two = slice(p * 2 * rows, (p + 1) * 2 * rows)
            query, grad = qs[g, two, :], gs[g, two, :]
            expo = jnp.where(valid, jnp.exp(chosen(nt(key, query))), 0.0)
            denominator = esink[g * (per // 2) + p] + jnp.sum(expo, axis=0, keepdims=True)
            probs = expo * (1.0 / denominator)
            dprob = chosen(nt(value, grad))
            delta = jnp.sum(probs * dprob, axis=0, keepdims=True)
            probs_b = spread(probs)
            dscore = spread(probs * (dprob - delta))
            prob_t[:, two] = probs_b
            dscore_t[:, two] = dscore
            out = nn(value_t, probs_b)
            dq = nn(key_t, dscore) * (HEAD_SIZE ** (-0.5))
            out = jnp.concatenate([out[:, :rows], out[:, rows:]], axis=0).T
            dq = jnp.concatenate([dq[:, :rows], dq[:, rows:]], axis=0).T
            here = pl.ds(pl.multiple_of(g * span + p * 128, 128), 128)
            attn_v[:, here] = out.astype(jnp.bfloat16)
            qgrad_v[:, here] = turn(dq, cosine, sine, True).astype(jnp.bfloat16)
        dkv = jnp.concatenate([nn(dscore_t[...], qs[g]), nn(prob_t[...], gs[g])], axis=1)
        hg_out[g] = dkv[:WINDOW].astype(jnp.bfloat16)
        own_g[g] = dkv[WINDOW:]
        hg_copy(g).start()

    def dkv_copy(g, e):
        piece = dkv_all.at[g, mine_rows, :]
        return remote(piece, piece, dsn.at[g, e - 1], drn.at[g, e - 1], (f, speer(e)))

    def finish(g):
        hg_copy(g).wait_recv()
        both = own_g[g] + hg_in[g].astype(jnp.float32)
        lane = lax.broadcasted_iota(jnp.int32, both.shape, 1)
        dkv = jnp.where(lane < HEAD_SIZE, turn(both, cosine, sine, True), both)
        dkv_all[g, mine_rows, :] = dkv.astype(jnp.bfloat16)
        for e in range(1, ns):
            dkv_copy(g, e).start()

    def core_copy(g):
        return remote(core_out.at[g], core_in.at[g], cs.at[g], cr.at[g], partner)

    def features(core):
        there = pl.ds(pl.multiple_of(core * half, 128), half)
        return jnp.concatenate([tokblk[t, there, :] for t in range(ns)], axis=1)

    def weight_part(g):
        for e in range(1, ns):
            src = lax.rem(s + ns - e, ns)
            piece = dkv_all.at[g, pl.ds(pl.multiple_of(src * rows, 128), rows), :]
            remote(piece, piece, dsn.at[g, e - 1], drn.at[g, e - 1], (f, src)).wait_recv()
        dkv = dkv_all[g]
        core_out[g] = nn(features(1 - c), dkv).astype(jnp.bfloat16)
        core_copy(g).start()
        mine[g] = nn(features(c), dkv)

    def z_copy(g, d):
        return remote(z_out.at[g, d - 1], z_in.at[g, d - 1], rs.at[g, d - 1], rr.at[g, d - 1], (zpeer(d), s))

    def z_part(g):
        core_copy(g).wait_recv()
        zsum[g] = (mine[g] + core_in[g].astype(jnp.float32)).reshape(nz, pad, 128)
        for d in range(1, nz):
            z_out[g, d - 1] = zsum[g, lax.rem(z + d, nz)].astype(jnp.bfloat16)
            z_copy(g, d).start()

    def token_blocks():
        for e in range(1, ns):
            src = lax.rem(s + ns - e, ns)
            remote(tokpad.at[src], tokblk.at[src], ts.at[e - 1], tr.at[e - 1], (f, src)).wait_recv()

    @pl.loop(0, groups)
    def _(g):
        attention(g)

        @pl.when(g >= 1)
        def _():
            finish(g - 1)

        @pl.when(g == 2)
        def _():
            token_blocks()

        @pl.when(g >= 2)
        def _():
            weight_part(g - 2)

        @pl.when(g >= 3)
        def _():
            z_part(g - 3)

    finish(groups - 1)
    weight_part(groups - 2)
    z_part(groups - 3)
    pieces = [dkv_all[g, mine_rows, :] for g in range(groups)]
    dkv = jnp.concatenate([b[:, :HEAD_SIZE] for b in pieces] + [b[:, HEAD_SIZE:] for b in pieces], axis=1)
    for i in range(nf):
        tgrad_v[i * krows : (i + 1) * krows, :] = nt(whole(i), dkv).astype(jnp.bfloat16)
    weight_part(groups - 1)
    z_part(groups - 2)
    z_part(groups - 1)

    sums = []
    for g in range(groups):
        acc = zsum[g, z]
        for d in range(1, nz):
            z_copy(g, d).wait_recv()
            acc = acc + z_in[g, d - 1].astype(jnp.float32)
        sums.append(acc[:share])
    order = []
    for lo in (0, HEAD_SIZE):
        for g in range(0, groups, 2):
            order.append(jnp.concatenate([sums[g][:, lo : lo + HEAD_SIZE], sums[g + 1][:, lo : lo + HEAD_SIZE]], axis=1))
    for j in range(groups):
        wgrad[pl.ds(j, share, stride=groups), :] = order[j]

    for cp in sent:
        cp.wait_send()
    for g in range(groups):
        hg_copy(g).wait_send()
        core_copy(g).wait_send()
        for e in range(1, ns):
            dkv_copy(g, e).wait_send()
        for d in range(1, nz):
            z_copy(g, d).wait_send()
    for k in range(nz):
        for right in (False, True):
            _, there, onward, _ = chain(k, right)

            @pl.when(there & onward)
            def _(k=k, right=right):
                link(k, right).wait_send()

            if k > 0:

                @pl.when(there)
                def _(k=k, right=right):
                    block = chain(k, right)[0]
                    for e in range(1, ns):
                        over_seq(block, e).wait_send()
                    over_core(block).wait_send()

    over_core(f).wait_send()


def write_out(*refs):
    done = refs[8]
    copies = [pltpu.make_async_copy(refs[i], refs[4 + i], done.at[i]) for i in range(4)]
    for cp in copies:
        cp.start()
    for cp in copies:
        cp.wait()


KW_COLUMNS = 2 * KEY_VALUE_HEADS * HEAD_SIZE


def fused(tokens, queries, kv_weight, sink_logit_values, roll_offsets, out_grad):
    nf = lax.axis_size("fsdp")
    ns = lax.axis_size("seq")
    nz = nf // 2
    rows, width = tokens.shape[1:]
    krows = kv_weight.shape[0]
    share = width // (nf * ns)
    pad = -(-share // 16) * 16
    half = nz * pad
    query_width = QUERY_HEADS * HEAD_SIZE
    groups = KEY_VALUE_HEADS
    per = QUERY_HEADS // groups
    bf, f32 = jnp.bfloat16, jnp.float32
    sem = pltpu.SemaphoreType.DMA
    vm = pltpu.VMEM
    shape = jax.ShapeDtypeStruct
    anywhere = pl.BlockSpec(memory_space=pl.ANY)
    inside = pl.BlockSpec(memory_space=pltpu.VMEM)
    scalars = pl.BlockSpec(memory_space=pltpu.SMEM)
    results = pl.pallas_call(
        functools.partial(fused_kernel, nz, ns, share, pad),
        out_shape=(
            shape((rows, query_width), bf),
            shape((rows, query_width), bf),
            shape((width, rows), bf),
            shape((share * groups, 128), f32),
        ),
        in_specs=[anywhere, anywhere, anywhere, scalars, scalars, anywhere],
        out_specs=[inside] * 4,
        scratch_shapes=[
            vm((ns, nf, krows, 128), bf),
            vm((width, rows), bf),
            vm((rows, query_width), bf),
            vm((rows, query_width), bf),
            vm((nf, rows, -(-krows // 128) * 128), bf),
            vm((ns, nf * pad, rows), bf),
            vm((ns, nf * pad, rows), bf),
            vm((groups, per * rows, HEAD_SIZE), bf),
            vm((groups, per * rows, HEAD_SIZE), bf),
            vm((groups, rows + WINDOW, 2 * HEAD_SIZE), bf),
            vm((rows + WINDOW, per * rows), bf),
            vm((rows + WINDOW, per * rows), bf),
            vm((groups, rows, 2 * HEAD_SIZE), f32),
            vm((groups, WINDOW, 2 * HEAD_SIZE), bf),
            vm((groups, WINDOW, 2 * HEAD_SIZE), bf),
            vm((groups, ns * rows, 2 * HEAD_SIZE), bf),
            vm((groups, half, 128), bf),
            vm((groups, half, 128), bf),
            vm((groups, half, 128), f32),
            vm((groups, nz, pad, 128), f32),
            vm((groups, nz - 1, pad, 128), bf),
            vm((groups, nz - 1, pad, 128), bf),
            vm((rows, KW_COLUMNS), f32),
            vm((QUERY_HEADS // 2, 1, 2 * rows), f32),
            sem((3 + ns,)),
            sem((nz,)), sem((nz,)), sem((nz,)), sem((nz,)),
            sem((nz, ns - 1)), sem((nz, ns - 1)),
            sem((nz,)), sem((nz,)),
            sem((ns - 1,)), sem((ns - 1,)),
            sem, sem,
            sem((groups,)), sem((groups,)),
            sem((groups, ns - 1)), sem((groups, ns - 1)),
            sem((groups,)), sem((groups,)),
            sem((groups, nz - 1)), sem((groups, nz - 1)),
        ],
        compiler_params=pltpu.CompilerParams(
            collective_id=0, has_side_effects=True, vmem_limit_bytes=56 * 1024 * 1024
        ),
    )(tokens[0].T, queries[0], kv_weight, sink_logit_values, roll_offsets, out_grad[0])
    attn, qgrad, tgrad, wgrad = pl.pallas_call(
        write_out,
        out_shape=tuple(shape(x.shape, x.dtype) for x in results),
        in_specs=[inside] * 4,
        out_specs=[anywhere] * 4,
        scratch_shapes=[sem((4,))],
    )(*results)
    return (attn[None], qgrad[None], tgrad.T[None], wgrad[None])


def fits_fused(mesh):
    nf, ns = mesh.shape["fsdp"], mesh.shape["seq"]
    return nf == 8 and KW_COLUMNS == 128 * ns


def solution(mesh):
    placed = (
        P("fsdp", "seq", None),
        P("fsdp", "seq", None),
        P("fsdp", None),
        P(),
        P("fsdp"),
        P("fsdp", "seq", None),
    )
    return jax.shard_map(
        fused if fits_fused(mesh) else local,
        mesh=mesh,
        in_specs=placed,
        out_specs=(
            P("fsdp", "seq", None),
            P("fsdp", "seq", None),
            P("fsdp", "seq", None),
            P("seq", "fsdp", None),
        ),
        check_vma=False,
    )
```

```python
import functools
import math

import jax
import jax.numpy as jnp
from jax import lax
from jax.experimental import pallas as pl
from jax.experimental.pallas import tpu as pltpu
from jax.sharding import PartitionSpec as P

QUERY_HEADS = 32
KEY_VALUE_HEADS = 4
HEAD_SIZE = 64
WINDOW = 128


rope_base = 150000.0


def from_behind(array, axis, by):
    peers = lax.axis_size(axis)
    pairs = [(i, i + by) for i in range(peers) if 0 <= i + by < peers]
    return lax.ppermute(array, axis, pairs)


def rope_tables(positions):
    half_width = HEAD_SIZE // 2
    frequency = rope_base ** (-jnp.arange(half_width, dtype=jnp.float32) / half_width)
    angle = positions.astype(jnp.float32)[:, None] * frequency[None, :]
    return (jnp.cos(angle), jnp.sin(angle))


def apply_rotary(values, cosine_lookup, sine_lookup, head_count, direction):
    row_count = values.shape[0]
    halves = values.reshape(row_count, head_count, 2, HEAD_SIZE // 2)
    front_half = halves[:, :, 0]
    back_half = halves[:, :, 1]
    cosine_rows = cosine_lookup[:, None, :]
    sine_rows = sine_lookup[:, None, :] * direction
    turned = jnp.stack(
        [
            front_half * cosine_rows - back_half * sine_rows,
            front_half * sine_rows + back_half * cosine_rows,
        ],
        axis=2,
    )
    return turned.reshape(row_count, head_count * HEAD_SIZE)


def attend_group(query_g, key_g, value_g, grad_g, sink_g, allowed):
    score_scale = HEAD_SIZE ** (-0.5)
    scores = (
        jnp.einsum("bgd,kd->gbk", query_g, key_g, preferred_element_type=jnp.float32) * score_scale
    )
    exponent = jnp.where(allowed[None], jnp.exp(scores), 0.0)
    denominator = jnp.exp(sink_g)[:, None] + jnp.sum(exponent, axis=2)
    softmax_w = exponent / denominator[:, :, None]
    softmax_b = softmax_w.astype(jnp.bfloat16)
    attended = jnp.einsum("gbk,kd->bgd", softmax_b, value_g, preferred_element_type=jnp.float32)
    dprob = jnp.einsum("bgd,kd->gbk", grad_g, value_g, preferred_element_type=jnp.float32)
    row_delta = jnp.sum(softmax_w * dprob, axis=2)
    dscore = (softmax_w * (dprob - row_delta[:, :, None]) * score_scale).astype(jnp.bfloat16)
    query_diff = jnp.einsum("gbk,kd->bgd", dscore, key_g, preferred_element_type=jnp.float32)
    key_diff = jnp.einsum("gbk,bgd->kd", dscore, query_g, preferred_element_type=jnp.float32)
    value_diff = jnp.einsum("gbk,bgd->kd", softmax_b, grad_g, preferred_element_type=jnp.float32)
    return (attended.astype(jnp.bfloat16), query_diff, key_diff, value_diff)


def attend_block(query_block, key_block, gradient_block, sink_logit_values, key_first):
    block_row_span = query_block.shape[0]
    key_row_slice = key_block.shape[0]
    group_width = QUERY_HEADS // KEY_VALUE_HEADS
    key_span_width = KEY_VALUE_HEADS * HEAD_SIZE
    rows_idx = jnp.arange(block_row_span, dtype=jnp.int32)[:, None]
    cols_idx = jnp.arange(key_row_slice, dtype=jnp.int32)[None, :]
    allowed = (cols_idx > rows_idx) & (cols_idx <= rows_idx + WINDOW) & (cols_idx + key_first >= 0)
    query_head_rows = query_block.reshape(
        block_row_span, KEY_VALUE_HEADS, group_width, HEAD_SIZE
    ).transpose(1, 0, 2, 3)
    gradient_heads = gradient_block.reshape(
        block_row_span, KEY_VALUE_HEADS, group_width, HEAD_SIZE
    ).transpose(1, 0, 2, 3)
    key_head_rows = (
        key_block[:, :key_span_width]
        .reshape(key_row_slice, KEY_VALUE_HEADS, HEAD_SIZE)
        .transpose(1, 0, 2)
    )
    value_head_rows = (
        key_block[:, key_span_width:]
        .reshape(key_row_slice, KEY_VALUE_HEADS, HEAD_SIZE)
        .transpose(1, 0, 2)
    )
    sink_per_head = sink_logit_values.reshape(KEY_VALUE_HEADS, group_width)

    def per_group(packed):
        return attend_group(packed[0], packed[1], packed[2], packed[3], packed[4], allowed)

    attended, query_diff, key_diff, value_diff = lax.map(
        per_group, (query_head_rows, key_head_rows, value_head_rows, gradient_heads, sink_per_head)
    )
    attended = attended.transpose(1, 0, 2, 3).reshape(block_row_span, QUERY_HEADS * HEAD_SIZE)
    query_diff = query_diff.transpose(1, 0, 2, 3).reshape(block_row_span, QUERY_HEADS * HEAD_SIZE)
    kv_diff = jnp.concatenate(
        [
            key_diff.transpose(1, 0, 2).reshape(key_row_slice, key_span_width),
            value_diff.transpose(1, 0, 2).reshape(key_row_slice, key_span_width),
        ],
        axis=1,
    )
    return (attended, query_diff, kv_diff)


def band_pass(query_rot, keys_all, grad_out, sink_logit_values, row_start):
    row_total = query_rot.shape[0]
    block_row_span = min(row_total, 512)

    def block_step(grad_all, block_index):
        block_begin = block_index * block_row_span
        attended, query_diff, kv_diff = attend_block(
            query_rot, keys_all, grad_out, sink_logit_values, row_start + block_begin - WINDOW
        )
        previous = grad_all
        grad_all = previous + kv_diff
        return (grad_all, (attended, query_diff))

    start_grad = jnp.zeros((row_total + WINDOW, keys_all.shape[1]), jnp.float32)
    grad_all, (attended, query_diff) = lax.scan(
        block_step, start_grad, jnp.arange(row_total // block_row_span, dtype=jnp.int32)
    )
    return (
        attended.reshape(row_total, QUERY_HEADS * HEAD_SIZE),
        query_diff.reshape(row_total, QUERY_HEADS * HEAD_SIZE),
        grad_all,
    )


def local(tokens, queries, kv_weight, sink_logit_values, roll_offsets, out_grad):
    token_rows = tokens[0]
    query_rows = queries[0]
    grad_rows = out_grad[0]
    row_total = token_rows.shape[0]
    key_span_width = KEY_VALUE_HEADS * HEAD_SIZE
    seq_index = lax.axis_index("seq")
    seq_count = lax.axis_size("seq")
    stream_length = row_total * seq_count
    row_start = seq_index * row_total
    whole_weight = lax.all_gather(kv_weight, "fsdp", axis=0, tiled=True)
    projected_rows = jnp.dot(token_rows, whole_weight, preferred_element_type=jnp.float32)
    positions = (
        row_start + jnp.arange(row_total, dtype=jnp.int32) + roll_offsets[0]
    ) % stream_length
    cosine_lookup, sine_lookup = rope_tables(positions)
    key_value_rotated = jnp.concatenate(
        [
            apply_rotary(
                projected_rows[:, :key_span_width], cosine_lookup, sine_lookup, KEY_VALUE_HEADS, 1.0
            ),
            projected_rows[:, key_span_width:],
        ],
        axis=1,
    ).astype(jnp.bfloat16)
    query_rot = apply_rotary(
        query_rows.astype(jnp.float32), cosine_lookup, sine_lookup, QUERY_HEADS, 1.0
    ).astype(jnp.bfloat16)
    edge_rows = from_behind(key_value_rotated, "seq", 1)
    keys_all = jnp.concatenate([edge_rows, key_value_rotated], axis=0)
    attended, query_diff, grad_all = band_pass(
        query_rot, keys_all, grad_rows, sink_logit_values, row_start
    )
    incoming = from_behind(grad_all[:WINDOW].astype(jnp.bfloat16), "seq", -1).astype(jnp.float32)
    local_gradient = grad_all[WINDOW:]
    local_gradient = jnp.concatenate(
        [local_gradient[: row_total - WINDOW], local_gradient + incoming], axis=0
    )
    query_back = apply_rotary(query_diff, cosine_lookup, sine_lookup, QUERY_HEADS, -1.0).astype(
        jnp.bfloat16
    )
    key_value_backward = jnp.concatenate(
        [
            apply_rotary(
                local_gradient[:, :key_span_width],
                cosine_lookup,
                sine_lookup,
                KEY_VALUE_HEADS,
                -1.0,
            ),
            local_gradient[:, key_span_width:],
        ],
        axis=1,
    ).astype(jnp.bfloat16)
    token_back = lax.dot_general(
        key_value_backward,
        whole_weight,
        (((1,), (1,)), ((), ())),
        preferred_element_type=jnp.float32,
    ).astype(jnp.bfloat16)
    feature_block = lax.all_to_all(token_rows, "seq", split_axis=1, concat_axis=0, tiled=True)
    block_term = lax.dot_general(
        feature_block,
        lax.all_gather(key_value_backward, "seq", axis=0, tiled=True),
        (((0,), (0,)), ((), ())),
        preferred_element_type=jnp.float32,
    )
    flat_block = block_term.reshape(-1, 128)
    weight_share = lax.psum_scatter(flat_block, "fsdp", scatter_dimension=0, tiled=True)
    return (attended[None], query_back[None], token_back[None], weight_share[None])


def nt(a, b):
    return lax.dot_general(a, b, (((1,), (1,)), ((), ())), preferred_element_type=jnp.float32)


def tn(a, b):
    return lax.dot_general(a, b, (((0,), (0,)), ((), ())), preferred_element_type=jnp.float32)


def nn(a, b):
    return lax.dot_general(a, b, (((1,), (0,)), ((), ())), preferred_element_type=jnp.float32)


def turn(x, cosine, sine, back):
    width = x.shape[1]
    lane = lax.broadcasted_iota(jnp.int32, x.shape, 1)
    swapped = jnp.where(
        lane % HEAD_SIZE < HEAD_SIZE // 2,
        pltpu.roll(x, width - HEAD_SIZE // 2, 1),
        pltpu.roll(x, HEAD_SIZE // 2, 1),
    )
    times = width // cosine.shape[1]
    cosine = jnp.concatenate([cosine] * times, axis=1)
    sine = jnp.concatenate([sine] * times, axis=1)
    if back:
        return x * cosine - swapped * sine
    return x * cosine + swapped * sine


def fused_kernel(
    nz, ns, share, pad,
    tok_hbm, q_hbm, w, sinks, rolls, og_hbm,
    attn_v, qgrad_v, tgrad_v, wgrad,
    wall, tok, q, og, tokf, tokpad, tokblk, qs, gs, kvbuf, prob_t, dscore_t,
    own_g, hg_out, hg_in, dkv_all, core_out, core_in, mine, zsum, z_out, z_in, total, esink,
    ins, rs_l, rr_l, rs_r, rr_r, qsn, qrn, ps, pr, ts, tr, hs, hr, gsn, grn, dsn, drn, cs, cr, rs, rr,
):
    nf = 2 * nz
    rows = q.shape[0]
    krows = w.shape[0]
    groups = KEY_VALUE_HEADS
    per = QUERY_HEADS // KEY_VALUE_HEADS
    span = per * HEAD_SIZE
    half = nz * pad
    f = lax.axis_index("fsdp")
    s = lax.axis_index("seq")
    z = f // 2
    c = f % 2
    partner = (f + 1 - 2 * c, s)

    def zpeer(d):
        return lax.rem(z + d, nz) * 2 + c

    def speer(d):
        return lax.rem(s + d, ns)

    def remote(src, dst, a, b, dev):
        return pltpu.make_async_remote_copy(
            src_ref=src, dst_ref=dst, send_sem=a, recv_sem=b,
            device_id=dev, device_id_type=pl.DeviceIdType.MESH,
        )

    def lanes_of(i, size):
        return pl.ds(pl.multiple_of(i * size, 128), size)

    cols = lanes_of(s, 128)
    loads = [
        pltpu.make_async_copy(tok_hbm, tok, ins.at[0]),
        pltpu.make_async_copy(q_hbm, q, ins.at[1]),
        pltpu.make_async_copy(og_hbm, og, ins.at[2]),
    ]
    for j in range(ns):
        own = w.at[:, j * 128 : (j + 1) * 128]
        loads.append(pltpu.make_async_copy(own, wall.at[j, f], ins.at[3 + j]))
    for cp in loads:
        cp.start()

    barrier = pltpu.get_barrier_semaphore()
    for d in range(1, nz):
        pl.semaphore_signal(barrier, inc=1, device_id=(zpeer(d), s), device_id_type=pl.DeviceIdType.MESH)
    for d in range(1, ns):
        pl.semaphore_signal(barrier, inc=1, device_id=(f, speer(d)), device_id_type=pl.DeviceIdType.MESH)
    pl.semaphore_signal(barrier, inc=1, device_id=partner, device_id_type=pl.DeviceIdType.MESH)
    lane = lax.broadcasted_iota(jnp.int32, (rows, 128), 1)
    turn_lane = (lane % (HEAD_SIZE // 2)).astype(jnp.float32) / (HEAD_SIZE // 2)
    frequency = jnp.exp(turn_lane * (-math.log(rope_base)))
    position = lax.rem(
        s * rows + rolls[0] + lax.broadcasted_iota(jnp.int32, (rows, 128), 0), rows * ns
    )
    angle = position.astype(jnp.float32) * frequency
    cosine = jnp.cos(angle)
    sine = jnp.sin(angle)
    sine = jnp.where(lane % HEAD_SIZE < HEAD_SIZE // 2, -sine, sine)
    for p in range(QUERY_HEADS // 2):
        pair = [jnp.full((1, rows), sinks[2 * p + i], jnp.float32) for i in range(2)]
        esink[p] = jnp.exp(jnp.concatenate(pair, axis=1))

    pl.semaphore_wait(barrier, nz + ns - 1)

    sent = []

    def send(*args):
        cp = remote(*args)
        cp.start()
        sent.append(cp)

    def chain(k, right):
        at = z + k if right else z - k
        there = at < nz if right else at >= 0
        onward = z >= 1 if right else z + 1 < nz
        onto = ((z - 1 if right else z + 1) * 2 + c, s)
        return at * 2 + c, there, onward, onto

    def link(k, right):
        block, _, _, onto = chain(k, right)
        a, b = (rs_r, rr_r) if right else (rs_l, rr_l)
        piece = wall.at[s, block]
        source = w.at[:, cols] if k == 0 else piece
        return remote(source, piece, a.at[k], b.at[k], onto)

    def arrived(k, right):
        block, _, _, onto = chain(k, right)
        b = rr_r if right else rr_l
        piece = wall.at[s, block]
        return remote(piece, piece, rs_l.at[0], b.at[k - 1], onto)

    across = s + 1 - 2 * (s % 2)
    along = s + 2 - 4 * (s // 2)
    corner = ns - 1 - s

    def over_seq(owner, block, e, peer):
        piece = wall.at[owner, block]
        return remote(piece, piece, qsn.at[block // 2, e], qrn.at[block // 2, e], (f, peer))

    def relay(block):
        way = (block // 2 + c) % 2
        owner = across + way * (along - across)
        peer = along + way * (across - along)
        return over_seq(owner, block, 2, peer)

    def over_core(block):
        piece = wall.at[:, block]
        return remote(piece, piece, ps.at[block // 2], pr.at[block // 2], partner)

    ways = [(k, right) for k in range(1, nz) for right in (False, True)]

    for right in (False, True):

        @pl.when(chain(0, right)[2])
        def _(right=right):
            link(0, right).start()

    for cp in loads[3:]:
        cp.wait()
    over_core(f).start()

    loads[0].wait()
    for i in range(nf):
        tokf[i, :, :krows] = tok[i * krows : (i + 1) * krows, :].T

    for k, right in ways:
        block, there, onward, _ = chain(k, right)

        @pl.when(there)
        def _(k=k, right=right, block=block):
            arrived(k, right).wait_recv()
            over_seq(s, block, 0, across).start()
            over_seq(s, block, 1, along).start()

        @pl.when(there & onward)
        def _(k=k, right=right):
            link(k, right).start()

    tokpad[...] = jnp.zeros_like(tokpad)
    for t in range(ns):
        for j in range(2):
            for i in range(nz):
                start = (t * nf + 2 * i + j) * share
                to = (j * nz + i) * pad
                tokpad[t, to : to + share, :] = tok[start : start + share, :]
    tokblk[s] = tokpad[s]

    loads[1].wait()
    loads[2].wait()

    def stack_heads(g):
        if g >= groups:
            return
        here = lanes_of(g, span)
        x = turn(q[:, here].astype(jnp.float32), cosine, sine, False).astype(jnp.bfloat16)
        x = x * jnp.asarray(HEAD_SIZE ** (-0.5), jnp.bfloat16)
        o = og[:, here]
        for h in range(per):
            qs[g, h * rows : (h + 1) * rows, :] = x[:, h * HEAD_SIZE : (h + 1) * HEAD_SIZE]
            gs[g, h * rows : (h + 1) * rows, :] = o[:, h * HEAD_SIZE : (h + 1) * HEAD_SIZE]

    def whole(block):
        return jnp.concatenate([wall[j, block] for j in range(ns)], axis=1)

    def part(block):
        return nn(tokf[block][:, :krows], whole(block))

    def pass_on(k, right):
        block, there, _, _ = chain(k, right)

        @pl.when(there)
        def _():
            over_seq(across, block, 0, across).wait_recv()
            over_seq(along, block, 1, along).wait_recv()
            relay(block).start()

    def take(k, right):
        block, there, _, _ = chain(k, right)

        @pl.when(there)
        def _():
            over_seq(corner, block, 2, along).wait_recv()
            over_core(block).start()
            total[...] += part(block)

    other = f + 1 - 2 * c
    total[...] = part(f)
    for i, way in enumerate(ways):
        stack_heads(i)
        pass_on(*way)
        if i == 1:
            over_core(other).wait_recv()
            total[...] += part(other)
        if i > 0:
            take(*ways[i - 1])
    take(*ways[-1])
    for k, right in ways:
        block, there, _, _ = chain(k, right)

        @pl.when(there)
        def _(block=block):
            over_core(block + 1 - 2 * c).wait_recv()
            total[...] += part(block + 1 - 2 * c)

    def halo_copy(g):
        edge = kvbuf.at[g, pl.ds(WINDOW, WINDOW), :]
        return remote(edge, kvbuf.at[g, pl.ds(0, WINDOW), :], hs.at[g], hr.at[g], (f, speer(1)))

    key_width = groups * HEAD_SIZE
    keys = turn(total[:, :key_width], cosine, sine, False).astype(jnp.bfloat16)
    values = total[:, key_width:].astype(jnp.bfloat16)
    for g in range(groups):
        lo, hi = g * HEAD_SIZE, (g + 1) * HEAD_SIZE
        kvbuf[g, WINDOW:, :] = jnp.concatenate([keys[:, lo:hi], values[:, lo:hi]], axis=1)
        halo_copy(g).start()
    halo_copy(0).wait_recv()
    for e in range(1, ns):
        send(tokpad.at[speer(e)], tokblk.at[s], ts.at[e - 1], tr.at[e - 1], (f, speer(e)))
    before = speer(ns - 1)
    mine_rows = pl.ds(pl.multiple_of(s * rows, 128), rows)

    def hg_copy(g):
        return remote(hg_out.at[g], hg_in.at[g], gsn.at[g], grn.at[g], (f, before))

    def attention(g):
        @pl.when(g > 0)
        def _():
            halo_copy(g).wait_recv()

        kv = kvbuf[g]
        key, value = kv[:, :HEAD_SIZE], kv[:, HEAD_SIZE:]
        kv_t = kv.T
        key_t, value_t = kv_t[:HEAD_SIZE], kv_t[HEAD_SIZE:]
        slot = lax.broadcasted_iota(jnp.int32, (rows, 2 * rows), 0)
        at = lax.broadcasted_iota(jnp.int32, (rows, 2 * rows), 1) & (rows - 1)
        is_own = slot <= at
        valid = slot <= at + s * rows

        def chosen(x):
            return jnp.where(is_own, x[WINDOW:], x[:WINDOW])

        def spread(x):
            borrowed = jnp.where(is_own, 0.0, x)
            return jnp.concatenate([borrowed, jnp.where(is_own, x, 0.0)], axis=0).astype(jnp.bfloat16)

        for p in range(per // 2):
            two = slice(p * 2 * rows, (p + 1) * 2 * rows)
            query, grad = qs[g, two, :], gs[g, two, :]
            expo = jnp.where(valid, jnp.exp(chosen(nt(key, query))), 0.0)
            denominator = esink[g * (per // 2) + p] + jnp.sum(expo, axis=0, keepdims=True)
            probs = expo * (1.0 / denominator)
            dprob = chosen(nt(value, grad))
            delta = jnp.sum(probs * dprob, axis=0, keepdims=True)
            probs_b = spread(probs)
            dscore = spread(probs * (dprob - delta))
            prob_t[:, two] = probs_b
            dscore_t[:, two] = dscore
            out = nn(value_t, probs_b)
            dq = nn(key_t, dscore) * (HEAD_SIZE ** (-0.5))
            out = jnp.concatenate([out[:, :rows], out[:, rows:]], axis=0).T
            dq = jnp.concatenate([dq[:, :rows], dq[:, rows:]], axis=0).T
            here = pl.ds(pl.multiple_of(g * span + p * 128, 128), 128)
            attn_v[:, here] = out.astype(jnp.bfloat16)
            qgrad_v[:, here] = turn(dq, cosine, sine, True).astype(jnp.bfloat16)
        dkv = jnp.concatenate([nn(dscore_t[...], qs[g]), nn(prob_t[...], gs[g])], axis=1)
        hg_out[g] = dkv[:WINDOW].astype(jnp.bfloat16)
        own_g[g] = dkv[WINDOW:]
        hg_copy(g).start()

    def dkv_copy(g, e):
        piece = dkv_all.at[g, mine_rows, :]
        return remote(piece, piece, dsn.at[g, e - 1], drn.at[g, e - 1], (f, speer(e)))

    def finish(g):
        hg_copy(g).wait_recv()
        both = own_g[g] + hg_in[g].astype(jnp.float32)
        lane = lax.broadcasted_iota(jnp.int32, both.shape, 1)
        dkv = jnp.where(lane < HEAD_SIZE, turn(both, cosine, sine, True), both)
        dkv_all[g, mine_rows, :] = dkv.astype(jnp.bfloat16)
        for e in range(1, ns):
            dkv_copy(g, e).start()

    def core_copy(g):
        return remote(core_out.at[g], core_in.at[g], cs.at[g], cr.at[g], partner)

    def features(core):
        there = pl.ds(pl.multiple_of(core * half, 128), half)
        return jnp.concatenate([tokblk[t, there, :] for t in range(ns)], axis=1)

    def weight_part(g):
        for e in range(1, ns):
            src = lax.rem(s + ns - e, ns)
            piece = dkv_all.at[g, pl.ds(pl.multiple_of(src * rows, 128), rows), :]
            remote(piece, piece, dsn.at[g, e - 1], drn.at[g, e - 1], (f, src)).wait_recv()
        dkv = dkv_all[g]
        core_out[g] = nn(features(1 - c), dkv).astype(jnp.bfloat16)
        core_copy(g).start()
        mine[g] = nn(features(c), dkv)

    def z_copy(g, d):
        return remote(z_out.at[g, d - 1], z_in.at[g, d - 1], rs.at[g, d - 1], rr.at[g, d - 1], (zpeer(d), s))

    def z_part(g):
        core_copy(g).wait_recv()
        zsum[g] = (mine[g] + core_in[g].astype(jnp.float32)).reshape(nz, pad, 128)
        for d in range(1, nz):
            z_out[g, d - 1] = zsum[g, lax.rem(z + d, nz)].astype(jnp.bfloat16)
            z_copy(g, d).start()

    def token_blocks():
        for e in range(1, ns):
            src = lax.rem(s + ns - e, ns)
            remote(tokpad.at[src], tokblk.at[src], ts.at[e - 1], tr.at[e - 1], (f, src)).wait_recv()

    @pl.loop(0, groups)
    def _(g):
        attention(g)

        @pl.when(g >= 1)
        def _():
            finish(g - 1)

        @pl.when(g == 2)
        def _():
            token_blocks()

        @pl.when(g >= 2)
        def _():
            weight_part(g - 2)

        @pl.when(g >= 3)
        def _():
            z_part(g - 3)

    finish(groups - 1)
    weight_part(groups - 2)
    z_part(groups - 3)
    pieces = [dkv_all[g, mine_rows, :] for g in range(groups)]
    dkv = jnp.concatenate([b[:, :HEAD_SIZE] for b in pieces] + [b[:, HEAD_SIZE:] for b in pieces], axis=1)
    for i in range(nf):
        tgrad_v[i * krows : (i + 1) * krows, :] = nt(whole(i), dkv).astype(jnp.bfloat16)
    weight_part(groups - 1)
    z_part(groups - 2)
    z_part(groups - 1)

    sums = []
    for g in range(groups):
        acc = zsum[g, z]
        for d in range(1, nz):
            z_copy(g, d).wait_recv()
            acc = acc + z_in[g, d - 1].astype(jnp.float32)
        sums.append(acc[:share])
    order = []
    for lo in (0, HEAD_SIZE):
        for g in range(0, groups, 2):
            order.append(jnp.concatenate([sums[g][:, lo : lo + HEAD_SIZE], sums[g + 1][:, lo : lo + HEAD_SIZE]], axis=1))
    for j in range(groups):
        wgrad[pl.ds(j, share, stride=groups), :] = order[j]

    for cp in sent:
        cp.wait_send()
    for g in range(groups):
        hg_copy(g).wait_send()
        halo_copy(g).wait_send()
        core_copy(g).wait_send()
        for e in range(1, ns):
            dkv_copy(g, e).wait_send()
        for d in range(1, nz):
            z_copy(g, d).wait_send()
    for k in range(nz):
        for right in (False, True):
            _, there, onward, _ = chain(k, right)

            @pl.when(there & onward)
            def _(k=k, right=right):
                link(k, right).wait_send()

            if k > 0:

                @pl.when(there)
                def _(k=k, right=right):
                    block = chain(k, right)[0]
                    over_seq(s, block, 0, across).wait_send()
                    over_seq(s, block, 1, along).wait_send()
                    relay(block).wait_send()
                    over_core(block).wait_send()

    over_core(f).wait_send()


def write_out(*refs):
    done = refs[8]
    copies = [pltpu.make_async_copy(refs[i], refs[4 + i], done.at[i]) for i in range(4)]
    for cp in copies:
        cp.start()
    for cp in copies:
        cp.wait()


KW_COLUMNS = 2 * KEY_VALUE_HEADS * HEAD_SIZE


def fused(tokens, queries, kv_weight, sink_logit_values, roll_offsets, out_grad):
    nf = lax.axis_size("fsdp")
    ns = lax.axis_size("seq")
    nz = nf // 2
    rows, width = tokens.shape[1:]
    krows = kv_weight.shape[0]
    share = width // (nf * ns)
    pad = -(-share // 16) * 16
    half = nz * pad
    query_width = QUERY_HEADS * HEAD_SIZE
    groups = KEY_VALUE_HEADS
    per = QUERY_HEADS // groups
    bf, f32 = jnp.bfloat16, jnp.float32
    sem = pltpu.SemaphoreType.DMA
    vm = pltpu.VMEM
    shape = jax.ShapeDtypeStruct
    anywhere = pl.BlockSpec(memory_space=pl.ANY)
    inside = pl.BlockSpec(memory_space=pltpu.VMEM)
    scalars = pl.BlockSpec(memory_space=pltpu.SMEM)
    results = pl.pallas_call(
        functools.partial(fused_kernel, nz, ns, share, pad),
        out_shape=(
            shape((rows, query_width), bf),
            shape((rows, query_width), bf),
            shape((width, rows), bf),
            shape((share * groups, 128), f32),
        ),
        in_specs=[anywhere, anywhere, anywhere, scalars, scalars, anywhere],
        out_specs=[inside] * 4,
        scratch_shapes=[
            vm((ns, nf, krows, 128), bf),
            vm((width, rows), bf),
            vm((rows, query_width), bf),
            vm((rows, query_width), bf),
            vm((nf, rows, -(-krows // 128) * 128), bf),
            vm((ns, nf * pad, rows), bf),
            vm((ns, nf * pad, rows), bf),
            vm((groups, per * rows, HEAD_SIZE), bf),
            vm((groups, per * rows, HEAD_SIZE), bf),
            vm((groups, rows + WINDOW, 2 * HEAD_SIZE), bf),
            vm((rows + WINDOW, per * rows), bf),
            vm((rows + WINDOW, per * rows), bf),
            vm((groups, rows, 2 * HEAD_SIZE), f32),
            vm((groups, WINDOW, 2 * HEAD_SIZE), bf),
            vm((groups, WINDOW, 2 * HEAD_SIZE), bf),
            vm((groups, ns * rows, 2 * HEAD_SIZE), bf),
            vm((groups, half, 128), bf),
            vm((groups, half, 128), bf),
            vm((groups, half, 128), f32),
            vm((groups, nz, pad, 128), f32),
            vm((groups, nz - 1, pad, 128), bf),
            vm((groups, nz - 1, pad, 128), bf),
            vm((rows, KW_COLUMNS), f32),
            vm((QUERY_HEADS // 2, 1, 2 * rows), f32),
            sem((3 + ns,)),
            sem((nz,)), sem((nz,)), sem((nz,)), sem((nz,)),
            sem((nz, ns - 1)), sem((nz, ns - 1)),
            sem((nz,)), sem((nz,)),
            sem((ns - 1,)), sem((ns - 1,)),
            sem((groups,)), sem((groups,)),
            sem((groups,)), sem((groups,)),
            sem((groups, ns - 1)), sem((groups, ns - 1)),
            sem((groups,)), sem((groups,)),
            sem((groups, nz - 1)), sem((groups, nz - 1)),
        ],
        compiler_params=pltpu.CompilerParams(
            collective_id=0, has_side_effects=True, vmem_limit_bytes=56 * 1024 * 1024
        ),
    )(tokens[0].T, queries[0], kv_weight, sink_logit_values, roll_offsets, out_grad[0])
    attn, qgrad, tgrad, wgrad = pl.pallas_call(
        write_out,
        out_shape=tuple(shape(x.shape, x.dtype) for x in results),
        in_specs=[inside] * 4,
        out_specs=[anywhere] * 4,
        scratch_shapes=[sem((4,))],
    )(*results)
    return (attn[None], qgrad[None], tgrad.T[None], wgrad[None])


def fits_fused(mesh):
    nf, ns = mesh.shape["fsdp"], mesh.shape["seq"]
    return nf == 8 and KW_COLUMNS == 128 * ns


def solution(mesh):
    placed = (
        P("fsdp", "seq", None),
        P("fsdp", "seq", None),
        P("fsdp", None),
        P(),
        P("fsdp"),
        P("fsdp", "seq", None),
    )
    return jax.shard_map(
        fused if fits_fused(mesh) else local,
        mesh=mesh,
        in_specs=placed,
        out_specs=(
            P("fsdp", "seq", None),
            P("fsdp", "seq", None),
            P("fsdp", "seq", None),
            P("seq", "fsdp", None),
        ),
        check_vma=False,
    )
```

```python
import functools
import math

import jax
import jax.numpy as jnp
from jax import lax
from jax.experimental import pallas as pl
from jax.experimental.pallas import tpu as pltpu
from jax.sharding import PartitionSpec as P

QUERY_HEADS = 32
KEY_VALUE_HEADS = 4
HEAD_SIZE = 64
WINDOW = 128


rope_base = 150000.0


def from_behind(array, axis, by):
    peers = lax.axis_size(axis)
    pairs = [(i, i + by) for i in range(peers) if 0 <= i + by < peers]
    return lax.ppermute(array, axis, pairs)


def rope_tables(positions):
    half_width = HEAD_SIZE // 2
    frequency = rope_base ** (-jnp.arange(half_width, dtype=jnp.float32) / half_width)
    angle = positions.astype(jnp.float32)[:, None] * frequency[None, :]
    return (jnp.cos(angle), jnp.sin(angle))


def apply_rotary(values, cosine_lookup, sine_lookup, head_count, direction):
    row_count = values.shape[0]
    halves = values.reshape(row_count, head_count, 2, HEAD_SIZE // 2)
    front_half = halves[:, :, 0]
    back_half = halves[:, :, 1]
    cosine_rows = cosine_lookup[:, None, :]
    sine_rows = sine_lookup[:, None, :] * direction
    turned = jnp.stack(
        [
            front_half * cosine_rows - back_half * sine_rows,
            front_half * sine_rows + back_half * cosine_rows,
        ],
        axis=2,
    )
    return turned.reshape(row_count, head_count * HEAD_SIZE)


def attend_group(query_g, key_g, value_g, grad_g, sink_g, allowed):
    score_scale = HEAD_SIZE ** (-0.5)
    scores = (
        jnp.einsum("bgd,kd->gbk", query_g, key_g, preferred_element_type=jnp.float32) * score_scale
    )
    exponent = jnp.where(allowed[None], jnp.exp(scores), 0.0)
    denominator = jnp.exp(sink_g)[:, None] + jnp.sum(exponent, axis=2)
    softmax_w = exponent / denominator[:, :, None]
    softmax_b = softmax_w.astype(jnp.bfloat16)
    attended = jnp.einsum("gbk,kd->bgd", softmax_b, value_g, preferred_element_type=jnp.float32)
    dprob = jnp.einsum("bgd,kd->gbk", grad_g, value_g, preferred_element_type=jnp.float32)
    row_delta = jnp.sum(softmax_w * dprob, axis=2)
    dscore = (softmax_w * (dprob - row_delta[:, :, None]) * score_scale).astype(jnp.bfloat16)
    query_diff = jnp.einsum("gbk,kd->bgd", dscore, key_g, preferred_element_type=jnp.float32)
    key_diff = jnp.einsum("gbk,bgd->kd", dscore, query_g, preferred_element_type=jnp.float32)
    value_diff = jnp.einsum("gbk,bgd->kd", softmax_b, grad_g, preferred_element_type=jnp.float32)
    return (attended.astype(jnp.bfloat16), query_diff, key_diff, value_diff)


def attend_block(query_block, key_block, gradient_block, sink_logit_values, key_first):
    block_row_span = query_block.shape[0]
    key_row_slice = key_block.shape[0]
    group_width = QUERY_HEADS // KEY_VALUE_HEADS
    key_span_width = KEY_VALUE_HEADS * HEAD_SIZE
    rows_idx = jnp.arange(block_row_span, dtype=jnp.int32)[:, None]
    cols_idx = jnp.arange(key_row_slice, dtype=jnp.int32)[None, :]
    allowed = (cols_idx > rows_idx) & (cols_idx <= rows_idx + WINDOW) & (cols_idx + key_first >= 0)
    query_head_rows = query_block.reshape(
        block_row_span, KEY_VALUE_HEADS, group_width, HEAD_SIZE
    ).transpose(1, 0, 2, 3)
    gradient_heads = gradient_block.reshape(
        block_row_span, KEY_VALUE_HEADS, group_width, HEAD_SIZE
    ).transpose(1, 0, 2, 3)
    key_head_rows = (
        key_block[:, :key_span_width]
        .reshape(key_row_slice, KEY_VALUE_HEADS, HEAD_SIZE)
        .transpose(1, 0, 2)
    )
    value_head_rows = (
        key_block[:, key_span_width:]
        .reshape(key_row_slice, KEY_VALUE_HEADS, HEAD_SIZE)
        .transpose(1, 0, 2)
    )
    sink_per_head = sink_logit_values.reshape(KEY_VALUE_HEADS, group_width)

    def per_group(packed):
        return attend_group(packed[0], packed[1], packed[2], packed[3], packed[4], allowed)

    attended, query_diff, key_diff, value_diff = lax.map(
        per_group, (query_head_rows, key_head_rows, value_head_rows, gradient_heads, sink_per_head)
    )
    attended = attended.transpose(1, 0, 2, 3).reshape(block_row_span, QUERY_HEADS * HEAD_SIZE)
    query_diff = query_diff.transpose(1, 0, 2, 3).reshape(block_row_span, QUERY_HEADS * HEAD_SIZE)
    kv_diff = jnp.concatenate(
        [
            key_diff.transpose(1, 0, 2).reshape(key_row_slice, key_span_width),
            value_diff.transpose(1, 0, 2).reshape(key_row_slice, key_span_width),
        ],
        axis=1,
    )
    return (attended, query_diff, kv_diff)


def band_pass(query_rot, keys_all, grad_out, sink_logit_values, row_start):
    row_total = query_rot.shape[0]
    block_row_span = min(row_total, 512)

    def block_step(grad_all, block_index):
        block_begin = block_index * block_row_span
        attended, query_diff, kv_diff = attend_block(
            query_rot, keys_all, grad_out, sink_logit_values, row_start + block_begin - WINDOW
        )
        previous = grad_all
        grad_all = previous + kv_diff
        return (grad_all, (attended, query_diff))

    start_grad = jnp.zeros((row_total + WINDOW, keys_all.shape[1]), jnp.float32)
    grad_all, (attended, query_diff) = lax.scan(
        block_step, start_grad, jnp.arange(row_total // block_row_span, dtype=jnp.int32)
    )
    return (
        attended.reshape(row_total, QUERY_HEADS * HEAD_SIZE),
        query_diff.reshape(row_total, QUERY_HEADS * HEAD_SIZE),
        grad_all,
    )


def local(tokens, queries, kv_weight, sink_logit_values, roll_offsets, out_grad):
    token_rows = tokens[0]
    query_rows = queries[0]
    grad_rows = out_grad[0]
    row_total = token_rows.shape[0]
    key_span_width = KEY_VALUE_HEADS * HEAD_SIZE
    seq_index = lax.axis_index("seq")
    seq_count = lax.axis_size("seq")
    stream_length = row_total * seq_count
    row_start = seq_index * row_total
    whole_weight = lax.all_gather(kv_weight, "fsdp", axis=0, tiled=True)
    projected_rows = jnp.dot(token_rows, whole_weight, preferred_element_type=jnp.float32)
    positions = (
        row_start + jnp.arange(row_total, dtype=jnp.int32) + roll_offsets[0]
    ) % stream_length
    cosine_lookup, sine_lookup = rope_tables(positions)
    key_value_rotated = jnp.concatenate(
        [
            apply_rotary(
                projected_rows[:, :key_span_width], cosine_lookup, sine_lookup, KEY_VALUE_HEADS, 1.0
            ),
            projected_rows[:, key_span_width:],
        ],
        axis=1,
    ).astype(jnp.bfloat16)
    query_rot = apply_rotary(
        query_rows.astype(jnp.float32), cosine_lookup, sine_lookup, QUERY_HEADS, 1.0
    ).astype(jnp.bfloat16)
    edge_rows = from_behind(key_value_rotated, "seq", 1)
    keys_all = jnp.concatenate([edge_rows, key_value_rotated], axis=0)
    attended, query_diff, grad_all = band_pass(
        query_rot, keys_all, grad_rows, sink_logit_values, row_start
    )
    incoming = from_behind(grad_all[:WINDOW].astype(jnp.bfloat16), "seq", -1).astype(jnp.float32)
    local_gradient = grad_all[WINDOW:]
    local_gradient = jnp.concatenate(
        [local_gradient[: row_total - WINDOW], local_gradient + incoming], axis=0
    )
    query_back = apply_rotary(query_diff, cosine_lookup, sine_lookup, QUERY_HEADS, -1.0).astype(
        jnp.bfloat16
    )
    key_value_backward = jnp.concatenate(
        [
            apply_rotary(
                local_gradient[:, :key_span_width],
                cosine_lookup,
                sine_lookup,
                KEY_VALUE_HEADS,
                -1.0,
            ),
            local_gradient[:, key_span_width:],
        ],
        axis=1,
    ).astype(jnp.bfloat16)
    token_back = lax.dot_general(
        key_value_backward,
        whole_weight,
        (((1,), (1,)), ((), ())),
        preferred_element_type=jnp.float32,
    ).astype(jnp.bfloat16)
    feature_block = lax.all_to_all(token_rows, "seq", split_axis=1, concat_axis=0, tiled=True)
    block_term = lax.dot_general(
        feature_block,
        lax.all_gather(key_value_backward, "seq", axis=0, tiled=True),
        (((0,), (0,)), ((), ())),
        preferred_element_type=jnp.float32,
    )
    flat_block = block_term.reshape(-1, 128)
    weight_share = lax.psum_scatter(flat_block, "fsdp", scatter_dimension=0, tiled=True)
    return (attended[None], query_back[None], token_back[None], weight_share[None])


def nt(a, b):
    return lax.dot_general(a, b, (((1,), (1,)), ((), ())), preferred_element_type=jnp.float32)


def tn(a, b):
    return lax.dot_general(a, b, (((0,), (0,)), ((), ())), preferred_element_type=jnp.float32)


def nn(a, b):
    return lax.dot_general(a, b, (((1,), (0,)), ((), ())), preferred_element_type=jnp.float32)


def cos_sin(angle):
    count = jnp.floor(angle * (2.0 / math.pi) + 0.5)
    rest = angle - count * 1.5703125
    rest = rest - count * 4.837512969970703125e-4
    rest = rest - count * 7.54978995489188216e-8
    z = rest * rest
    s = rest + rest * z * ((-1.9515295891e-4 * z + 8.3321608736e-3) * z - 1.6666654611e-1)
    c = 1.0 - 0.5 * z + z * z * ((2.443315711809948e-5 * z - 1.388731625493765e-3) * z + 4.166664568298827e-2)
    quarter = count.astype(jnp.int32) & 3
    odd = (quarter & 1) == 1
    cosine = jnp.where(odd, s, c)
    sine = jnp.where(odd, c, s)
    return (
        jnp.where((quarter == 1) | (quarter == 2), -cosine, cosine),
        jnp.where(quarter >= 2, -sine, sine),
    )


def turn(x, cosine, sine, back):
    width = x.shape[1]
    lane = lax.broadcasted_iota(jnp.int32, x.shape, 1)
    swapped = jnp.where(
        (lane & (HEAD_SIZE - 1)) < HEAD_SIZE // 2,
        pltpu.roll(x, width - HEAD_SIZE // 2, 1),
        pltpu.roll(x, HEAD_SIZE // 2, 1),
    )
    times = width // cosine.shape[1]
    cosine = jnp.concatenate([cosine] * times, axis=1)
    sine = jnp.concatenate([sine] * times, axis=1)
    if back:
        return x * cosine - swapped * sine
    return x * cosine + swapped * sine


def fused_kernel(
    nz, ns, share, pad,
    tok_hbm, q_hbm, w, sinks, rolls, og_hbm,
    attn_v, qgrad_v, tgrad_v, wgrad,
    wall, tok, q, og, tokf, tokpad, tokblk, qs, gs, kvbuf, prob_t, dscore_t,
    own_g, hg_out, hg_in, dkv_all, core_out, core_in, mine, zsum, z_out, z_in, total, esink,
    ins, rs_l, rr_l, rs_r, rr_r, qsn, qrn, ps, pr, ts, tr, hs, hr, gsn, grn, dsn, drn, cs, cr, rs, rr,
):
    nf = 2 * nz
    rows = q.shape[0]
    krows = w.shape[0]
    groups = KEY_VALUE_HEADS
    per = QUERY_HEADS // KEY_VALUE_HEADS
    span = per * HEAD_SIZE
    half = nz * pad
    f = lax.axis_index("fsdp")
    s = lax.axis_index("seq")
    z = f // 2
    c = f % 2
    partner = (f + 1 - 2 * c, s)

    def zpeer(d):
        return lax.rem(z + d, nz) * 2 + c

    def speer(d):
        return lax.rem(s + d, ns)

    def remote(src, dst, a, b, dev):
        return pltpu.make_async_remote_copy(
            src_ref=src, dst_ref=dst, send_sem=a, recv_sem=b,
            device_id=dev, device_id_type=pl.DeviceIdType.MESH,
        )

    def lanes_of(i, size):
        return pl.ds(pl.multiple_of(i * size, 128), size)

    cols = lanes_of(s, 128)
    loads = [
        pltpu.make_async_copy(tok_hbm, tok, ins.at[0]),
        pltpu.make_async_copy(q_hbm, q, ins.at[1]),
        pltpu.make_async_copy(og_hbm, og, ins.at[2]),
    ]
    for j in range(ns):
        own = w.at[:, j * 128 : (j + 1) * 128]
        loads.append(pltpu.make_async_copy(own, wall.at[j, f], ins.at[3 + j]))
    for cp in loads:
        cp.start()

    barrier = pltpu.get_barrier_semaphore()
    for d in range(1, nz):
        pl.semaphore_signal(barrier, inc=1, device_id=(zpeer(d), s), device_id_type=pl.DeviceIdType.MESH)
    for d in range(1, ns):
        pl.semaphore_signal(barrier, inc=1, device_id=(f, speer(d)), device_id_type=pl.DeviceIdType.MESH)
    pl.semaphore_signal(barrier, inc=1, device_id=partner, device_id_type=pl.DeviceIdType.MESH)
    lane = lax.broadcasted_iota(jnp.int32, (rows, 128), 1)
    turn_lane = (lane & (HEAD_SIZE // 2 - 1)).astype(jnp.float32) / (HEAD_SIZE // 2)
    frequency = jnp.exp(turn_lane * (-math.log(rope_base)))
    position = lax.rem(
        s * rows + rolls[0] + lax.broadcasted_iota(jnp.int32, (rows, 128), 0), rows * ns
    )
    angle = position.astype(jnp.float32) * frequency
    cosine, sine = cos_sin(angle)
    sine = jnp.where((lane & (HEAD_SIZE - 1)) < HEAD_SIZE // 2, -sine, sine)
    for p in range(QUERY_HEADS // 2):
        pair = [jnp.full((1, rows), sinks[2 * p + i], jnp.float32) for i in range(2)]
        esink[p] = jnp.exp(jnp.concatenate(pair, axis=1))

    pl.semaphore_wait(barrier, nz + ns - 1)

    sent = []

    def send(*args):
        cp = remote(*args)
        cp.start()
        sent.append(cp)

    def chain(k, right):
        at = z + k if right else z - k
        there = at < nz if right else at >= 0
        onward = z >= 1 if right else z + 1 < nz
        onto = ((z - 1 if right else z + 1) * 2 + c, s)
        return at * 2 + c, there, onward, onto

    def link(k, right):
        block, _, _, onto = chain(k, right)
        a, b = (rs_r, rr_r) if right else (rs_l, rr_l)
        piece = wall.at[s, block]
        source = w.at[:, cols] if k == 0 else piece
        return remote(source, piece, a.at[k], b.at[k], onto)

    def arrived(k, right):
        block, _, _, onto = chain(k, right)
        b = rr_r if right else rr_l
        piece = wall.at[s, block]
        return remote(piece, piece, rs_l.at[0], b.at[k - 1], onto)

    across = s + 1 - 2 * (s % 2)
    along = s + 2 - 4 * (s // 2)
    corner = ns - 1 - s

    def over_seq(owner, block, e, peer):
        piece = wall.at[owner, block]
        return remote(piece, piece, qsn.at[block // 2, e], qrn.at[block // 2, e], (f, peer))

    def relay(block):
        way = (block // 2 + c) % 2
        owner = across + way * (along - across)
        peer = along + way * (across - along)
        return over_seq(owner, block, 2, peer)

    def over_core(block):
        piece = wall.at[:, block]
        return remote(piece, piece, ps.at[block // 2], pr.at[block // 2], partner)

    ways = [(k, right) for k in range(1, nz) for right in (False, True)]

    for right in (False, True):

        @pl.when(chain(0, right)[2])
        def _(right=right):
            link(0, right).start()

    for cp in loads[3:]:
        cp.wait()
    over_core(f).start()

    loads[0].wait()
    for i in range(nf):
        tokf[i, :, :krows] = tok[i * krows : (i + 1) * krows, :].T

    for k, right in ways:
        block, there, onward, _ = chain(k, right)

        @pl.when(there)
        def _(k=k, right=right, block=block):
            arrived(k, right).wait_recv()
            over_seq(s, block, 0, across).start()
            over_seq(s, block, 1, along).start()

        @pl.when(there & onward)
        def _(k=k, right=right):
            link(k, right).start()

    tokpad[...] = jnp.zeros_like(tokpad)
    for t in range(ns):
        for j in range(2):
            for i in range(nz):
                start = (t * nf + 2 * i + j) * share
                to = (j * nz + i) * pad
                tokpad[t, to : to + share, :] = tok[start : start + share, :]
    tokblk[s] = tokpad[s]

    loads[1].wait()
    loads[2].wait()

    def stack_heads(g):
        if g >= groups:
            return
        here = lanes_of(g, span)
        x = turn(q[:, here].astype(jnp.float32), cosine, sine, False).astype(jnp.bfloat16)
        x = x * jnp.asarray(HEAD_SIZE ** (-0.5), jnp.bfloat16)
        o = og[:, here]
        for h in range(per):
            qs[g, h * rows : (h + 1) * rows, :] = x[:, h * HEAD_SIZE : (h + 1) * HEAD_SIZE]
            gs[g, h * rows : (h + 1) * rows, :] = o[:, h * HEAD_SIZE : (h + 1) * HEAD_SIZE]

    def whole(block):
        return jnp.concatenate([wall[j, block] for j in range(ns)], axis=1)

    def part(block):
        return nn(tokf[block][:, :krows], whole(block))

    def pass_on(k, right):
        block, there, _, _ = chain(k, right)

        @pl.when(there)
        def _():
            over_seq(across, block, 0, across).wait_recv()
            over_seq(along, block, 1, along).wait_recv()
            relay(block).start()

    def take(k, right):
        block, there, _, _ = chain(k, right)

        @pl.when(there)
        def _():
            over_seq(corner, block, 2, along).wait_recv()
            over_core(block).start()
            total[...] += part(block)

    other = f + 1 - 2 * c
    total[...] = part(f)
    for i, way in enumerate(ways):
        stack_heads(i)
        pass_on(*way)
        if i == 1:
            over_core(other).wait_recv()
            total[...] += part(other)
        if i > 0:
            take(*ways[i - 1])
    take(*ways[-1])
    for k, right in ways:
        block, there, _, _ = chain(k, right)

        @pl.when(there)
        def _(block=block):
            over_core(block + 1 - 2 * c).wait_recv()
            total[...] += part(block + 1 - 2 * c)

    def halo_copy(g):
        edge = kvbuf.at[g, pl.ds(WINDOW, WINDOW), :]
        return remote(edge, kvbuf.at[g, pl.ds(0, WINDOW), :], hs.at[g], hr.at[g], (f, speer(1)))

    key_width = groups * HEAD_SIZE
    keys = turn(total[:, :key_width], cosine, sine, False).astype(jnp.bfloat16)
    values = total[:, key_width:].astype(jnp.bfloat16)
    for g in range(groups):
        lo, hi = g * HEAD_SIZE, (g + 1) * HEAD_SIZE
        kvbuf[g, WINDOW:, :] = jnp.concatenate([keys[:, lo:hi], values[:, lo:hi]], axis=1)
        halo_copy(g).start()
    halo_copy(0).wait_recv()
    for e in range(1, ns):
        send(tokpad.at[speer(e)], tokblk.at[s], ts.at[e - 1], tr.at[e - 1], (f, speer(e)))
    before = speer(ns - 1)
    mine_rows = pl.ds(pl.multiple_of(s * rows, 128), rows)

    def hg_copy(g):
        return remote(hg_out.at[g], hg_in.at[g], gsn.at[g], grn.at[g], (f, before))

    def attention(g):
        @pl.when(g > 0)
        def _():
            halo_copy(g).wait_recv()

        kv = kvbuf[g]
        key, value = kv[:, :HEAD_SIZE], kv[:, HEAD_SIZE:]
        kv_t = kv.T
        key_t, value_t = kv_t[:HEAD_SIZE], kv_t[HEAD_SIZE:]
        slot = lax.broadcasted_iota(jnp.int32, (rows, 2 * rows), 0)
        at = lax.broadcasted_iota(jnp.int32, (rows, 2 * rows), 1) & (rows - 1)
        is_own = slot <= at
        valid = slot <= at + s * rows

        def chosen(x):
            return jnp.where(is_own, x[WINDOW:], x[:WINDOW])

        def spread(x):
            borrowed = jnp.where(is_own, 0.0, x)
            return jnp.concatenate([borrowed, jnp.where(is_own, x, 0.0)], axis=0).astype(jnp.bfloat16)

        for p in range(per // 2):
            two = slice(p * 2 * rows, (p + 1) * 2 * rows)
            query, grad = qs[g, two, :], gs[g, two, :]
            expo = jnp.where(valid, jnp.exp(chosen(nt(key, query))), 0.0)
            denominator = esink[g * (per // 2) + p] + jnp.sum(expo, axis=0, keepdims=True)
            probs = expo * (1.0 / denominator)
            dprob = chosen(nt(value, grad))
            delta = jnp.sum(probs * dprob, axis=0, keepdims=True)
            probs_b = spread(probs)
            dscore = spread(probs * (dprob - delta))
            prob_t[:, two] = probs_b
            dscore_t[:, two] = dscore
            out = nn(value_t, probs_b)
            dq = nn(key_t, dscore) * (HEAD_SIZE ** (-0.5))
            out = jnp.concatenate([out[:, :rows], out[:, rows:]], axis=0).T
            dq = jnp.concatenate([dq[:, :rows], dq[:, rows:]], axis=0).T
            here = pl.ds(pl.multiple_of(g * span + p * 128, 128), 128)
            attn_v[:, here] = out.astype(jnp.bfloat16)
            qgrad_v[:, here] = turn(dq, cosine, sine, True).astype(jnp.bfloat16)
        dkv = jnp.concatenate([nn(dscore_t[...], qs[g]), nn(prob_t[...], gs[g])], axis=1)
        hg_out[g] = dkv[:WINDOW].astype(jnp.bfloat16)
        own_g[g] = dkv[WINDOW:]
        hg_copy(g).start()

    def dkv_copy(g, e):
        piece = dkv_all.at[g, mine_rows, :]
        return remote(piece, piece, dsn.at[g, e - 1], drn.at[g, e - 1], (f, speer(e)))

    def finish(g):
        hg_copy(g).wait_recv()
        both = own_g[g] + hg_in[g].astype(jnp.float32)
        lane = lax.broadcasted_iota(jnp.int32, both.shape, 1)
        dkv = jnp.where(lane < HEAD_SIZE, turn(both, cosine, sine, True), both)
        dkv_all[g, mine_rows, :] = dkv.astype(jnp.bfloat16)
        for e in range(1, ns):
            dkv_copy(g, e).start()

    def core_copy(g):
        return remote(core_out.at[g], core_in.at[g], cs.at[g], cr.at[g], partner)

    def features(core):
        there = pl.ds(pl.multiple_of(core * half, 128), half)
        return jnp.concatenate([tokblk[t, there, :] for t in range(ns)], axis=1)

    def weight_part(g):
        for e in range(1, ns):
            src = lax.rem(s + ns - e, ns)
            piece = dkv_all.at[g, pl.ds(pl.multiple_of(src * rows, 128), rows), :]
            remote(piece, piece, dsn.at[g, e - 1], drn.at[g, e - 1], (f, src)).wait_recv()
        dkv = dkv_all[g]
        core_out[g] = nn(features(1 - c), dkv).astype(jnp.bfloat16)
        core_copy(g).start()
        mine[g] = nn(features(c), dkv)

    def z_copy(g, d):
        return remote(z_out.at[g, d - 1], z_in.at[g, d - 1], rs.at[g, d - 1], rr.at[g, d - 1], (zpeer(d), s))

    def z_part(g):
        core_copy(g).wait_recv()
        zsum[g] = (mine[g] + core_in[g].astype(jnp.float32)).reshape(nz, pad, 128)
        for d in range(1, nz):
            z_out[g, d - 1] = zsum[g, lax.rem(z + d, nz)].astype(jnp.bfloat16)
            z_copy(g, d).start()

    def token_blocks():
        for e in range(1, ns):
            src = lax.rem(s + ns - e, ns)
            remote(tokpad.at[src], tokblk.at[src], ts.at[e - 1], tr.at[e - 1], (f, src)).wait_recv()

    @pl.loop(0, groups)
    def _(g):
        attention(g)

        @pl.when(g >= 1)
        def _():
            finish(g - 1)

        @pl.when(g == 2)
        def _():
            token_blocks()

        @pl.when(g >= 2)
        def _():
            weight_part(g - 2)

        @pl.when(g >= 3)
        def _():
            z_part(g - 3)

    finish(groups - 1)
    weight_part(groups - 2)
    z_part(groups - 3)
    pieces = [dkv_all[g, mine_rows, :] for g in range(groups)]
    dkv = jnp.concatenate([b[:, :HEAD_SIZE] for b in pieces] + [b[:, HEAD_SIZE:] for b in pieces], axis=1)
    for i in range(nf):
        tgrad_v[i * krows : (i + 1) * krows, :] = nt(whole(i), dkv).astype(jnp.bfloat16)
    weight_part(groups - 1)
    z_part(groups - 2)
    z_part(groups - 1)

    sums = []
    for g in range(groups):
        acc = zsum[g, z]
        for d in range(1, nz):
            z_copy(g, d).wait_recv()
            acc = acc + z_in[g, d - 1].astype(jnp.float32)
        sums.append(acc[:share])
    order = []
    for lo in (0, HEAD_SIZE):
        for g in range(0, groups, 2):
            order.append(jnp.concatenate([sums[g][:, lo : lo + HEAD_SIZE], sums[g + 1][:, lo : lo + HEAD_SIZE]], axis=1))
    for j in range(groups):
        wgrad[pl.ds(j, share, stride=groups), :] = order[j]

    for cp in sent:
        cp.wait_send()
    for g in range(groups):
        hg_copy(g).wait_send()
        halo_copy(g).wait_send()
        core_copy(g).wait_send()
        for e in range(1, ns):
            dkv_copy(g, e).wait_send()
        for d in range(1, nz):
            z_copy(g, d).wait_send()
    for k in range(nz):
        for right in (False, True):
            _, there, onward, _ = chain(k, right)

            @pl.when(there & onward)
            def _(k=k, right=right):
                link(k, right).wait_send()

            if k > 0:

                @pl.when(there)
                def _(k=k, right=right):
                    block = chain(k, right)[0]
                    over_seq(s, block, 0, across).wait_send()
                    over_seq(s, block, 1, along).wait_send()
                    relay(block).wait_send()
                    over_core(block).wait_send()

    over_core(f).wait_send()


def write_out(*refs):
    done = refs[8]
    copies = [pltpu.make_async_copy(refs[i], refs[4 + i], done.at[i]) for i in range(4)]
    for cp in copies:
        cp.start()
    for cp in copies:
        cp.wait()


KW_COLUMNS = 2 * KEY_VALUE_HEADS * HEAD_SIZE


def fused(tokens, queries, kv_weight, sink_logit_values, roll_offsets, out_grad):
    nf = lax.axis_size("fsdp")
    ns = lax.axis_size("seq")
    nz = nf // 2
    rows, width = tokens.shape[1:]
    krows = kv_weight.shape[0]
    share = width // (nf * ns)
    pad = -(-share // 16) * 16
    half = nz * pad
    query_width = QUERY_HEADS * HEAD_SIZE
    groups = KEY_VALUE_HEADS
    per = QUERY_HEADS // groups
    bf, f32 = jnp.bfloat16, jnp.float32
    sem = pltpu.SemaphoreType.DMA
    vm = pltpu.VMEM
    shape = jax.ShapeDtypeStruct
    anywhere = pl.BlockSpec(memory_space=pl.ANY)
    inside = pl.BlockSpec(memory_space=pltpu.VMEM)
    scalars = pl.BlockSpec(memory_space=pltpu.SMEM)
    results = pl.pallas_call(
        functools.partial(fused_kernel, nz, ns, share, pad),
        out_shape=(
            shape((rows, query_width), bf),
            shape((rows, query_width), bf),
            shape((width, rows), bf),
            shape((share * groups, 128), f32),
        ),
        in_specs=[anywhere, anywhere, anywhere, scalars, scalars, anywhere],
        out_specs=[inside] * 4,
        scratch_shapes=[
            vm((ns, nf, krows, 128), bf),
            vm((width, rows), bf),
            vm((rows, query_width), bf),
            vm((rows, query_width), bf),
            vm((nf, rows, -(-krows // 128) * 128), bf),
            vm((ns, nf * pad, rows), bf),
            vm((ns, nf * pad, rows), bf),
            vm((groups, per * rows, HEAD_SIZE), bf),
            vm((groups, per * rows, HEAD_SIZE), bf),
            vm((groups, rows + WINDOW, 2 * HEAD_SIZE), bf),
            vm((rows + WINDOW, per * rows), bf),
            vm((rows + WINDOW, per * rows), bf),
            vm((groups, rows, 2 * HEAD_SIZE), f32),
            vm((groups, WINDOW, 2 * HEAD_SIZE), bf),
            vm((groups, WINDOW, 2 * HEAD_SIZE), bf),
            vm((groups, ns * rows, 2 * HEAD_SIZE), bf),
            vm((groups, half, 128), bf),
            vm((groups, half, 128), bf),
            vm((groups, half, 128), f32),
            vm((groups, nz, pad, 128), f32),
            vm((groups, nz - 1, pad, 128), bf),
            vm((groups, nz - 1, pad, 128), bf),
            vm((rows, KW_COLUMNS), f32),
            vm((QUERY_HEADS // 2, 1, 2 * rows), f32),
            sem((3 + ns,)),
            sem((nz,)), sem((nz,)), sem((nz,)), sem((nz,)),
            sem((nz, ns - 1)), sem((nz, ns - 1)),
            sem((nz,)), sem((nz,)),
            sem((ns - 1,)), sem((ns - 1,)),
            sem((groups,)), sem((groups,)),
            sem((groups,)), sem((groups,)),
            sem((groups, ns - 1)), sem((groups, ns - 1)),
            sem((groups,)), sem((groups,)),
            sem((groups, nz - 1)), sem((groups, nz - 1)),
        ],
        compiler_params=pltpu.CompilerParams(
            collective_id=0, has_side_effects=True, vmem_limit_bytes=56 * 1024 * 1024
        ),
    )(tokens[0].T, queries[0], kv_weight, sink_logit_values, roll_offsets, out_grad[0])
    attn, qgrad, tgrad, wgrad = pl.pallas_call(
        write_out,
        out_shape=tuple(shape(x.shape, x.dtype) for x in results),
        in_specs=[inside] * 4,
        out_specs=[anywhere] * 4,
        scratch_shapes=[sem((4,))],
    )(*results)
    return (attn[None], qgrad[None], tgrad.T[None], wgrad[None])


def fits_fused(mesh):
    nf, ns = mesh.shape["fsdp"], mesh.shape["seq"]
    return nf == 8 and KW_COLUMNS == 128 * ns


def solution(mesh):
    placed = (
        P("fsdp", "seq", None),
        P("fsdp", "seq", None),
        P("fsdp", None),
        P(),
        P("fsdp"),
        P("fsdp", "seq", None),
    )
    return jax.shard_map(
        fused if fits_fused(mesh) else local,
        mesh=mesh,
        in_specs=placed,
        out_specs=(
            P("fsdp", "seq", None),
            P("fsdp", "seq", None),
            P("fsdp", "seq", None),
            P("seq", "fsdp", None),
        ),
        check_vma=False,
    )
```

```python
import functools
import math

import jax
import jax.numpy as jnp
from jax import lax
from jax.experimental import pallas as pl
from jax.experimental.pallas import tpu as pltpu
from jax.sharding import PartitionSpec as P

QUERY_HEADS = 32
KEY_VALUE_HEADS = 4
HEAD_SIZE = 64
WINDOW = 128


rope_base = 150000.0


def from_behind(array, axis, by):
    peers = lax.axis_size(axis)
    pairs = [(i, i + by) for i in range(peers) if 0 <= i + by < peers]
    return lax.ppermute(array, axis, pairs)


def rope_tables(positions):
    half_width = HEAD_SIZE // 2
    frequency = rope_base ** (-jnp.arange(half_width, dtype=jnp.float32) / half_width)
    angle = positions.astype(jnp.float32)[:, None] * frequency[None, :]
    return (jnp.cos(angle), jnp.sin(angle))


def apply_rotary(values, cosine_lookup, sine_lookup, head_count, direction):
    row_count = values.shape[0]
    halves = values.reshape(row_count, head_count, 2, HEAD_SIZE // 2)
    front_half = halves[:, :, 0]
    back_half = halves[:, :, 1]
    cosine_rows = cosine_lookup[:, None, :]
    sine_rows = sine_lookup[:, None, :] * direction
    turned = jnp.stack(
        [
            front_half * cosine_rows - back_half * sine_rows,
            front_half * sine_rows + back_half * cosine_rows,
        ],
        axis=2,
    )
    return turned.reshape(row_count, head_count * HEAD_SIZE)


def attend_group(query_g, key_g, value_g, grad_g, sink_g, allowed):
    score_scale = HEAD_SIZE ** (-0.5)
    scores = (
        jnp.einsum("bgd,kd->gbk", query_g, key_g, preferred_element_type=jnp.float32) * score_scale
    )
    exponent = jnp.where(allowed[None], jnp.exp(scores), 0.0)
    denominator = jnp.exp(sink_g)[:, None] + jnp.sum(exponent, axis=2)
    softmax_w = exponent / denominator[:, :, None]
    softmax_b = softmax_w.astype(jnp.bfloat16)
    attended = jnp.einsum("gbk,kd->bgd", softmax_b, value_g, preferred_element_type=jnp.float32)
    dprob = jnp.einsum("bgd,kd->gbk", grad_g, value_g, preferred_element_type=jnp.float32)
    row_delta = jnp.sum(softmax_w * dprob, axis=2)
    dscore = (softmax_w * (dprob - row_delta[:, :, None]) * score_scale).astype(jnp.bfloat16)
    query_diff = jnp.einsum("gbk,kd->bgd", dscore, key_g, preferred_element_type=jnp.float32)
    key_diff = jnp.einsum("gbk,bgd->kd", dscore, query_g, preferred_element_type=jnp.float32)
    value_diff = jnp.einsum("gbk,bgd->kd", softmax_b, grad_g, preferred_element_type=jnp.float32)
    return (attended.astype(jnp.bfloat16), query_diff, key_diff, value_diff)


def attend_block(query_block, key_block, gradient_block, sink_logit_values, key_first):
    block_row_span = query_block.shape[0]
    key_row_slice = key_block.shape[0]
    group_width = QUERY_HEADS // KEY_VALUE_HEADS
    key_span_width = KEY_VALUE_HEADS * HEAD_SIZE
    rows_idx = jnp.arange(block_row_span, dtype=jnp.int32)[:, None]
    cols_idx = jnp.arange(key_row_slice, dtype=jnp.int32)[None, :]
    allowed = (cols_idx > rows_idx) & (cols_idx <= rows_idx + WINDOW) & (cols_idx + key_first >= 0)
    query_head_rows = query_block.reshape(
        block_row_span, KEY_VALUE_HEADS, group_width, HEAD_SIZE
    ).transpose(1, 0, 2, 3)
    gradient_heads = gradient_block.reshape(
        block_row_span, KEY_VALUE_HEADS, group_width, HEAD_SIZE
    ).transpose(1, 0, 2, 3)
    key_head_rows = (
        key_block[:, :key_span_width]
        .reshape(key_row_slice, KEY_VALUE_HEADS, HEAD_SIZE)
        .transpose(1, 0, 2)
    )
    value_head_rows = (
        key_block[:, key_span_width:]
        .reshape(key_row_slice, KEY_VALUE_HEADS, HEAD_SIZE)
        .transpose(1, 0, 2)
    )
    sink_per_head = sink_logit_values.reshape(KEY_VALUE_HEADS, group_width)

    def per_group(packed):
        return attend_group(packed[0], packed[1], packed[2], packed[3], packed[4], allowed)

    attended, query_diff, key_diff, value_diff = lax.map(
        per_group, (query_head_rows, key_head_rows, value_head_rows, gradient_heads, sink_per_head)
    )
    attended = attended.transpose(1, 0, 2, 3).reshape(block_row_span, QUERY_HEADS * HEAD_SIZE)
    query_diff = query_diff.transpose(1, 0, 2, 3).reshape(block_row_span, QUERY_HEADS * HEAD_SIZE)
    kv_diff = jnp.concatenate(
        [
            key_diff.transpose(1, 0, 2).reshape(key_row_slice, key_span_width),
            value_diff.transpose(1, 0, 2).reshape(key_row_slice, key_span_width),
        ],
        axis=1,
    )
    return (attended, query_diff, kv_diff)


def band_pass(query_rot, keys_all, grad_out, sink_logit_values, row_start):
    row_total = query_rot.shape[0]
    block_row_span = min(row_total, 512)

    def block_step(grad_all, block_index):
        block_begin = block_index * block_row_span
        attended, query_diff, kv_diff = attend_block(
            query_rot, keys_all, grad_out, sink_logit_values, row_start + block_begin - WINDOW
        )
        previous = grad_all
        grad_all = previous + kv_diff
        return (grad_all, (attended, query_diff))

    start_grad = jnp.zeros((row_total + WINDOW, keys_all.shape[1]), jnp.float32)
    grad_all, (attended, query_diff) = lax.scan(
        block_step, start_grad, jnp.arange(row_total // block_row_span, dtype=jnp.int32)
    )
    return (
        attended.reshape(row_total, QUERY_HEADS * HEAD_SIZE),
        query_diff.reshape(row_total, QUERY_HEADS * HEAD_SIZE),
        grad_all,
    )


def local(tokens, queries, kv_weight, sink_logit_values, roll_offsets, out_grad):
    token_rows = tokens[0]
    query_rows = queries[0]
    grad_rows = out_grad[0]
    row_total = token_rows.shape[0]
    key_span_width = KEY_VALUE_HEADS * HEAD_SIZE
    seq_index = lax.axis_index("seq")
    seq_count = lax.axis_size("seq")
    stream_length = row_total * seq_count
    row_start = seq_index * row_total
    whole_weight = lax.all_gather(kv_weight, "fsdp", axis=0, tiled=True)
    projected_rows = jnp.dot(token_rows, whole_weight, preferred_element_type=jnp.float32)
    positions = (
        row_start + jnp.arange(row_total, dtype=jnp.int32) + roll_offsets[0]
    ) % stream_length
    cosine_lookup, sine_lookup = rope_tables(positions)
    key_value_rotated = jnp.concatenate(
        [
            apply_rotary(
                projected_rows[:, :key_span_width], cosine_lookup, sine_lookup, KEY_VALUE_HEADS, 1.0
            ),
            projected_rows[:, key_span_width:],
        ],
        axis=1,
    ).astype(jnp.bfloat16)
    query_rot = apply_rotary(
        query_rows.astype(jnp.float32), cosine_lookup, sine_lookup, QUERY_HEADS, 1.0
    ).astype(jnp.bfloat16)
    edge_rows = from_behind(key_value_rotated, "seq", 1)
    keys_all = jnp.concatenate([edge_rows, key_value_rotated], axis=0)
    attended, query_diff, grad_all = band_pass(
        query_rot, keys_all, grad_rows, sink_logit_values, row_start
    )
    incoming = from_behind(grad_all[:WINDOW].astype(jnp.bfloat16), "seq", -1).astype(jnp.float32)
    local_gradient = grad_all[WINDOW:]
    local_gradient = jnp.concatenate(
        [local_gradient[: row_total - WINDOW], local_gradient + incoming], axis=0
    )
    query_back = apply_rotary(query_diff, cosine_lookup, sine_lookup, QUERY_HEADS, -1.0).astype(
        jnp.bfloat16
    )
    key_value_backward = jnp.concatenate(
        [
            apply_rotary(
                local_gradient[:, :key_span_width],
                cosine_lookup,
                sine_lookup,
                KEY_VALUE_HEADS,
                -1.0,
            ),
            local_gradient[:, key_span_width:],
        ],
        axis=1,
    ).astype(jnp.bfloat16)
    token_back = lax.dot_general(
        key_value_backward,
        whole_weight,
        (((1,), (1,)), ((), ())),
        preferred_element_type=jnp.float32,
    ).astype(jnp.bfloat16)
    feature_block = lax.all_to_all(token_rows, "seq", split_axis=1, concat_axis=0, tiled=True)
    block_term = lax.dot_general(
        feature_block,
        lax.all_gather(key_value_backward, "seq", axis=0, tiled=True),
        (((0,), (0,)), ((), ())),
        preferred_element_type=jnp.float32,
    )
    flat_block = block_term.reshape(-1, 128)
    weight_share = lax.psum_scatter(flat_block, "fsdp", scatter_dimension=0, tiled=True)
    return (attended[None], query_back[None], token_back[None], weight_share[None])


def nt(a, b):
    return lax.dot_general(a, b, (((1,), (1,)), ((), ())), preferred_element_type=jnp.float32)


def tn(a, b):
    return lax.dot_general(a, b, (((0,), (0,)), ((), ())), preferred_element_type=jnp.float32)


def nn(a, b):
    return lax.dot_general(a, b, (((1,), (0,)), ((), ())), preferred_element_type=jnp.float32)


def cos_sin(angle):
    count = jnp.floor(angle * (2.0 / math.pi) + 0.5)
    rest = angle - count * 1.5703125
    rest = rest - count * 4.837512969970703125e-4
    rest = rest - count * 7.54978995489188216e-8
    z = rest * rest
    s = rest + rest * z * ((-1.9515295891e-4 * z + 8.3321608736e-3) * z - 1.6666654611e-1)
    c = 1.0 - 0.5 * z + z * z * ((2.443315711809948e-5 * z - 1.388731625493765e-3) * z + 4.166664568298827e-2)
    quarter = count.astype(jnp.int32) & 3
    odd = (quarter & 1) == 1
    cosine = jnp.where(odd, s, c)
    sine = jnp.where(odd, c, s)
    return (
        jnp.where((quarter == 1) | (quarter == 2), -cosine, cosine),
        jnp.where(quarter >= 2, -sine, sine),
    )


def turn(x, cosine, sine, back):
    width = x.shape[1]
    lane = lax.broadcasted_iota(jnp.int32, x.shape, 1)
    swapped = jnp.where(
        (lane & (HEAD_SIZE - 1)) < HEAD_SIZE // 2,
        pltpu.roll(x, width - HEAD_SIZE // 2, 1),
        pltpu.roll(x, HEAD_SIZE // 2, 1),
    )
    times = width // cosine.shape[1]
    cosine = jnp.concatenate([cosine] * times, axis=1)
    sine = jnp.concatenate([sine] * times, axis=1)
    if back:
        return x * cosine - swapped * sine
    return x * cosine + swapped * sine


def fused_kernel(
    nz, ns, share, pad,
    tok_hbm, q_hbm, w, sinks, rolls, og_hbm,
    attn_v, qgrad_v, tgrad_v, wgrad,
    wall, tok, q, og, tokf, tokpad, tokblk, qs, qpair, gpair, kvbuf, prob_t, dscore_t,
    own_g, hg_out, hg_in, dkv_all, core_out, core_in, mine, zsum, z_out, z_in, total, esink,
    ins, rs_l, rr_l, rs_r, rr_r, qsn, qrn, ps, pr, ts, tr, hs, hr, gsn, grn, dsn, drn, cs, cr, rs, rr,
):
    nf = 2 * nz
    rows = q.shape[0]
    krows = w.shape[0]
    groups = KEY_VALUE_HEADS
    per = QUERY_HEADS // KEY_VALUE_HEADS
    span = per * HEAD_SIZE
    half = nz * pad
    f = lax.axis_index("fsdp")
    s = lax.axis_index("seq")
    z = f // 2
    c = f % 2
    partner = (f + 1 - 2 * c, s)

    def zpeer(d):
        return lax.rem(z + d, nz) * 2 + c

    def speer(d):
        return lax.rem(s + d, ns)

    def remote(src, dst, a, b, dev):
        return pltpu.make_async_remote_copy(
            src_ref=src, dst_ref=dst, send_sem=a, recv_sem=b,
            device_id=dev, device_id_type=pl.DeviceIdType.MESH,
        )

    def lanes_of(i, size):
        return pl.ds(pl.multiple_of(i * size, 128), size)

    cols = lanes_of(s, 128)
    loads = [
        pltpu.make_async_copy(tok_hbm, tok, ins.at[0]),
        pltpu.make_async_copy(q_hbm, q, ins.at[1]),
        pltpu.make_async_copy(og_hbm, og, ins.at[2]),
    ]
    for j in range(ns):
        own = w.at[:, j * 128 : (j + 1) * 128]
        loads.append(pltpu.make_async_copy(own, wall.at[j, f], ins.at[3 + j]))
    for cp in loads:
        cp.start()

    barrier = pltpu.get_barrier_semaphore()
    for d in range(1, nz):
        pl.semaphore_signal(barrier, inc=1, device_id=(zpeer(d), s), device_id_type=pl.DeviceIdType.MESH)
    for d in range(1, ns):
        pl.semaphore_signal(barrier, inc=1, device_id=(f, speer(d)), device_id_type=pl.DeviceIdType.MESH)
    pl.semaphore_signal(barrier, inc=1, device_id=partner, device_id_type=pl.DeviceIdType.MESH)
    pl.semaphore_wait(barrier, nz + ns - 1)

    sent = []

    def send(*args):
        cp = remote(*args)
        cp.start()
        sent.append(cp)

    def chain(k, right):
        at = z + k if right else z - k
        there = at < nz if right else at >= 0
        onward = z >= 1 if right else z + 1 < nz
        onto = ((z - 1 if right else z + 1) * 2 + c, s)
        return at * 2 + c, there, onward, onto

    def link(k, right):
        block, _, _, onto = chain(k, right)
        a, b = (rs_r, rr_r) if right else (rs_l, rr_l)
        piece = wall.at[s, block]
        source = w.at[:, cols] if k == 0 else piece
        return remote(source, piece, a.at[k], b.at[k], onto)

    def arrived(k, right):
        block, _, _, onto = chain(k, right)
        b = rr_r if right else rr_l
        piece = wall.at[s, block]
        return remote(piece, piece, rs_l.at[0], b.at[k - 1], onto)

    def over_seq(block, e):
        piece = wall.at[s, block]
        return remote(piece, piece, qsn.at[block // 2, e - 1], qrn.at[block // 2, e - 1], (f, speer(e)))

    def over_core(block):
        piece = wall.at[:, block]
        return remote(piece, piece, ps.at[block // 2], pr.at[block // 2], partner)

    ways = [(k, right) for k in range(1, nz) for right in (False, True)]

    for right in (False, True):

        @pl.when(chain(0, right)[2])
        def _(right=right):
            link(0, right).start()

    for cp in loads[3:]:
        cp.wait()
    over_core(f).start()

    loads[0].wait()
    for i in range(nf):
        tokf[i, :, :krows] = tok[i * krows : (i + 1) * krows, :].T

    for k, right in ways:
        block, there, onward, _ = chain(k, right)

        @pl.when(there)
        def _(k=k, right=right, block=block):
            arrived(k, right).wait_recv()
            for e in range(1, ns):
                over_seq(block, e).start()

        @pl.when(there & onward)
        def _(k=k, right=right):
            link(k, right).start()

    lane = lax.broadcasted_iota(jnp.int32, (rows, 128), 1)
    turn_lane = (lane % (HEAD_SIZE // 2)).astype(jnp.float32) / (HEAD_SIZE // 2)
    frequency = jnp.exp(turn_lane * (-math.log(rope_base)))
    position = lax.rem(
        s * rows + rolls[0] + lax.broadcasted_iota(jnp.int32, (rows, 128), 0), rows * ns
    )
    angle = position.astype(jnp.float32) * frequency
    cosine, sine = cos_sin(angle)
    sine = jnp.where(lane % HEAD_SIZE < HEAD_SIZE // 2, -sine, sine)
    for p in range(QUERY_HEADS // 2):
        pair = [jnp.full((1, rows), sinks[2 * p + i], jnp.float32) for i in range(2)]
        esink[p] = jnp.exp(jnp.concatenate(pair, axis=1))

    tokpad[...] = jnp.zeros_like(tokpad)
    for t in range(ns):
        for j in range(2):
            for i in range(nz):
                start = (t * nf + 2 * i + j) * share
                to = (j * nz + i) * pad
                tokpad[t, to : to + share, :] = tok[start : start + share, :]
    tokblk[s] = tokpad[s]

    loads[1].wait()
    loads[2].wait()

    @pl.loop(0, groups)
    def _(g):
        here = lanes_of(g, span)
        x = turn(q[:, here].astype(jnp.float32), cosine, sine, False).astype(jnp.bfloat16)
        qs[:, here] = x * jnp.asarray(HEAD_SIZE ** (-0.5), jnp.bfloat16)

    def whole(block):
        return jnp.concatenate([wall[j, block] for j in range(ns)], axis=1)

    def part(block):
        return nn(tokf[block][:, :krows], whole(block))

    total[...] = part(f)
    other = f + 1 - 2 * c
    over_core(other).wait_recv()
    total[...] += part(other)
    for k, right in ways:
        block, there, _, _ = chain(k, right)

        @pl.when(there)
        def _(block=block):
            for e in range(1, ns):
                piece = wall.at[lax.rem(s + ns - e, ns), block]
                remote(
                    piece, piece, qsn.at[block // 2, e - 1], qrn.at[block // 2, e - 1], (f, speer(e))
                ).wait_recv()
            over_core(block).start()
            total[...] += part(block)

    for k, right in ways:
        block, there, _, _ = chain(k, right)

        @pl.when(there)
        def _(block=block):
            over_core(block + 1 - 2 * c).wait_recv()
            total[...] += part(block + 1 - 2 * c)

    key_width = groups * HEAD_SIZE
    keys = turn(total[:, :key_width], cosine, sine, False).astype(jnp.bfloat16)
    values = total[:, key_width:].astype(jnp.bfloat16)
    for g in range(groups):
        lo, hi = g * HEAD_SIZE, (g + 1) * HEAD_SIZE
        kvbuf[g, WINDOW:, :] = jnp.concatenate([keys[:, lo:hi], values[:, lo:hi]], axis=1)
    halo = remote(
        kvbuf.at[:, pl.ds(WINDOW, WINDOW), :], kvbuf.at[:, pl.ds(0, WINDOW), :], hs, hr, (f, speer(1))
    )
    halo.start()
    halo.wait()
    for e in range(1, ns):
        send(tokpad.at[speer(e)], tokblk.at[s], ts.at[e - 1], tr.at[e - 1], (f, speer(e)))
    before = speer(ns - 1)
    mine_rows = pl.ds(pl.multiple_of(s * rows, 128), rows)

    def hg_copy(g):
        return remote(hg_out.at[g], hg_in.at[g], gsn.at[g], grn.at[g], (f, before))

    def attention(g):
        kv = kvbuf[g]
        key, value = kv[:, :HEAD_SIZE], kv[:, HEAD_SIZE:]
        kv_t = kv.T
        key_t, value_t = kv_t[:HEAD_SIZE], kv_t[HEAD_SIZE:]
        low = lax.broadcasted_iota(jnp.int32, kv.shape, 1) < HEAD_SIZE
        none = jnp.zeros_like(kv)
        swap = jnp.concatenate([value, key], axis=1)
        keys2 = jnp.concatenate([jnp.where(low, kv, none), jnp.where(low, none, swap)], axis=0)
        values2 = jnp.concatenate([jnp.where(low, swap, none), jnp.where(low, none, kv)], axis=0)
        slot = lax.broadcasted_iota(jnp.int32, (rows, 2 * rows), 0)
        at = lax.broadcasted_iota(jnp.int32, (rows, 2 * rows), 1) & (rows - 1)
        is_own = slot <= at
        valid = slot <= at + s * rows
        first = low[:rows]
        empty = none[:rows]

        def side_by_side(x):
            return jnp.concatenate([x[: rows + WINDOW], x[rows + WINDOW :]], axis=1)

        def apart(x):
            return jnp.concatenate([jnp.where(first, x, empty), jnp.where(first, empty, x)], axis=0)

        def chosen(x):
            return jnp.where(is_own, x[WINDOW:], x[:WINDOW])

        def spread(x):
            borrowed = jnp.where(is_own, 0.0, x)
            return jnp.concatenate([borrowed, jnp.where(is_own, x, 0.0)], axis=0).astype(jnp.bfloat16)

        for p in range(per // 2):
            two = slice(p * 2 * rows, (p + 1) * 2 * rows)
            here = pl.ds(pl.multiple_of(g * span + p * 128, 128), 128)
            query, grad = qs[:, here], og[:, here]
            qpair[two, :] = apart(query)
            gpair[two, :] = apart(grad)
            expo = jnp.where(valid, jnp.exp(chosen(side_by_side(nt(keys2, query)))), 0.0)
            denominator = esink[g * (per // 2) + p] + jnp.sum(expo, axis=0, keepdims=True)
            probs = expo * (1.0 / denominator)
            dprob = chosen(side_by_side(nt(values2, grad)))
            delta = jnp.sum(probs * dprob, axis=0, keepdims=True)
            probs_b = spread(probs)
            dscore = spread(probs * (dprob - delta))
            prob_t[:, two] = probs_b
            dscore_t[:, two] = dscore
            out = nn(value_t, probs_b)
            dq = nn(key_t, dscore) * (HEAD_SIZE ** (-0.5))
            out = jnp.concatenate([out[:, :rows], out[:, rows:]], axis=0).T
            dq = jnp.concatenate([dq[:, :rows], dq[:, rows:]], axis=0).T
            here = pl.ds(pl.multiple_of(g * span + p * 128, 128), 128)
            attn_v[:, here] = out.astype(jnp.bfloat16)
            qgrad_v[:, here] = turn(dq, cosine, sine, True).astype(jnp.bfloat16)
        dk = nn(dscore_t[...], qpair[...])
        dv = nn(prob_t[...], gpair[...])
        dkv = jnp.concatenate(
            [dk[:, :HEAD_SIZE] + dk[:, HEAD_SIZE:], dv[:, :HEAD_SIZE] + dv[:, HEAD_SIZE:]], axis=1
        )
        hg_out[g] = dkv[:WINDOW].astype(jnp.bfloat16)
        own_g[g] = dkv[WINDOW:]
        hg_copy(g).start()

    def dkv_copy(g, e):
        piece = dkv_all.at[g, mine_rows, :]
        return remote(piece, piece, dsn.at[g, e - 1], drn.at[g, e - 1], (f, speer(e)))

    def finish(g):
        hg_copy(g).wait_recv()
        both = own_g[g] + hg_in[g].astype(jnp.float32)
        lane = lax.broadcasted_iota(jnp.int32, both.shape, 1)
        dkv = jnp.where(lane < HEAD_SIZE, turn(both, cosine, sine, True), both)
        dkv_all[g, mine_rows, :] = dkv.astype(jnp.bfloat16)
        for e in range(1, ns):
            dkv_copy(g, e).start()

    def core_copy(g):
        return remote(core_out.at[g], core_in.at[g], cs.at[g], cr.at[g], partner)

    def features(core):
        there = pl.ds(pl.multiple_of(core * half, 128), half)
        return jnp.concatenate([tokblk[t, there, :] for t in range(ns)], axis=1)

    def weight_part(g):
        for e in range(1, ns):
            src = lax.rem(s + ns - e, ns)
            piece = dkv_all.at[g, pl.ds(pl.multiple_of(src * rows, 128), rows), :]
            remote(piece, piece, dsn.at[g, e - 1], drn.at[g, e - 1], (f, src)).wait_recv()
        dkv = dkv_all[g]
        core_out[g] = nn(features(1 - c), dkv).astype(jnp.bfloat16)
        core_copy(g).start()
        mine[g] = nn(features(c), dkv)

    def z_copy(g, d):
        return remote(z_out.at[g, d - 1], z_in.at[g, d - 1], rs.at[g, d - 1], rr.at[g, d - 1], (zpeer(d), s))

    def z_part(g):
        core_copy(g).wait_recv()
        zsum[g] = (mine[g] + core_in[g].astype(jnp.float32)).reshape(nz, pad, 128)
        for d in range(1, nz):
            z_out[g, d - 1] = zsum[g, lax.rem(z + d, nz)].astype(jnp.bfloat16)
            z_copy(g, d).start()

    def token_blocks():
        for e in range(1, ns):
            src = lax.rem(s + ns - e, ns)
            remote(tokpad.at[src], tokblk.at[src], ts.at[e - 1], tr.at[e - 1], (f, src)).wait_recv()

    @pl.loop(0, groups)
    def _(g):
        attention(g)

        @pl.when(g >= 1)
        def _():
            finish(g - 1)

        @pl.when(g == 2)
        def _():
            token_blocks()

        @pl.when(g >= 2)
        def _():
            weight_part(g - 2)

        @pl.when(g >= 3)
        def _():
            z_part(g - 3)

    finish(groups - 1)
    weight_part(groups - 2)
    z_part(groups - 3)
    pieces = [dkv_all[g, mine_rows, :] for g in range(groups)]
    dkv = jnp.concatenate([b[:, :HEAD_SIZE] for b in pieces] + [b[:, HEAD_SIZE:] for b in pieces], axis=1)
    for i in range(nf):
        tgrad_v[i * krows : (i + 1) * krows, :] = nt(whole(i), dkv).astype(jnp.bfloat16)
    weight_part(groups - 1)
    z_part(groups - 2)
    z_part(groups - 1)

    sums = []
    for g in range(groups):
        acc = zsum[g, z]
        for d in range(1, nz):
            z_copy(g, d).wait_recv()
            acc = acc + z_in[g, d - 1].astype(jnp.float32)
        sums.append(acc[:share])
    order = []
    for lo in (0, HEAD_SIZE):
        for g in range(0, groups, 2):
            order.append(jnp.concatenate([sums[g][:, lo : lo + HEAD_SIZE], sums[g + 1][:, lo : lo + HEAD_SIZE]], axis=1))
    for j in range(groups):
        wgrad[pl.ds(j, share, stride=groups), :] = order[j]

    for cp in sent:
        cp.wait_send()
    for g in range(groups):
        hg_copy(g).wait_send()
        core_copy(g).wait_send()
        for e in range(1, ns):
            dkv_copy(g, e).wait_send()
        for d in range(1, nz):
            z_copy(g, d).wait_send()
    for k in range(nz):
        for right in (False, True):
            _, there, onward, _ = chain(k, right)

            @pl.when(there & onward)
            def _(k=k, right=right):
                link(k, right).wait_send()

            if k > 0:

                @pl.when(there)
                def _(k=k, right=right):
                    block = chain(k, right)[0]
                    for e in range(1, ns):
                        over_seq(block, e).wait_send()
                    over_core(block).wait_send()

    over_core(f).wait_send()


def write_out(*refs):
    done = refs[8]
    copies = [pltpu.make_async_copy(refs[i], refs[4 + i], done.at[i]) for i in range(4)]
    for cp in copies:
        cp.start()
    for cp in copies:
        cp.wait()


KW_COLUMNS = 2 * KEY_VALUE_HEADS * HEAD_SIZE


def fused(tokens, queries, kv_weight, sink_logit_values, roll_offsets, out_grad):
    nf = lax.axis_size("fsdp")
    ns = lax.axis_size("seq")
    nz = nf // 2
    rows, width = tokens.shape[1:]
    krows = kv_weight.shape[0]
    share = width // (nf * ns)
    pad = -(-share // 16) * 16
    half = nz * pad
    query_width = QUERY_HEADS * HEAD_SIZE
    groups = KEY_VALUE_HEADS
    per = QUERY_HEADS // groups
    bf, f32 = jnp.bfloat16, jnp.float32
    sem = pltpu.SemaphoreType.DMA
    vm = pltpu.VMEM
    shape = jax.ShapeDtypeStruct
    anywhere = pl.BlockSpec(memory_space=pl.ANY)
    inside = pl.BlockSpec(memory_space=pltpu.VMEM)
    scalars = pl.BlockSpec(memory_space=pltpu.SMEM)
    results = pl.pallas_call(
        functools.partial(fused_kernel, nz, ns, share, pad),
        out_shape=(
            shape((rows, query_width), bf),
            shape((rows, query_width), bf),
            shape((width, rows), bf),
            shape((share * groups, 128), f32),
        ),
        in_specs=[anywhere, anywhere, anywhere, scalars, scalars, anywhere],
        out_specs=[inside] * 4,
        scratch_shapes=[
            vm((ns, nf, krows, 128), bf),
            vm((width, rows), bf),
            vm((rows, query_width), bf),
            vm((rows, query_width), bf),
            vm((nf, rows, -(-krows // 128) * 128), bf),
            vm((ns, nf * pad, rows), bf),
            vm((ns, nf * pad, rows), bf),
            vm((rows, query_width), bf),
            vm((per * rows, 2 * HEAD_SIZE), bf),
            vm((per * rows, 2 * HEAD_SIZE), bf),
            vm((groups, rows + WINDOW, 2 * HEAD_SIZE), bf),
            vm((rows + WINDOW, per * rows), bf),
            vm((rows + WINDOW, per * rows), bf),
            vm((groups, rows, 2 * HEAD_SIZE), f32),
            vm((groups, WINDOW, 2 * HEAD_SIZE), bf),
            vm((groups, WINDOW, 2 * HEAD_SIZE), bf),
            vm((groups, ns * rows, 2 * HEAD_SIZE), bf),
            vm((groups, half, 128), bf),
            vm((groups, half, 128), bf),
            vm((groups, half, 128), f32),
            vm((groups, nz, pad, 128), f32),
            vm((groups, nz - 1, pad, 128), bf),
            vm((groups, nz - 1, pad, 128), bf),
            vm((rows, KW_COLUMNS), f32),
            vm((QUERY_HEADS // 2, 1, 2 * rows), f32),
            sem((3 + ns,)),
            sem((nz,)), sem((nz,)), sem((nz,)), sem((nz,)),
            sem((nz, ns - 1)), sem((nz, ns - 1)),
            sem((nz,)), sem((nz,)),
            sem((ns - 1,)), sem((ns - 1,)),
            sem, sem,
            sem((groups,)), sem((groups,)),
            sem((groups, ns - 1)), sem((groups, ns - 1)),
            sem((groups,)), sem((groups,)),
            sem((groups, nz - 1)), sem((groups, nz - 1)),
        ],
        compiler_params=pltpu.CompilerParams(
            collective_id=0, has_side_effects=True, vmem_limit_bytes=56 * 1024 * 1024
        ),
    )(tokens[0].T, queries[0], kv_weight, sink_logit_values, roll_offsets, out_grad[0])
    attn, qgrad, tgrad, wgrad = pl.pallas_call(
        write_out,
        out_shape=tuple(shape(x.shape, x.dtype) for x in results),
        in_specs=[inside] * 4,
        out_specs=[anywhere] * 4,
        scratch_shapes=[sem((4,))],
    )(*results)
    return (attn[None], qgrad[None], tgrad.T[None], wgrad[None])


def fits_fused(mesh):
    nf, ns = mesh.shape["fsdp"], mesh.shape["seq"]
    return nf == 8 and KW_COLUMNS == 128 * ns


def solution(mesh):
    placed = (
        P("fsdp", "seq", None),
        P("fsdp", "seq", None),
        P("fsdp", None),
        P(),
        P("fsdp"),
        P("fsdp", "seq", None),
    )
    return jax.shard_map(
        fused if fits_fused(mesh) else local,
        mesh=mesh,
        in_specs=placed,
        out_specs=(
            P("fsdp", "seq", None),
            P("fsdp", "seq", None),
            P("fsdp", "seq", None),
            P("seq", "fsdp", None),
        ),
        check_vma=False,
    )
```
